32 devices in a mesh: fsdp: 2 (over y), ctx: 16 (over z, x, core).
Axes of the slice: x: 2, y: 2, z: 4, core: 2. Of those that a mesh axis runs over, the one named last changes fastest.
Arguments:
- tokens: bfloat16 [2048, 8, 768], P('ctx', 'fsdp'), may hold values from -6 to 6
- segments: int32 [2048, 8], P('ctx', 'fsdp'), may hold values from 0 to 20, as said below
- rand_blocks: int32 [8, 32, 12, 3], P('fsdp', 'ctx'), may hold values from 2 to 31, as said below
- w_qkv: bfloat16 [768, 2304], P('fsdp'), may hold values from -0.21875 to 0.21875
- w_out: bfloat16 [768, 768], P('fsdp'), may hold values from -1.75 to 1.75
- w_up: bfloat16 [768, 3072], P('fsdp'), may hold values from -0.21875 to 0.21875
- w_down: bfloat16 [3072, 768], P('fsdp'), may hold values from -0.21875 to 0.21875
- ln_gains: bfloat16 [2, 768], P(None, 'fsdp'), may hold values from 0.5 to 1.5
- biases: bfloat16 [6, 768], P(None, 'fsdp'), may hold values from -3 to 3
- up_bias: bfloat16 [3072], P('fsdp'), may hold values from -3 to 3
- cotangent: bfloat16 [2048, 8, 768], P('ctx', 'fsdp'), may hold values from -6 to 6
Outputs:
- output: bfloat16 [2048, 8, 768], P('ctx', 'fsdp')
- input_grad: bfloat16 [2048, 8, 768], P('ctx', 'fsdp')
- grad_w_qkv: float32 [768, 2304], P('fsdp')
- grad_w_out: float32 [768, 768], P('fsdp')
- grad_w_up: float32 [768, 3072], P('fsdp')
- grad_w_down: float32 [3072, 768], P('fsdp')
- grad_ln_gains: float32 [2, 768], P(None, 'fsdp')
- grad_biases: float32 [6, 768], P(None, 'fsdp')
- grad_up_bias: float32 [3072], P('fsdp')
The draws below stay inside these ranges and needn't reach their ends.
Inputs may be any that keep to these rules, and one draw needn't show every extreme that they name: `rand_blocks`: the 3 blocks of a query block and head are different, never block 0 or 1, never the query block or a neighbour of it. Counting over all query blocks, heads and random slots of one sequence that lie on one index of ctx, at most 6 of the blocks read lie on any one index of ctx; that many are read from some index in every draw. Blocks are never read from the reader's own index of ctx or the ones next to it. `segments`: document numbers start at 0 in each sequence and never fall; a document holds 102 to 1024 tokens, except the last of a sequence, which may be shorter; in each group of 4 sequences of one fsdp index one sequence is a single document and another is cut into documents of exactly 102 tokens but the last.
All inputs are finite; a program needn't handle non-finite values.
Results may differ from the reference program's by a relative error of at most 0.02.
Values may be sent and summed in bfloat16 or wider, within the bound.
No kernel may reach another device: no remote copies, remote signals or barrier semaphores. Data moves between devices by JAX's collectives and lax.ppermute only.
A program may use at most 832 MiB of HBM per device.

```python
import jax
import jax.numpy as jnp
from jax import lax

D = 768
H = 12
HD = 64
FF = 3072
BLK = 64
NRAND = 3
SEQ_TOK = 128
SEQ_DEV = 4
LENGTH = 2048
SEQS = 8
N_FSDP = 2
N_CTX = 16


def draw_rand_blocks(key, part):
    key = jax.random.fold_in(key, 11)
    start_key, local_key = jax.random.split(key)
    per_device = SEQ_TOK // BLK
    pick_count = per_device * H * NRAND
    device_ids = jnp.arange(N_CTX, dtype=jnp.int32)
    owner_ids = jnp.arange(N_CTX, dtype=jnp.int32)
    permitted = (owner_ids[None, :] != 0) & (jnp.abs(owner_ids[None, :] - device_ids[:, None]) > 1)
    permitted_count = jnp.sum(permitted.astype(jnp.int32), axis=1)
    order_list = jnp.argsort(jnp.where(permitted, owner_ids[None, :], N_CTX + owner_ids[None, :]), axis=1).astype(jnp.int32)
    starting = jax.random.randint(start_key, (SEQS, N_CTX, 1), 0, 1 << 20, dtype=jnp.int32)
    pick_ids = jnp.arange(pick_count, dtype=jnp.int32)[None, None, :]
    position = (starting + pick_ids) % permitted_count[None, :, None]
    owners = order_list[device_ids[None, :, None], position]
    local_rows = jax.random.randint(local_key, (SEQS, N_CTX, pick_count), 0, per_device, dtype=jnp.int32)
    chosen = owners * per_device + local_rows
    return chosen.reshape(SEQS, LENGTH // BLK, H, NRAND).astype(jnp.int32)


def draw_segments(key, part):
    key = jax.random.fold_in(key, 23)
    sizes_key, single_key = jax.random.split(key)
    shortest = LENGTH // 20
    longest = LENGTH // 2
    doc_slots = LENGTH // shortest + 1
    sizes = jax.random.randint(sizes_key, (SEQS, doc_slots), shortest, longest + 1, dtype=jnp.int32)
    ends = jnp.cumsum(sizes, axis=1)
    places = jnp.arange(LENGTH, dtype=jnp.int32)
    doc_ids = jnp.sum((places[None, :, None] >= ends[:, None, :]).astype(jnp.int32), axis=2)
    chosen = jax.random.randint(single_key, (N_FSDP,), 0, SEQ_DEV, dtype=jnp.int32)
    seq_ids = jnp.arange(SEQS, dtype=jnp.int32)
    group_pick = chosen[seq_ids // SEQ_DEV]
    single = seq_ids % SEQ_DEV == group_pick
    uniform = seq_ids % SEQ_DEV == (group_pick + 1) % SEQ_DEV
    doc_ids = jnp.where(uniform[:, None], places[None, :] // shortest, doc_ids)
    doc_ids = jnp.where(single[:, None], 0, doc_ids)
    return doc_ids.T.astype(jnp.int32)


def block_levels(own_key, extent, pieces, smallest, top_value):
    def one(dim, blocks):
        heights = jax.random.uniform(jax.random.fold_in(jax.random.fold_in(own_key, 6), dim), (blocks,), jnp.float32, smallest / len(pieces), top_value / len(pieces))
        return jnp.repeat(jnp.exp(heights), extent[dim] // blocks).reshape((-1,) + (1,) * (len(extent) - dim - 1))

    loudness = one(*pieces[0])
    for cut in pieces[1:]:
        loudness = loudness * one(*cut)
    return loudness


def scatter_about(rng, dims, spread, most, shards=(), held_as=jnp.bfloat16):
    drawn = jax.random.normal(rng, dims, jnp.float32) * spread
    if len(shards) > 0:
        drawn = block_levels(rng, dims, shards, -0.22, 0.18) * drawn
    return jnp.clip(drawn, min=-most, max=most).astype(held_as)


def setup_inputs(seed: int = 0) -> dict:
    key_of = jax.random.split(jax.random.key(seed), 12)
    tokens = scatter_about(key_of[0], (LENGTH, SEQS, D), 1.0, 6.0, ((0, 16), (1, 2)))
    segments = draw_segments(jax.random.fold_in(key_of[11], 71), 0)
    rand_blocks = draw_rand_blocks(jax.random.fold_in(key_of[11], 71), 0)
    w_qkv = scatter_about(key_of[3], (D, 3 * D), D ** -0.5, 0.21875, ((0, 2),))
    w_out = scatter_about(key_of[4], (D, D), (max(D // 64, 1)) ** -0.5, 1.75, ((0, 2),))
    w_up = scatter_about(key_of[5], (D, FF), D ** -0.5, 0.21875, ((0, 2),))
    w_down = scatter_about(key_of[6], (FF, D), (FF // 4) ** -0.5, 0.21875, ((0, 2),))
    ln_gains = jnp.clip(1.0 + 0.1 * jax.random.normal(key_of[7], (2, D), jnp.float32), 0.5, 1.5).astype(jnp.bfloat16)
    biases = scatter_about(key_of[8], (6, D), 0.5, 3.0, ((1, 2),))
    up_bias = scatter_about(key_of[9], (FF,), 0.5, 3.0, ((0, 2),))
    cotangent = scatter_about(key_of[10], (LENGTH, SEQS, D), 1.0, 6.0, ((0, 16), (1, 2)))
    return dict(tokens=tokens, segments=segments, rand_blocks=rand_blocks, w_qkv=w_qkv, w_out=w_out, w_up=w_up, w_down=w_down, ln_gains=ln_gains, biases=biases, up_bias=up_bias, cotangent=cotangent)


EPSILON = 1e-06
NEGATIVE = -1e+30

@jax.custom_vjp
def low(v):
    return lax.optimization_barrier(v.astype(jnp.bfloat16)).astype(jnp.float32)

@jax.custom_vjp
def low_back(v):
    return v

def low_keep(v):
    return (low(v), None)

def low_pass(kept, grad):
    return (grad,)

def back_keep(v):
    return (v, None)

def back_low(kept, grad):
    return (low(grad),)
low.defvjp(low_keep, low_pass)
low_back.defvjp(back_keep, back_low)

def exact_dot(left_side, right_side):
    return jnp.dot(left_side, right_side, precision=lax.Precision.HIGHEST)

def layer_norm(values, gain_row, shift_row):
    average = lax.optimization_barrier(jnp.mean(values, axis=-1, keepdims=True))
    centred = values - average
    variance = lax.optimization_barrier(jnp.mean(centred * centred, axis=-1, keepdims=True))
    return centred * lax.rsqrt(variance + EPSILON) * gain_row + shift_row

def attend(queries, key_rows, value_rows, seg_ids, rand_ids):
    block_total = LENGTH // BLK
    query_blocks = queries.reshape(block_total, BLK, H, HD)
    key_heads = key_rows.reshape(block_total, BLK, H, HD).transpose(2, 0, 1, 3)
    value_heads = value_rows.reshape(block_total, BLK, H, HD).transpose(2, 0, 1, 3)
    seg_blocks = seg_ids.reshape(block_total, BLK)
    block_ids = jnp.arange(block_total, dtype=jnp.int32)
    near_ids = block_ids[:, None] + jnp.arange(-1, 2, dtype=jnp.int32)[None, :]
    near_valid = (near_ids >= 0) & (near_ids < block_total)
    near_ids = jnp.clip(near_ids, 0, block_total - 1)
    glob_ids = jnp.broadcast_to(jnp.arange(2, dtype=jnp.int32)[None, :], (block_total, 2))
    glob_valid = jnp.abs(glob_ids - block_ids[:, None]) > 1
    slot_ids = jnp.concatenate([jnp.broadcast_to(near_ids[:, None, :], (block_total, H, 3)), jnp.broadcast_to(glob_ids[:, None, :], (block_total, H, 2)), rand_ids], axis=2)
    slot_valid = jnp.concatenate([jnp.broadcast_to(near_valid[:, None, :], (block_total, H, 3)), jnp.broadcast_to(glob_valid[:, None, :], (block_total, H, 2)), jnp.ones((block_total, H, NRAND), dtype=bool)], axis=2)
    head_ids = jnp.arange(H, dtype=jnp.int32)[None, :, None]
    picked_keys = key_heads[head_ids, slot_ids]
    picked_values = value_heads[head_ids, slot_ids]
    key_segs = seg_blocks[slot_ids]
    raw_scores = jnp.einsum('nbhd,nhskd->nhbsk', query_blocks, picked_keys, precision=lax.Precision.HIGHEST)
    allowed = slot_valid[:, :, None, :, None] & (seg_blocks[:, None, :, None, None] == key_segs[:, :, None, :, :])
    scores = low_back(jnp.where(allowed, raw_scores * HD ** (-0.5), NEGATIVE))
    row_max = lax.optimization_barrier(jnp.max(scores, axis=(3, 4), keepdims=True))
    exp_scores = jnp.exp(scores - row_max)
    attn_prob = low(exp_scores / lax.optimization_barrier(jnp.sum(exp_scores, axis=(3, 4), keepdims=True)))
    mixed_rows = jnp.einsum('nhbsk,nhskd->nbhd', attn_prob, picked_values, precision=lax.Precision.HIGHEST)
    return mixed_rows.reshape(LENGTH, D)

def sequence_layer(seq_tokens, seg_ids, rand_ids, weights):
    w_qkv, w_out, w_up, w_down, ln_gains, biases, up_bias = weights
    projected = exact_dot(seq_tokens, w_qkv)
    queries = low_back(low(projected[:, :D] + biases[0]))
    key_rows = low_back(low(projected[:, D:2 * D]))
    value_rows = low_back(low(projected[:, 2 * D:] + biases[1]))
    context = low_back(low(attend(queries, key_rows, value_rows, seg_ids, rand_ids)))
    branch = low_back(exact_dot(context, w_out)) + biases[2]
    first_norm = layer_norm(seq_tokens + branch, ln_gains[0], biases[3])
    hidden = low_back(exact_dot(low(first_norm), w_up) + up_bias)
    active = low(jax.nn.gelu(hidden, approximate=True))
    second = low_back(exact_dot(active, w_down)) + biases[5]
    return layer_norm(first_norm + second, ln_gains[1], biases[4])

def reference(tokens, segments, rand_blocks, w_qkv, w_out, w_up, w_down, ln_gains, biases, up_bias, cotangent):
    weights = tuple((array_in.astype(jnp.float32) for array_in in (w_qkv, w_out, w_up, w_down, ln_gains, biases, up_bias)))
    inputs = tokens.astype(jnp.float32).transpose(1, 0, 2)
    seg_rows = segments.T
    layer_fn = jax.checkpoint(sequence_layer)

    def forward(inputs, weights):

        def per_sequence(scan_state, scan_entry):
            seq_tokens, seg_ids, rand_ids = scan_entry
            return (scan_state, layer_fn(seq_tokens, seg_ids, rand_ids, weights))
        _, outputs = lax.scan(per_sequence, jnp.zeros((), jnp.float32), (inputs, seg_rows, rand_blocks))
        return outputs
    outputs, pullback = jax.vjp(forward, inputs, weights)
    input_grad, weight_grads = pullback(cotangent.astype(jnp.float32).transpose(1, 0, 2))
    return (outputs.transpose(1, 0, 2).astype(jnp.bfloat16), input_grad.transpose(1, 0, 2).astype(jnp.bfloat16), weight_grads[0], weight_grads[1], weight_grads[2], weight_grads[3], weight_grads[4], weight_grads[5], weight_grads[6])
```

```python
import math
from functools import partial

import jax
import jax.numpy as jnp
from jax import lax
from jax.experimental import pallas as pl
from jax.experimental.pallas import tpu as pltpu
from jax.sharding import PartitionSpec as P

HD = 64
BLK = 64
LANES = 128
SLOTS = 8
DOCS = 32
EPSILON = 1e-06
NEGATIVE = -1e30
SCALE = HD**-0.5
RATE = SCALE / math.log(2.0)
VMEM = 56 * 1024 * 1024

BF16 = jnp.bfloat16
F32 = jnp.float32


def dot(left, right, dims):
    return lax.dot_general(left, right, ((dims[0], dims[1]), ((), ())), preferred_element_type=F32)


def swap(value, axis, mask):
    count = lax.axis_size(axis)
    return lax.ppermute(value, axis, [(i, i ^ mask) for i in range(count)])


def bits_of(count):
    return [1 << k for k in range((count - 1).bit_length())]


def choose(index, cases):
    return cases[0] if len(cases) == 1 else lax.select_n(index, *cases)


def to_absolute(relative, index):
    count = len(relative)
    return [choose(index, [relative[k ^ i] for i in range(count)]) for k in range(count)]


def split_three(values):
    high = values.astype(BF16)
    rest = values - high.astype(F32)
    middle = rest.astype(BF16)
    return high, middle, (rest - middle.astype(F32)).astype(BF16)


def lane_ids(shape):
    return lax.broadcasted_iota(jnp.int32, shape, len(shape) - 1)


def place_three(base, values, lane, first):
    high, middle, small = split_three(values)
    base = jnp.where(lane == first, high.astype(F32), base)
    base = jnp.where(lane == first + 1, middle.astype(F32), base)
    return jnp.where(lane == first + 2, small.astype(F32), base)


def picked(ref, loc_ref, head, place):
    parts = [
        ref[head, pl.ds(pl.multiple_of(loc_ref[place + s] * BLK, BLK), BLK), :]
        for s in range(SLOTS)
    ]
    return jnp.concatenate(parts, axis=0)


def forward_kernel(heads, loc_ref, x_ref, w_ref, bias_ref, seg_ref, qa_ref, ka_ref, va_ref, ctx_ref):
    rows = x_ref.shape[0]
    tile = 256
    width = heads * LANES

    def project(i, carry):
        at = pl.ds(pl.multiple_of(i * tile, tile), tile)
        x = x_ref[at, :]
        lane = lane_ids((tile, LANES))
        same = (lane - HD) == seg_ref[at, :]
        coded = (lane >= HD) & (lane < HD + DOCS)
        ones = (lane >= HD + DOCS) & (lane < HD + DOCS + 3)
        q_extra = jnp.where(coded & same, NEGATIVE, 0.0)
        k_extra = jnp.where((coded & jnp.logical_not(same)) | ones, 1.0, 0.0)
        v_extra = jnp.where((lane >= HD) & (lane < HD + 3), 1.0, 0.0)
        for part, extra, out_ref in ((0, q_extra, qa_ref), (1, k_extra, ka_ref), (2, v_extra, va_ref)):
            cols = slice(part * width, (part + 1) * width)
            y = dot(x, w_ref[:, cols], ((1,), (0,))) + bias_ref[:, cols]
            for h in range(heads):
                out_ref[h, at, :] = (y[:, h * LANES : (h + 1) * LANES] + extra).astype(BF16)
        return carry

    lax.fori_loop(0, rows // tile, project, 0)
    lane = lane_ids((BLK, LANES))
    null_key = jnp.where((lane >= HD) & (lane < HD + DOCS), 1.0, 0.0).astype(BF16)
    for h in range(heads):
        ka_ref[h, rows : rows + BLK, :] = null_key
        va_ref[h, rows : rows + BLK, :] = jnp.zeros((BLK, LANES), BF16)

    def attend(j, carry):
        at = pl.ds(pl.multiple_of(j * BLK, BLK), BLK)
        done = []
        for h in range(heads):
            place = (j * heads + h) * SLOTS
            q = qa_ref[h, at, :]
            scores = dot(q, picked(ka_ref, loc_ref, h, place), ((1,), (1,)))
            top = jnp.max(scores, axis=1, keepdims=True)
            prob = jnp.exp2((scores - top) * RATE).astype(BF16)
            mixed = dot(prob, picked(va_ref, loc_ref, h, place), ((1,), (0,)))
            total = mixed[:, HD : HD + 1]
            done.append((mixed / total)[:, :HD])
            level = -(top + jnp.log2(total) * (1.0 / RATE))
            qa_ref[h, at, :] = place_three(q.astype(F32), level, lane, HD + DOCS).astype(BF16)
        ctx_ref[at, :] = jnp.concatenate(done, axis=1).astype(BF16)
        return carry

    lax.fori_loop(0, rows // BLK, attend, 0)


def backward_kernel(heads, group, loc_ref, qa_ref, ka_ref, va_ref, ctx_ref, *rest):
    grad_refs = rest[:group]
    out_ref, da_ref, dq_ref, dk_ref, dv_ref = rest[group:]
    rows = ctx_ref.shape[0]
    part_rows = rows // group
    lane = lane_ids((BLK, LANES))
    tile = 128
    lane_tile = lane_ids((tile, LANES))
    blank = jnp.zeros((tile, LANES - HD), F32)

    for r in range(group):

        def load(i, carry, r=r):
            at = pl.ds(pl.multiple_of(i * tile, tile), tile)
            all_at = pl.ds(pl.multiple_of(r * part_rows + i * tile, tile), tile)
            grads = grad_refs[r][at, :].astype(F32)
            mixed = ctx_ref[all_at, :].astype(F32)
            for h in range(heads):
                cols = slice(h * HD, (h + 1) * HD)
                delta = jnp.sum(grads[:, cols] * mixed[:, cols], axis=1, keepdims=True)
                wide = jnp.concatenate([grads[:, cols], blank], axis=1)
                da_ref[h, all_at, :] = place_three(wide, -delta, lane_tile, HD).astype(BF16)
            return carry

        lax.fori_loop(0, part_rows // tile, load, 0)

    def clear(i, carry):
        for h in range(heads):
            dk_ref[h, i] = jnp.zeros((HD, LANES), F32)
            dv_ref[h, i] = jnp.zeros((HD, LANES), F32)
        return carry

    lax.fori_loop(0, rows // BLK + 1, clear, 0)
    left_half = lane_ids((HD, LANES)) < BLK

    def attend(j, carry):
        at = pl.ds(pl.multiple_of(j * BLK, BLK), BLK)
        for h in range(heads):
            place = (j * heads + h) * SLOTS
            q = qa_ref[h, at, :]
            d_mixed = da_ref[h, at, :]
            keys = picked(ka_ref, loc_ref, h, place)
            values = picked(va_ref, loc_ref, h, place)
            prob = jnp.exp2(dot(q, keys, ((1,), (1,))) * RATE)
            d_scores = (prob * dot(d_mixed, values, ((1,), (1,)))).astype(BF16)
            dq_ref[h, at, :] = (dot(d_scores, keys, ((1,), (0,))) * SCALE).astype(BF16)
            q_turned = q.astype(F32).T[:HD].astype(BF16)
            d_turned = d_mixed.astype(F32).T[:HD].astype(BF16)
            d_keys = dot(q_turned, d_scores, ((1,), (0,)))
            d_values = dot(d_turned, prob.astype(BF16), ((1,), (0,)))
            for s in range(SLOTS):
                to = loc_ref[place + s]
                cols = slice((s // 2) * LANES, (s // 2 + 1) * LANES)
                mine = left_half if s % 2 == 0 else jnp.logical_not(left_half)
                dk_ref[h, to] += jnp.where(mine, d_keys[:, cols], 0.0)
                dv_ref[h, to] += jnp.where(mine, d_values[:, cols], 0.0)
        return carry

    lax.fori_loop(0, rows // BLK, attend, 0)

    def finish(j, carry):
        at = pl.ds(pl.multiple_of(j * BLK, BLK), BLK)
        done = [dq_ref[h, at, :][:, :HD].astype(F32) for h in range(heads)]
        for ref, factor in ((dk_ref, SCALE), (dv_ref, 1.0)):
            for h in range(heads):
                both = ref[h, j].T
                done.append((both[:BLK] + both[BLK:]) * factor)
        out_ref[at, :] = jnp.concatenate(done, axis=1).astype(BF16)
        return carry

    lax.fori_loop(0, rows // BLK, finish, 0)


def whole(memory):
    return pl.BlockSpec(memory_space=memory)


def attention_forward(loc, x, weight, bias, seg, heads):
    rows = x.shape[0]
    kept = jax.ShapeDtypeStruct((heads, rows + BLK, LANES), BF16)
    return pl.pallas_call(
        partial(forward_kernel, heads),
        out_shape=(
            jax.ShapeDtypeStruct((heads, rows, LANES), BF16),
            kept,
            kept,
            jax.ShapeDtypeStruct((rows, heads * HD), BF16),
        ),
        in_specs=[whole(pltpu.SMEM)] + [whole(pltpu.VMEM)] * 4,
        out_specs=(whole(pltpu.VMEM),) * 4,
        compiler_params=pltpu.CompilerParams(vmem_limit_bytes=VMEM),
        name="attention_forward",
    )(loc, x, weight, bias, seg)


def attention_backward(loc, qa, ka, va, ctx, grads, heads):
    rows = ctx.shape[0]
    blocks = rows // BLK
    return pl.pallas_call(
        partial(backward_kernel, heads, len(grads)),
        out_shape=jax.ShapeDtypeStruct((rows, 3 * heads * HD), BF16),
        in_specs=[whole(pltpu.SMEM)] + [whole(pltpu.VMEM)] * (4 + len(grads)),
        out_specs=whole(pltpu.VMEM),
        scratch_shapes=[
            pltpu.VMEM((heads, rows, LANES), BF16),
            pltpu.VMEM((heads, rows, LANES), BF16),
            pltpu.VMEM((heads, blocks + 1, HD, LANES), F32),
            pltpu.VMEM((heads, blocks + 1, HD, LANES), F32),
        ],
        compiler_params=pltpu.CompilerParams(vmem_limit_bytes=VMEM),
        name="attention_backward",
    )(loc, qa, ka, va, ctx, *grads)


def norm_forward(values, gain_row, shift_row):
    average = jnp.mean(values, axis=-1, keepdims=True)
    centred = values - average
    variance = jnp.mean(centred * centred, axis=-1, keepdims=True)
    inv_std = lax.rsqrt(variance + EPSILON)
    scaled = centred * inv_std
    return (scaled * gain_row + shift_row, scaled, inv_std)


def norm_backward(upstream, scaled, inv_std, gain_row):
    weighted = upstream * gain_row
    centre_term = jnp.mean(weighted, axis=-1, keepdims=True)
    slope_term = jnp.mean(weighted * scaled, axis=-1, keepdims=True)
    d_values = inv_std * (weighted - centre_term - scaled * slope_term)
    return (d_values, jnp.sum(upstream * scaled, axis=0), jnp.sum(upstream, axis=0))


def gather_fsdp(value):
    index = lax.axis_index("fsdp")
    parts = [value]
    for bit in bits_of(lax.axis_size("fsdp")):
        parts += [swap(part, "fsdp", bit) for part in parts]
    return to_absolute(parts, index)


def gather_weight(value):
    index = lax.axis_index("fsdp")
    core = lax.axis_index("ctx") & 1
    half = value.shape[0] // 2
    mine = lax.dynamic_slice_in_dim(value, core * half, half, 0)
    parts = [mine]
    for bit in bits_of(lax.axis_size("fsdp")):
        parts += [swap(part, "fsdp", bit) for part in parts]
    full = [value]
    for part in parts[1:]:
        other = swap(part, "ctx", 1)
        full.append(
            lax.select_n(
                core, jnp.concatenate([part, other]), jnp.concatenate([other, part])
            )
        )
    return jnp.concatenate(to_absolute(full, index), axis=0)


def halve(value, axis, dim, mask, index):
    half = value.shape[dim] // 2
    bit = (index // mask) & 1
    mine = lax.dynamic_slice_in_dim(value, bit * half, half, dim)
    theirs = lax.dynamic_slice_in_dim(value, (1 - bit) * half, half, dim)
    return mine + swap(theirs.astype(BF16), axis, mask).astype(F32)


def double(value, axis, dim, mask, index):
    bit = (index // mask) & 1
    other = swap(value, axis, mask)
    return lax.select_n(
        bit,
        jnp.concatenate([value, other], axis=dim),
        jnp.concatenate([other, value], axis=dim),
    )


def reduce_over_all(value):
    f_index, c_index = lax.axis_index("fsdp"), lax.axis_index("ctx")
    value = halve(value, "ctx", 1, 1, c_index)
    for bit in reversed(bits_of(lax.axis_size("fsdp"))):
        value = halve(value, "fsdp", 0, bit, f_index)
    value = value[0]
    rest = bits_of(lax.axis_size("ctx"))[1:]
    for bit in rest:
        value = halve(value, "ctx", 0, bit, c_index)
    value = value.astype(BF16)
    for bit in reversed(rest):
        value = double(value, "ctx", 0, bit, c_index)
    return double(value, "ctx", 0, 1, c_index).astype(F32)


def local(
    tokens, segments, rand_blocks, w_qkv, w_out, w_up, w_down, ln_gains, biases, up_bias, cotangent
):
    positions, seq_count, width = tokens.shape
    n_f, n_c = lax.axis_size("fsdp"), lax.axis_size("ctx")
    f_index, c_index = lax.axis_index("fsdp"), lax.axis_index("ctx")
    group = n_c // seq_count
    plane, member = c_index // group, c_index % group
    head_count = width // HD
    heads = -(-head_count // group)
    per_chunk = positions // BLK
    blocks = per_chunk * n_c
    rows_here = seq_count * positions
    f_width = width // n_f
    slab = heads * HD
    spare = group * slab - width

    def to_planes(array, dim):
        parts = [lax.dynamic_index_in_dim(array, plane ^ p, dim, keepdims=False) for p in range(seq_count)]
        return jnp.stack([swap(part, "ctx", p * group) if p else part for p, part in enumerate(parts)])

    def from_planes(array):
        parts = [swap(array[p], "ctx", p * group) if p else array[p] for p in range(seq_count)]
        return jnp.stack(to_absolute(parts, plane), axis=1)

    def over_plane(array):
        parts = {0: array}
        for bit in reversed(bits_of(group)):
            for r in list(parts):
                parts[r ^ bit] = swap(parts[r], "ctx", bit)
        return jnp.stack([parts[r] for r in range(group)])

    x_rows = to_planes(tokens, 1)
    x_seq = over_plane(x_rows).reshape(blocks * BLK, width)

    w_parts = jnp.pad(w_qkv.reshape(-1, 3, width), ((0, 0), (0, 0), (0, spare))) if spare else None
    if spare:
        w_mine = lax.dynamic_slice_in_dim(w_parts, member * slab, slab, 2).reshape(-1, 3 * slab)
    else:
        w_mine = jnp.concatenate(
            [lax.dynamic_slice_in_dim(w_qkv, k * width + member * slab, slab, 1) for k in range(3)], axis=1
        )
    w_heads = jnp.concatenate(gather_fsdp(w_mine), axis=0)
    w_wide = jnp.pad(
        w_heads.reshape(width, 3 * heads, HD), ((0, 0), (0, 0), (0, LANES - HD))
    ).reshape(width, 3 * heads * LANES)
    small = jnp.concatenate([ln_gains.reshape(-1), biases.reshape(-1), up_bias])
    small = jnp.stack(gather_fsdp(small)).astype(F32)
    gains_all = small[:, : 2 * f_width].reshape(n_f, 2, f_width).transpose(1, 0, 2).reshape(2, width)
    biases_all = (
        small[:, 2 * f_width : 8 * f_width].reshape(n_f, 6, f_width).transpose(1, 0, 2).reshape(6, width)
    )
    up_shift = small[:, 8 * f_width :].reshape(-1)
    out_full = gather_weight(w_out)
    up_full = gather_weight(w_up)
    down_full = gather_weight(w_down)

    meta = jnp.concatenate([segments.T, rand_blocks.reshape(seq_count, -1)], axis=1)
    meta = over_plane(to_planes(meta, 0))
    seg = meta[..., :positions].reshape(blocks * BLK, 1)
    rand = meta[..., positions:].reshape(blocks, head_count, -1)
    rand = jnp.pad(rand, ((0, 0), (0, group * heads - head_count), (0, 0)))
    rand = lax.dynamic_slice_in_dim(rand, member * heads, heads, 1)

    def place_of(block):
        relative = (block // per_chunk) ^ c_index
        return ((relative % group) * seq_count + relative // group) * per_chunk + block % per_chunk

    spot = jnp.arange(blocks, dtype=jnp.int32)
    turn = spot // per_chunk
    number = (((turn % seq_count) * group + turn // seq_count) ^ c_index) * per_chunk + spot % per_chunk
    near = number[:, None] + jnp.arange(-1, 2, dtype=jnp.int32)
    near = jnp.where((near >= 0) & (near < blocks), place_of(near), blocks)
    glob = jnp.arange(2, dtype=jnp.int32)[None, :]
    glob = jnp.where(jnp.abs(glob - number[:, None]) > 1, place_of(glob), blocks)
    fixed = jnp.concatenate([near, glob], axis=1)
    loc = jnp.concatenate(
        [jnp.broadcast_to(fixed[:, None, :], (blocks, heads, 5)), place_of(rand)], axis=2
    ).reshape(-1)

    bias_mine = lax.dynamic_slice_in_dim(
        jnp.pad(biases_all[:2], ((0, 0), (0, spare))), member * slab, slab, 1
    ).reshape(2, heads, HD)
    bias_mine = jnp.pad(bias_mine, ((0, 0), (0, 0), (0, LANES - HD)))
    bias_wide = jnp.concatenate(
        [bias_mine[0], jnp.zeros_like(bias_mine[0]), bias_mine[1]], axis=0
    ).reshape(1, -1)

    qa, ka, va, ctx = attention_forward(loc, x_seq, w_wide, bias_wide, seg, heads)

    ctx_parts = ctx.reshape(group, rows_here, slab)
    ctx_parts = [swap(ctx_parts[r], "ctx", r) if r else ctx_parts[0] for r in range(group)]
    context_low = jnp.concatenate(to_absolute(ctx_parts, member), axis=1)[:, :width]

    inputs = x_rows.reshape(rows_here, width).astype(F32)
    branch = jnp.dot(context_low, out_full, preferred_element_type=F32) + biases_all[2]
    first_norm, first_scaled, first_inv = norm_forward(inputs + branch, gains_all[0], biases_all[3])
    first_low = first_norm.astype(BF16)
    hidden = jnp.dot(first_low, up_full, preferred_element_type=F32) + up_shift
    active_low = jax.nn.gelu(hidden, approximate=True).astype(BF16)
    second = jnp.dot(active_low, down_full, preferred_element_type=F32) + biases_all[5]
    result, final_scaled, final_inv = norm_forward(first_norm + second, gains_all[1], biases_all[4])
    output = from_planes(result.astype(BF16).reshape(seq_count, positions, width))

    upstream = to_planes(cotangent, 1).reshape(rows_here, width).astype(F32)
    d_second, d_gain_two, d_shift_two = norm_backward(upstream, final_scaled, final_inv, gains_all[1])
    d_second_low = d_second.astype(BF16)
    grad_down = dot(active_low, d_second_low, ((0,), (0,)))
    d_active = dot(d_second_low, down_full, ((1,), (1,)))
    _, gelu_pull = jax.vjp(partial(jax.nn.gelu, approximate=True), hidden)
    d_hidden_low = gelu_pull(d_active)[0].astype(BF16)
    grad_up = dot(first_low, d_hidden_low, ((0,), (0,)))
    d_first = d_second + dot(d_hidden_low, up_full, ((1,), (1,)))
    d_branch, d_gain_one, d_shift_one = norm_backward(d_first, first_scaled, first_inv, gains_all[0])
    d_branch_low = d_branch.astype(BF16)
    grad_out = dot(context_low, d_branch_low, ((0,), (0,)))
    d_context = dot(d_branch_low, out_full, ((1,), (1,))).astype(BF16)

    d_wide = jnp.pad(d_context, ((0, 0), (0, spare)))
    d_parts = [
        lax.dynamic_slice_in_dim(d_wide, (member ^ r) * slab, slab, 1) for r in range(group)
    ]
    d_parts = [swap(part, "ctx", r) if r else part for r, part in enumerate(d_parts)]

    down_total = reduce_over_all(grad_down.reshape(n_f, -1, width))
    vectors = jnp.concatenate(
        [
            jnp.stack([d_gain_one, d_gain_two]),
            jnp.stack([jnp.sum(d_branch, axis=0), d_shift_one, d_shift_two, jnp.sum(d_second, axis=0)]),
        ]
    )
    up_bias_grad = jnp.sum(d_hidden_low.astype(F32), axis=0).reshape(n_f, -1)
    vectors = vectors.reshape(6, n_f, f_width).transpose(1, 0, 2).reshape(n_f, -1)
    vectors = jnp.concatenate([vectors, up_bias_grad], axis=1)
    used = vectors.shape[1]
    extra = -(-used // f_width // LANES) * LANES
    vectors = jnp.pad(vectors, ((0, 0), (0, f_width * extra - used))).reshape(n_f, f_width, extra)
    up_out = jnp.concatenate(
        [grad_up.reshape(n_f, f_width, -1), grad_out.reshape(n_f, f_width, -1), vectors], axis=2
    )
    up_out = reduce_over_all(up_out)
    hidden_width = up_full.shape[1]
    up_total = up_out[:, :hidden_width]
    out_total = up_out[:, hidden_width : hidden_width + width]
    vectors = up_out[:, hidden_width + width :].reshape(-1)
    gains_total = vectors[: 2 * f_width].reshape(2, f_width)
    biases_late = vectors[2 * f_width : 6 * f_width].reshape(4, f_width)
    up_bias_total = vectors[6 * f_width : used]

    d_qkv = attention_backward(loc, qa, ka, va, ctx, d_parts, heads)

    d_x = dot(d_qkv, w_heads, ((1,), (1,))).reshape(group, rows_here, width)
    pieces = {r: d_x[r] for r in range(group)}
    for bit in bits_of(group):
        for r in [r for r in pieces if r & bit]:
            pieces[r ^ bit] = pieces[r ^ bit] + swap(pieces.pop(r).astype(BF16), "ctx", bit).astype(F32)
    input_grad = (d_branch + pieces[0]).astype(BF16)
    input_grad = from_planes(input_grad.reshape(seq_count, positions, width))

    grad_qkv = dot(x_seq, d_qkv, ((0,), (0,))).reshape(n_f, f_width, 3 * slab)
    sums = jnp.sum(d_qkv.astype(F32), axis=0, keepdims=True)
    sums = jnp.pad(sums, ((0, 15), (0, 0)))
    value = jnp.concatenate([grad_qkv, jnp.broadcast_to(sums[None], (n_f,) + sums.shape)], axis=1)
    for bit in reversed(bits_of(n_f)):
        value = halve(value, "fsdp", 0, bit, f_index)
    value = value[0]
    plane_bits = [bit * group for bit in bits_of(seq_count)]
    for bit in plane_bits:
        value = halve(value, "ctx", 0, bit, c_index)
    value = value.astype(BF16)
    for bit in reversed(plane_bits):
        value = double(value, "ctx", 0, bit, c_index)
    parts = [value]
    for bit in bits_of(group):
        parts += [swap(part, "ctx", bit) for part in parts]
    parts = to_absolute(parts, member)
    qkv_total = jnp.stack([part.reshape(-1, 3, slab) for part in parts], axis=2).reshape(-1, 3, group * slab)
    qkv_total = qkv_total[:, :, :width].astype(F32)
    early = lax.dynamic_slice_in_dim(qkv_total[f_width][0::2], f_index * f_width, f_width, 1)
    qkv_total = qkv_total[:f_width].reshape(f_width, 3 * width)
    biases_total = jnp.concatenate([early, biases_late])
    return (
        output,
        input_grad,
        qkv_total,
        out_total,
        up_total,
        down_total,
        gains_total,
        biases_total,
        up_bias_total,
    )


def solution(mesh):
    placed = (
        P("ctx", "fsdp", None),
        P("ctx", "fsdp"),
        P("fsdp", "ctx", None, None),
        P("fsdp", None),
        P("fsdp", None),
        P("fsdp", None),
        P("fsdp", None),
        P(None, "fsdp"),
        P(None, "fsdp"),
        P("fsdp"),
        P("ctx", "fsdp", None),
    )
    return jax.shard_map(
        local,
        mesh=mesh,
        in_specs=placed,
        out_specs=(
            P("ctx", "fsdp", None),
            P("ctx", "fsdp", None),
            P("fsdp", None),
            P("fsdp", None),
            P("fsdp", None),
            P("fsdp", None),
            P(None, "fsdp"),
            P(None, "fsdp"),
            P("fsdp"),
        ),
        check_vma=False,
    )
```

```python
import math
from functools import partial

import jax
import jax.numpy as jnp
from jax import lax
from jax.experimental import pallas as pl
from jax.experimental.pallas import tpu as pltpu
from jax.sharding import PartitionSpec as P

HD = 64
BLK = 64
LANES = 128
SLOTS = 8
DOCS = 32
EPSILON = 1e-06
NEGATIVE = -1e30
SCALE = HD**-0.5
RATE = SCALE / math.log(2.0)
VMEM = 56 * 1024 * 1024
WEIGHT = 0

BF16 = jnp.bfloat16
F32 = jnp.float32


def dot(left, right, dims):
    return lax.dot_general(left, right, ((dims[0], dims[1]), ((), ())), preferred_element_type=F32)


def swap(value, axis, mask):
    count = lax.axis_size(axis)
    return lax.ppermute(value, axis, [(i, i ^ mask) for i in range(count)])


def gate(value, *after):
    return lax.optimization_barrier((value, *after))[0]


def bits_of(count):
    return [1 << k for k in range((count - 1).bit_length())]


def choose(index, cases):
    return cases[0] if len(cases) == 1 else lax.select_n(index, *cases)


def to_absolute(relative, index):
    count = len(relative)
    return [choose(index, [relative[k ^ i] for i in range(count)]) for k in range(count)]


def split_three(values):
    high = values.astype(BF16)
    rest = values - high.astype(F32)
    middle = rest.astype(BF16)
    return high, middle, (rest - middle.astype(F32)).astype(BF16)


def lane_ids(shape):
    return lax.broadcasted_iota(jnp.int32, shape, len(shape) - 1)


def place_three(base, values, lane, first):
    high, middle, small = split_three(values)
    base = jnp.where(lane == first, high.astype(F32), base)
    base = jnp.where(lane == first + 1, middle.astype(F32), base)
    return jnp.where(lane == first + 2, small.astype(F32), base)


def picked(ref, loc_ref, head, place):
    parts = [
        ref[head, pl.ds(pl.multiple_of(loc_ref[place + s] * BLK, BLK), BLK), :]
        for s in range(SLOTS)
    ]
    return jnp.concatenate(parts, axis=0)


def gathered(pieces, places, target, sem, first):
    copies = []
    for k, (piece, place) in enumerate(zip(pieces, places)):
        copy = pltpu.make_async_copy(piece, target.at[pl.ds(place, piece.shape[0])], sem.at[first + k])
        copy.start()
        copies.append(copy)
    return copies


def put(source, target, sem, place):
    copy = pltpu.make_async_copy(source, target, sem.at[place])
    copy.start()
    return copy


def absolute_chunk(turn, own, seqs, group):
    return ((turn % seqs) * group + turn // seqs) ^ own


def split_kernel(tail, at_ref, rows_ref, *rest):
    positions, seqs, width = rows_ref.shape
    if tail:
        line_ref, *rest = rest
    for p, ref in enumerate(rest):
        for s in range(seqs):

            @pl.when((at_ref[3] ^ p) == s)
            def _(ref=ref, s=s):
                ref[:positions, :] = rows_ref[:, s, :]
                if tail:
                    blank = jnp.zeros((tail - 1, width), F32)
                    line = line_ref[s : s + 1, :].astype(F32)
                    ref[positions:, :] = jnp.concatenate([line, blank], axis=0).astype(BF16)


def split_planes(turns, rows, line=None):
    positions, seqs, width = rows.shape
    tail = 0 if line is None else 16
    shape = jax.ShapeDtypeStruct((positions + tail, width), BF16)
    ins = (turns, rows) if line is None else (turns, rows, line)
    return local_call(partial(split_kernel, tail), (shape,) * seqs, ins, [], "split_planes")


def forward_kernel(heads, group, seqs, counts, at_ref, bias_ref, *rest):
    x_pieces, w_pieces, rest = rest[: counts[0]], rest[counts[0] : sum(counts)], rest[sum(counts) :]
    x_out, q_out, k_out, v_out, loc_ref = rest[:5]
    ctx_refs, rest = rest[5 : 5 + group], rest[5 + group :]
    x_s, q_s, k_s, v_s, w_s, seg_s, number_v, number_s, sem = rest
    chunks, tall, width = x_s.shape
    chunk, blocks = x_out.shape[1], q_s.shape[1] // BLK
    rows = chunks * chunk
    w_rows = width // counts[1]
    w_copies = gathered(
        [piece.at[pl.ds(0, w_rows)] for piece in w_pieces],
        [pl.multiple_of((at_ref[0] ^ k) * w_rows, 16) for k in range(counts[1])],
        w_s,
        sem,
        counts[0],
    )
    last = sum(counts)
    x_copies, turn = [], 0
    for piece in x_pieces:
        count = piece.shape[0]
        x_copies.append(put(piece, x_s.at[pl.ds(turn, count)], sem, last + 5 + turn))
        turn += count
    for copy in w_copies:
        copy.wait()
    for copy in x_copies:
        copy.wait()
    out_copies = [put(x_s.at[:, pl.ds(0, chunk)], x_out, sem, last)]
    tile = 2 * chunk
    lines = jnp.concatenate(
        [x_s[k, chunk:, : 2 * LANES].astype(F32)[:1] for k in range(chunks)], axis=0
    )
    number_v[...] = lines[:, LANES:].astype(jnp.int32)
    number_copy = put(number_v, number_s, sem, last + 4)
    seg_s[...] = jnp.concatenate([lines[:, :LANES], jnp.zeros((LANES - chunks, LANES), F32)], axis=0).T
    number_copy.wait()
    per = chunk // BLK
    own, member = at_ref[5], at_ref[4]

    def place_of(block):
        c = (block // per) ^ own
        return ((c % group) * seqs + c // group) * per + block % per

    def slots_of(j):
        turn = j // per
        real = absolute_chunk(turn, own, seqs, group) * per + j % per
        fixed = []
        for d in (-1, 0, 1):
            near = jnp.clip(real + d, 0, blocks - 1)
            fixed.append(jnp.where(near == real + d, place_of(near), blocks))
        for b in range(2):
            fixed.append(jnp.where(jnp.abs(real - b) > 1, place_of(jnp.int32(b)), blocks))
        first = member * (LANES // group) + (j % per) * heads * 3
        for h in range(heads):
            free = [place_of(number_s[turn, first + h * 3 + r]) for r in range(3)]
            for s, value in enumerate(fixed + free):
                loc_ref[(j * heads + h) * SLOTS + s] = value

    def project(i, carry):
        at = pl.ds(pl.multiple_of(i * tile, tile), tile)
        x = jnp.concatenate([x_s[2 * i, :chunk, :], x_s[2 * i + 1, :chunk, :]], axis=0)
        lane = lane_ids((tile, LANES))
        seg = []
        for k in range(2):
            mine = lane_ids((LANES, LANES)) == 2 * i + k
            seg.append(jnp.sum(jnp.where(mine, seg_s[...], 0.0), axis=1, keepdims=True))
        same = (lane - HD).astype(F32) == jnp.concatenate(seg, axis=0)
        coded = (lane >= HD) & (lane < HD + DOCS)
        ones = (lane >= HD + DOCS) & (lane < HD + DOCS + 3)
        q_extra = jnp.where(coded & same, NEGATIVE, 0.0)
        k_extra = jnp.where((coded & jnp.logical_not(same)) | ones, 1.0, 0.0)
        v_extra = jnp.where((lane >= HD) & (lane < HD + 3), 1.0, 0.0)
        head_lane = lane < HD
        y = dot(x, w_s[...], ((1,), (0,))) + bias_ref[...]
        for part, extra, ref in ((0, k_extra, k_s), (1, v_extra, v_s), (2, q_extra, q_s)):
            for h in range(heads):
                n = part * heads + h
                here = y[:, n // 2 * LANES : (n // 2 + 1) * LANES]
                if n % 2:
                    here = pltpu.roll(here, HD, 1)
                elif here.shape[1] < LANES:
                    here = jnp.concatenate([here, jnp.zeros((tile, LANES - here.shape[1]), F32)], axis=1)
                ref[h, at, :] = jnp.where(head_lane, here, extra).astype(BF16)
        for k in range(2 * per):
            slots_of(i * 2 * per + k)
        return carry

    lax.fori_loop(0, rows // tile, project, 0)
    lane = lane_ids((BLK, LANES))
    null_key = jnp.where((lane >= HD) & (lane < HD + DOCS), 1.0, 0.0).astype(BF16)
    for h in range(heads):
        k_s[h, rows : rows + BLK, :] = null_key
        v_s[h, rows : rows + BLK, :] = jnp.zeros((BLK, LANES), BF16)
    out_copies += [put(k_s, k_out, sem, last + 1), put(v_s, v_out, sem, last + 2)]
    part_blocks = rows // BLK // group
    together = 4

    for r in range(group):

        def attend(i, carry, r=r):
            units = [(u, h) for u in range(together) for h in range(heads)]
            row = [r * part_blocks + i * together + u for u in range(together)]
            at = [pl.ds(pl.multiple_of(j * BLK, BLK), BLK) for j in row]
            place = [(row[u] * heads + h) * SLOTS for u, h in units]
            q = [q_s[h, at[u], :] for u, h in units]
            scores = [
                dot(q[n], picked(k_s, loc_ref, h, place[n]), ((1,), (1,))) for n, (u, h) in enumerate(units)
            ]
            top = [jnp.max(t, axis=1, keepdims=True) for t in scores]
            prob = [jnp.exp2((t - m) * RATE).astype(BF16) for t, m in zip(scores, top)]
            mixed = [
                dot(prob[n], picked(v_s, loc_ref, h, place[n]), ((1,), (0,))) for n, (u, h) in enumerate(units)
            ]
            total = [m[:, HD : HD + 1] for m in mixed]
            done = [(m / t)[:, :HD] for m, t in zip(mixed, total)]
            level = [-(m + jnp.log2(t) * (1.0 / RATE)) for m, t in zip(top, total)]
            for n, (u, h) in enumerate(units):
                q_s[h, at[u], :] = place_three(q[n].astype(F32), level[n], lane, HD + DOCS).astype(BF16)
            for u in range(together):
                here = pl.ds(pl.multiple_of((i * together + u) * BLK, BLK), BLK)
                ctx_refs[r][here, :] = jnp.concatenate(done[u * heads : (u + 1) * heads], axis=1).astype(BF16)
            return carry

        lax.fori_loop(0, part_blocks // together, attend, 0)
    out_copies.append(put(q_s, q_out, sem, last + 3))
    for copy in out_copies:
        copy.wait()


def backward_kernel(heads, group, count, fast, loc_ref, at_ref, qa_ref, ka_ref, va_ref, x_ref, *rest):
    w_pieces, rest = rest[:count], rest[count:]
    ctx_refs, grad_refs, rest = rest[:group], rest[group : 2 * group], rest[2 * group :]
    keep_ref, send_ref, *rest = rest
    if fast:
        mine_ref, theirs_ref, *rest = rest
    else:
        out_ref, *rest = rest
    da_s, dq_s, x_s, w_s, keep_s, send_s, sem, *rest = rest
    dk_even, dk_odd, dv_even, dv_odd = (rest[i * heads : (i + 1) * heads] for i in range(4))
    if fast:
        out_ref = rest[4 * heads]
    rows, width = x_ref.shape
    w_rows = width // count
    w_copies = gathered(
        [piece.at[pl.ds(0, w_rows)] for piece in w_pieces],
        [pl.multiple_of((at_ref[0] ^ k) * w_rows, 16) for k in range(count)],
        w_s,
        sem,
        0,
    )
    if fast:
        x_copy = put(x_ref, x_s, sem, count)
    part_rows = rows // group
    tile = 128
    lane_tile = lane_ids((tile, LANES))
    blank = jnp.zeros((tile, LANES - HD), F32)

    def load(i, carry):
        at = pl.ds(pl.multiple_of(i * tile, tile), tile)
        for r in range(group):
            all_at = pl.ds(pl.multiple_of(r * part_rows + i * tile, tile), tile)
            grads = grad_refs[r][at, :].astype(F32)
            both = grads * ctx_refs[r][at, :].astype(F32)
            for h in range(heads):
                cols = slice(h * HD, (h + 1) * HD)
                delta = jnp.sum(both[:, cols], axis=1, keepdims=True)
                wide = jnp.concatenate([grads[:, cols], blank], axis=1)
                da_s[h, all_at, :] = place_three(wide, -delta, lane_tile, HD).astype(BF16)
        for b in range(rows // BLK // (part_rows // tile)):
            for ref in (*dk_even, *dk_odd, *dv_even, *dv_odd):
                ref[i * (rows // BLK // (part_rows // tile)) + b] = jnp.zeros((HD, LANES), F32)
        return carry

    lax.fori_loop(0, part_rows // tile, load, 0)
    for ref in (*dk_even, *dk_odd, *dv_even, *dv_odd):
        ref[rows // BLK] = jnp.zeros((HD, LANES), F32)
    together = 4

    def attend(i, carry):
        units = [(u, h) for u in range(together) for h in range(heads)]
        row = [i * together + u for u in range(together)]
        at = [pl.ds(pl.multiple_of(j * BLK, BLK), BLK) for j in row]
        place = [(row[u] * heads + h) * SLOTS for u, h in units]
        q = [qa_ref[h, at[u], :] for u, h in units]
        d_mixed = [da_s[h, at[u], :] for u, h in units]
        keys = [picked(ka_ref, loc_ref, h, place[n]) for n, (u, h) in enumerate(units)]
        values = [picked(va_ref, loc_ref, h, place[n]) for n, (u, h) in enumerate(units)]
        scores = [dot(a, b, ((1,), (1,))) for a, b in zip(q, keys)]
        d_prob = [dot(a, b, ((1,), (1,))) for a, b in zip(d_mixed, values)]
        prob = [jnp.exp2(t * RATE) for t in scores]
        d_scores = [(a * b).astype(BF16) for a, b in zip(prob, d_prob)]
        prob = [t.astype(BF16) for t in prob]
        d_q = [dot(a, b, ((1,), (0,))) for a, b in zip(d_scores, keys)]
        q_turned = [t.astype(F32).T[:HD].astype(BF16) for t in q]
        d_turned = [t.astype(F32).T[:HD].astype(BF16) for t in d_mixed]
        d_keys = [dot(a, b, ((1,), (0,))) for a, b in zip(q_turned, d_scores)]
        d_values = [dot(a, b, ((1,), (0,))) for a, b in zip(d_turned, prob)]
        for n, (u, h) in enumerate(units):
            dq_s[h, at[u], :] = (d_q[n] * SCALE).astype(BF16)
        for u in range(together):
            for s in range(SLOTS):
                for h in range(heads):
                    n = u * heads + h
                    to = loc_ref[place[n] + s]
                    cols = slice((s // 2) * LANES, (s // 2 + 1) * LANES)
                    dk_ref, dv_ref = (dk_odd[h], dv_odd[h]) if s % 2 else (dk_even[h], dv_even[h])
                    dk_ref[to] += d_keys[n][:, cols]
                    dv_ref[to] += d_values[n][:, cols]
        return carry

    lax.fori_loop(0, rows // BLK // together, attend, 0)
    low_lane = lane_ids((HD, LANES)) < BLK

    def finish(i, carry):
        at = [pl.ds(pl.multiple_of((2 * i + u) * BLK, BLK), BLK) for u in range(2)]
        turned = []
        for even, odd, factor in ((dk_even, dk_odd, SCALE), (dv_even, dv_odd, 1.0)):
            for h in range(heads):
                first = even[h][2 * i] + pltpu.roll(odd[h][2 * i], BLK, 1)
                second = pltpu.roll(even[h][2 * i + 1], BLK, 1) + odd[h][2 * i + 1]
                turned.append(jnp.where(low_lane, first, second) * factor)
        pair = pl.ds(pl.multiple_of(2 * i * BLK, 2 * BLK), 2 * BLK)
        for n in range(heads):
            both = jnp.concatenate([turned[2 * n], turned[2 * n + 1]], axis=0)
            out_ref[pair, n * LANES : (n + 1) * LANES] = both.T.astype(BF16)
        done = [dq_s[h, pair, :][:, :HD].astype(F32) for h in range(heads)]
        out_ref[pair, heads * LANES :] = jnp.concatenate(done, axis=1).astype(BF16)
        return carry

    lax.fori_loop(0, rows // BLK // 2, finish, 0)
    for copy in w_copies:
        copy.wait()
    out_copies = []
    for odd, hold, ref in ((1, send_s, send_ref), (0, keep_s, keep_ref)):

        def to_rows(i, carry, odd=odd, hold=hold):
            at = pl.ds(pl.multiple_of((2 * i + odd) * part_rows, BLK), part_rows)
            hold[i] = dot(out_ref[at, :], w_s[...], ((1,), (1,))).astype(hold.dtype)
            return carry

        lax.fori_loop(0, group // 2, to_rows, 0)
        out_copies.append(put(hold, ref, sem, count + 1 + odd))
    if fast:
        x_copy.wait()
        sums = jnp.zeros((1, out_ref.shape[1]), F32)
        for r in range(group):
            sums = sums + row_sum(out_ref[r * part_rows : (r + 1) * part_rows, :].astype(F32))
        shape = (64, sums.shape[1])
        tail = jnp.where(
            lax.broadcasted_iota(jnp.int32, shape, 0) == 0, jnp.broadcast_to(sums, shape), 0.0
        )
        for k, ref in ((1, theirs_ref), (0, mine_ref)):
            cols = pl.ds(pl.multiple_of((at_ref[0] ^ k) * w_rows, LANES), w_rows)
            half = dot(x_s[:, cols], out_ref[...], ((0,), (0,)))
            half = jnp.concatenate([half, tail], axis=0).astype(BF16)
            size = half.shape[0] // 4
            for z in range(4):
                ref[plane_spot(z, at_ref[3])] = half[z * size : (z + 1) * size]
    for copy in out_copies:
        copy.wait()


def cost(microseconds):
    return pl.CostEstimate(flops=int(microseconds * WEIGHT), bytes_accessed=0, transcendentals=0)


def whole(memory):
    return pl.BlockSpec(memory_space=memory)


def attention_forward(turns, x_pieces, w_pieces, bias, heads, group, seqs, positions):
    chunks, width = group * seqs, x_pieces[0].shape[2]
    rows = positions * chunks
    counts = (len(x_pieces), len(w_pieces))
    kept = jax.ShapeDtypeStruct((heads, rows + BLK, LANES), BF16)
    return pl.pallas_call(
        partial(forward_kernel, heads, group, seqs, counts),
        out_shape=(
            jax.ShapeDtypeStruct((chunks, positions, width), BF16),
            jax.ShapeDtypeStruct((heads, rows, LANES), BF16),
            kept,
            kept,
            jax.ShapeDtypeStruct((rows // BLK * heads * SLOTS,), jnp.int32),
        )
        + (jax.ShapeDtypeStruct((rows // group, heads * HD), BF16),) * group,
        in_specs=[whole(pltpu.SMEM), whole(pltpu.VMEM)] + [whole(pl.ANY)] * sum(counts),
        out_specs=(whole(pl.ANY),) * 4 + (whole(pltpu.SMEM),) + (whole(pltpu.VMEM),) * group,
        scratch_shapes=[
            pltpu.VMEM((chunks, positions + 16, width), BF16),
            pltpu.VMEM((heads, rows, LANES), BF16),
            pltpu.VMEM((heads, rows + BLK, LANES), BF16),
            pltpu.VMEM((heads, rows + BLK, LANES), BF16),
            pltpu.VMEM((width, 3 * heads * HD), BF16),
            pltpu.VMEM((LANES, LANES), F32),
            pltpu.VMEM((chunks, LANES), jnp.int32),
            pltpu.SMEM((chunks, LANES), jnp.int32),
            pltpu.SemaphoreType.DMA((sum(counts) + 5 + chunks,)),
        ],
        compiler_params=pltpu.CompilerParams(vmem_limit_bytes=VMEM),
        cost_estimate=cost(19),
        name="attention_forward",
    )(turns, bias, *x_pieces, *w_pieces)


def attention_backward(loc, turns, qa, ka, va, x, w_pieces, ctx_parts, grads, heads, fast):
    rows, width = x.shape
    blocks, group, count, slab = rows // BLK, len(grads), len(w_pieces), heads * HD
    part = (group // 2, rows // group, width)
    piece = jax.ShapeDtypeStruct((4, (width // 2 + 64) // 4, 3 * slab), BF16)
    d_qkv = jax.ShapeDtypeStruct((rows, 3 * slab), BF16)
    outs = (jax.ShapeDtypeStruct(part, F32), jax.ShapeDtypeStruct(part, BF16))
    outs += (piece, piece) if fast else (d_qkv,)
    return pl.pallas_call(
        partial(backward_kernel, heads, group, count, fast),
        out_shape=outs,
        in_specs=[whole(pltpu.SMEM)] * 2
        + [whole(pltpu.VMEM)] * 3
        + [whole(pl.ANY)] * (1 + count)
        + [whole(pltpu.VMEM)] * (2 * group),
        out_specs=(whole(pl.ANY),) * 2 + (whole(pltpu.VMEM),) * (len(outs) - 2),
        scratch_shapes=[
            pltpu.VMEM((heads, rows, LANES), BF16),
            pltpu.VMEM((heads, rows, LANES), BF16),
            pltpu.VMEM((rows, width), BF16),
            pltpu.VMEM((width, 3 * slab), BF16),
            pltpu.VMEM(part, F32),
            pltpu.VMEM(part, BF16),
            pltpu.SemaphoreType.DMA((count + 3,)),
        ]
        + [pltpu.VMEM((blocks + 1, HD, LANES), F32)] * (4 * heads)
        + ([pltpu.VMEM((rows, 3 * slab), BF16)] if fast else []),
        compiler_params=pltpu.CompilerParams(vmem_limit_bytes=VMEM),
        cost_estimate=cost(50),
        name="attention_backward",
    )(loc, turns, qa, ka, va, x, *w_pieces, *ctx_parts, *grads)


def norm_values(values):
    average = jnp.mean(values, axis=-1, keepdims=True)
    centred = values - average
    inv_std = lax.rsqrt(jnp.mean(centred * centred, axis=-1, keepdims=True) + EPSILON)
    return centred * inv_std, inv_std


def norm_pull(upstream, scaled, inv_std, gain_row):
    weighted = upstream * gain_row
    centre_term = jnp.mean(weighted, axis=-1, keepdims=True)
    slope_term = jnp.mean(weighted * scaled, axis=-1, keepdims=True)
    return inv_std * (weighted - centre_term - scaled * slope_term)


def gelu_pair(v):
    rate = math.sqrt(2.0 / math.pi)
    square = v * v
    t = jnp.tanh(rate * v * (1.0 + 0.044715 * square))
    half = 0.5 * (1.0 + t)
    slope = half + (0.5 * rate) * v * (1.0 - t * t) * (1.0 + (3.0 * 0.044715) * square)
    return v * half, slope


def row_sum(values):
    return jnp.sum(values, axis=0, keepdims=True)


def layer_kernel(group, count, plan, seqs, fast, at_ref, x_ref, vec_ref, upb_ref, *rest):
    ctx_refs = rest[:group]
    arrays, rest = rest[group : group + count], rest[group + count :]
    cot_refs, result_refs, rest = rest[:seqs], rest[seqs : 2 * seqs], rest[2 * seqs :]
    if fast:
        dh1_ref, act_mine, pack_one, dsec_ref, dhid_mine, dbr_mine, pack_two, first_low_ref, small_ref = rest[:9]
        dctx_refs, rest = rest[9 : 9 + group], rest[9 + group :]
        slab = ctx_refs[0].shape[1]
    else:
        dh1_ref, active_ref, dhid_ref, first_low_ref, dsec_ref, dbr_ref, sums_out, upb_out = rest[:8]
        dctx_refs, rest = rest[8 : 8 + group], rest[8 + group :]
    out_s, up_s, down_s, slope_s, scaled_s, inv_s, acc_s, cot_s, result_s, x_s, dbr_s, sums_s, upb_s, sem = rest
    rows, width = acc_s.shape
    hidden = up_s.shape[1]
    member = at_ref[0]
    core = member & 1
    copies = []
    for k, (array, column, w) in enumerate(plan):
        scratch, source = (out_s, up_s, down_s)[w], arrays[array]
        if column is not None:
            source = source.at[:, pl.ds(column, scratch.shape[-1])]
        start = pl.multiple_of(at_ref[1 + k], 1 if w == 0 else 16)
        one = w == 0 and len(source.shape) == 2
        copies.append(put(source, scratch.at[start] if one else scratch.at[pl.ds(start, source.shape[0])], sem, k))
    k = len(plan)
    part_rows = rows // seqs
    starts = [p * part_rows for p in range(seqs)]
    cot_copies = gathered(cot_refs, starts, cot_s, sem, k)
    x_copy = put(x_ref.at[pl.ds(0, rows)], x_s, sem, k + 2 * seqs)
    b_out, b_first, b_last, b_second = (vec_ref[i : i + 1, :] for i in (2, 3, 4, 5))
    gain_one, gain_two = vec_ref[6:7, :], vec_ref[7:8, :]
    tile = min(256, rows)
    sums_s[...] = jnp.zeros_like(sums_s)

    for copy in [x_copy] + [copy for copy, (_, _, w) in zip(copies, plan) if w == 0]:
        copy.wait()

    def first_norm(i, carry):
        at = pl.ds(pl.multiple_of(i * tile, tile), tile)
        total = x_s[at, :].astype(F32) + b_out
        for r in range(group):
            total = total + dot(ctx_refs[r][at, :], out_s[member ^ r], ((1,), (0,)))
        scaled, inv_std = norm_values(total)
        first = scaled * gain_one + b_first
        scaled_s[at, :] = scaled
        inv_s[at, :] = jnp.broadcast_to(inv_std, (tile, LANES))
        first_low_ref[at, :] = first.astype(BF16)
        acc_s[at, :] = first + b_second
        return carry

    lax.fori_loop(0, rows // tile, first_norm, 0)
    for copy in [copy for copy, (_, _, w) in zip(copies, plan) if w > 0]:
        copy.wait()

    def up_down(start, step, ref, to):
        at = pl.ds(pl.multiple_of(start, step), step)
        v = dot(first_low_ref[...], up_s[:, at], ((1,), (0,))) + upb_ref[:, at]
        active, slope = gelu_pair(v)
        active = active.astype(BF16)
        ref[:, pl.ds(pl.multiple_of(to, step), step)] = active
        slope_s[:, at] = slope
        acc_s[...] += dot(active, down_s[at, :], ((1,), (0,)))

    def down_up(start, step, ref, to):
        at = pl.ds(pl.multiple_of(start, step), step)
        d_hidden = dot(dsec_ref[...], down_s[at, :], ((1,), (1,))) * slope_s[:, at]
        low = d_hidden.astype(BF16)
        ref[:rows, pl.ds(pl.multiple_of(to, step), step)] = low
        upb_s[:, at] = row_sum(low.astype(F32))
        acc_s[...] += dot(low, up_s[:, at], ((1,), (1,)))

    def over_hidden(one, refs):
        if fast:
            step = hidden // 4
            for c, ref in enumerate(refs):

                def part(i, carry, c=c, ref=ref):
                    turn = c ^ core
                    one((i * 2 + turn if one is up_down else turn * 2 + i) * step, step, ref, i * step)
                    return carry

                lax.fori_loop(0, 2, part, 0)
        else:
            step = 512

            def part(i, carry):
                one(i * step, step, refs[0], i * step)
                return carry

            lax.fori_loop(0, hidden // step, part, 0)

    over_hidden(up_down, (act_mine, pack_one) if fast else (active_ref,))
    for copy in cot_copies:
        copy.wait()

    def last_norm(i, carry):
        at = pl.ds(pl.multiple_of(i * tile, tile), tile)
        scaled, inv_std = norm_values(acc_s[at, :])
        result_s[at, :] = (scaled * gain_two + b_last).astype(BF16)
        upstream = cot_s[at, :].astype(F32)
        pulled = norm_pull(upstream, scaled, inv_std, gain_two)
        acc_s[at, :] = pulled
        low = pulled.astype(BF16)
        dsec_ref[at, :] = low
        if fast:
            pack_one[at, hidden // 2 :] = low
        sums_s[1:2, :] += row_sum(upstream * scaled)
        sums_s[4:5, :] += row_sum(upstream)
        sums_s[5:6, :] += row_sum(pulled)
        return carry

    lax.fori_loop(0, rows // tile, last_norm, 0)
    result_copies = [
        put(result_s.at[pl.ds(starts[p], part_rows)], result_refs[p], sem, k + seqs + p) for p in range(seqs)
    ]
    over_hidden(down_up, (dhid_mine, pack_two) if fast else (dhid_ref,))

    def first_back(i, carry):
        at = pl.ds(pl.multiple_of(i * tile, tile), tile)
        upstream, scaled = acc_s[at, :], scaled_s[at, :]
        pulled = norm_pull(upstream, scaled, inv_s[at, :1], gain_one)
        dh1_ref[at, :] = pulled
        low = pulled.astype(BF16)
        dbr_s[at, :] = low
        sums_s[0:1, :] += row_sum(upstream * scaled)
        sums_s[2:3, :] += row_sum(pulled)
        sums_s[3:4, :] += row_sum(upstream)
        for r in range(group):
            dctx_refs[r][at, :] = dot(low, out_s[member ^ r], ((1,), (1,))).astype(BF16)
        return carry

    lax.fori_loop(0, rows // tile, first_back, 0)
    if fast:
        half, wide = width // 2, hidden // 2
        dbr_mine[...] = dbr_s[:, pl.ds(pl.multiple_of(core * half, LANES), half)]
        pack_two[:rows, wide : wide + half] = dbr_s[:, pl.ds(pl.multiple_of((1 - core) * half, LANES), half)]
        pack_two[:rows, wide + half : wide + half + width] = first_low_ref[...]
        pack_two[:rows, wide + half + width :] = jnp.concatenate([ref[...] for ref in ctx_refs], axis=1)
        long = [upb_s[:, i * width : (i + 1) * width] for i in range(hidden // width)]
        blank = jnp.zeros((8 - len(long), width), F32)
        small = jnp.concatenate([sums_s[...], *long, blank], axis=0).astype(BF16)
        small_ref[...] = small
        pack_two[rows:, :width] = small
        pack_two[rows:, width:] = jnp.zeros((16, pack_two.shape[1] - width), BF16)
    else:
        dbr_ref[...] = dbr_s[...]
        sums_out[...] = sums_s[...]
        upb_out[...] = upb_s[...]
    for copy in result_copies:
        copy.wait()


def layer(place, x_seq, cots, vectors, up_shift, ctx_parts, parts, plan, fast):
    rows, width = len(cots) * cots[0].shape[0], x_seq.shape[1]
    group, slab = len(ctx_parts), ctx_parts[0].shape[1]
    hidden = up_shift.shape[1]

    def like(columns, dtype=BF16, count=rows):
        return jax.ShapeDtypeStruct((count, columns), dtype)

    half, wide = width // 2, hidden // 2
    if fast:
        outs = (like(width, F32), like(wide), like(wide + width), like(width), like(wide), like(half))
        outs += (like(wide + half + 2 * width, BF16, rows + 16), like(width), like(width, BF16, 16))
    else:
        outs = (like(width, F32), like(hidden), like(hidden), like(width), like(width), like(width))
        outs += (like(width, F32, 8), like(hidden, F32, 1))
    outs = (jax.ShapeDtypeStruct(cots[0].shape, BF16),) * len(cots) + outs + (like(slab),) * group
    return pl.pallas_call(
        partial(layer_kernel, group, len(parts), plan, len(cots), fast),
        out_shape=outs,
        in_specs=[whole(pltpu.SMEM), whole(pl.ANY)]
        + [whole(pltpu.VMEM)] * (2 + group)
        + [whole(pl.ANY)] * (len(parts) + len(cots)),
        out_specs=(whole(pl.ANY),) * len(cots) + (whole(pltpu.VMEM),) * (len(outs) - len(cots)),
        scratch_shapes=[
            pltpu.VMEM((group, slab, width), BF16),
            pltpu.VMEM((width, hidden), BF16),
            pltpu.VMEM((hidden, width), BF16),
            pltpu.VMEM((rows, hidden), F32),
            pltpu.VMEM((rows, width), F32),
            pltpu.VMEM((rows, LANES), F32),
            pltpu.VMEM((rows, width), F32),
            pltpu.VMEM((rows, width), BF16),
            pltpu.VMEM((rows, width), BF16),
            pltpu.VMEM((rows, width), BF16),
            pltpu.VMEM((rows, width), BF16),
            pltpu.VMEM((8, width), F32),
            pltpu.VMEM((1, hidden), F32),
            pltpu.SemaphoreType.DMA((len(plan) + 2 * len(cots) + 1,)),
        ],
        compiler_params=pltpu.CompilerParams(vmem_limit_bytes=VMEM),
        cost_estimate=cost(29),
        name="feed_forward",
    )(place, x_seq, vectors, up_shift, *ctx_parts, *parts, *cots)


def plane_spot(z, own):
    turn = z ^ own
    return (turn & 1) * 2 + (turn >> 1)


def down_grad_kernel(at_ref, act_ref, d_ref, got_ref, *outs):
    piece = outs[0].shape[2]
    chunk = 4 * piece
    wide = act_ref.shape[1]
    for f, ref in ((1, outs[1]), (0, outs[0])):
        for x in range(2):
            t = (f ^ at_ref[0]) * 2 + (x ^ at_ref[2])
            at = pl.ds(pl.multiple_of(t * chunk, LANES), chunk)
            grad = dot(act_ref[:, at], d_ref[...], ((0,), (0,)))
            grad = (grad + dot(got_ref[:, at], got_ref[:, wide:], ((0,), (0,)))).astype(BF16)
            for z in range(4):
                ref[x, plane_spot(z, at_ref[3])] = grad[z * piece : (z + 1) * piece]


def up_grad_kernel(at_ref, first_ref, dhid_ref, dbr_ref, small_ref, got_ref, *rest):
    ctx_refs, (keep_ref, send_ref), (first_s, ctx_s, extra_s) = rest[:4], rest[4:6], rest[6:]
    half, step = keep_ref.shape[2:]
    rows, width = first_ref.shape
    slab = ctx_refs[0].shape[1]
    wide, narrow = dhid_ref.shape[1], dbr_ref.shape[1]
    first_s[:, :rows] = first_ref[...].astype(F32).T.astype(BF16)
    first_s[:, rows:] = got_ref[:rows, wide + narrow : wide + narrow + width].astype(F32).T.astype(BF16)
    got_ctx = got_ref[:rows, wide + narrow + width :].astype(F32).T.astype(BF16)
    for r in range(4):
        ctx_s[at_ref[4] ^ r, :, :rows] = ctx_refs[r][...].astype(F32).T.astype(BF16)
        ctx_s[at_ref[4] ^ r ^ 1, :, rows:] = got_ctx[r * slab : (r + 1) * slab]
    extra_s[...] = jnp.zeros_like(extra_s)
    vectors = small_ref[...].astype(F32) + got_ref[rows:, :width].astype(F32)
    for f in range(2):
        for i in range(6):
            for k in range(half // LANES):
                start = f * half + k * LANES
                extra_s[f, i * (half // LANES) + k : i * (half // LANES) + k + 1, :] = vectors[
                    i : i + 1, start : start + LANES
                ]
        row = 6 * (half // LANES)
        for k in range(wide // LANES):
            start = f * wide + k * LANES
            extra_s[f, row + k : row + k + 1, :] = vectors[
                8 + start // width : 9 + start // width, start % width : start % width + LANES
            ]
    ups = wide // step
    for x, ref in ((1, send_ref), (0, keep_ref)):

        def one(i, carry, x=x, ref=ref):
            spot = (i & 1) * 2 + (i >> 1)
            k = (x ^ at_ref[2]) * 4 + (i ^ at_ref[3])

            def store(grad):
                for f in range(2):
                    ref[f ^ at_ref[0], spot] = grad[f * half : (f + 1) * half].astype(BF16)

            def out_grad(lanes):
                turned = ctx_s[...].reshape(width, 2 * rows)
                right = jnp.concatenate([dbr_ref[:, lanes], got_ref[:rows, wide + lanes.start : wide + lanes.stop]], axis=0)
                return dot(turned, right, ((1,), (0,)))

            @pl.when(k < ups)
            def _():
                at = pl.ds(pl.multiple_of(k * step, step), step)
                right = jnp.concatenate([dhid_ref[:, at], got_ref[:rows, at]], axis=0)
                store(dot(first_s[...], right, ((1,), (0,))))

            @pl.when(k == ups)
            def _():
                store(out_grad(slice(0, step)))

            @pl.when(k > ups)
            def _():
                extra = extra_s[...].reshape(width, LANES)
                store(jnp.concatenate([out_grad(slice(step, narrow)), extra], axis=1))

            return carry

        lax.fori_loop(0, 4, one, 0)


def down_final_kernel(at_ref, *rest):
    parts, (out_ref, in_s, out_s, sem) = rest[:4], rest[4:]
    piece = parts[0].shape[1]
    copies_in = [put(part, in_s.at[i], sem, i) for i, part in enumerate(parts)]
    copies = []
    for i in range(4):
        copies_in[i].wait()
        for z in range(4):
            k = (((i & 1) ^ at_ref[1]) * 2 + ((i >> 1) ^ at_ref[2])) * 4 + (z ^ at_ref[3])
            at = pl.ds(pl.multiple_of(k * piece, 16), piece)
            out_s[at, :] = in_s[i, (z & 1) * 2 + (z >> 1)].astype(F32)
            copies.append(put(out_s.at[at], out_ref.at[at], sem, 4 + i * 4 + z))
    for copy in copies:
        copy.wait()


def up_final_kernel(at_ref, early_ref, *rest):
    parts, (up_ref, out_ref, gains_ref, biases_ref, upb_ref, in_s, out_s, sem) = rest[:4], rest[4:]
    step = parts[0].shape[2]
    wide, narrow = up_ref.shape[1] // 2, out_ref.shape[1] // 2
    ups = wide // step
    half = gains_ref.shape[1]
    count = half // LANES
    copies_in = [put(part, in_s.at[i], sem, i) for i, part in enumerate(parts)]
    biases_ref[0:2, :] = early_ref[...]

    def each(i, z, act):
        core = (i & 1) ^ at_ref[1]
        k = ((i >> 1) ^ at_ref[2]) * 4 + (z ^ at_ref[3])
        n = i * 4 + z

        @pl.when(k < ups)
        def _():
            at = pl.ds(pl.multiple_of(core * wide + k * step, LANES), step)
            act(pltpu.make_async_copy(out_s.at[n], up_ref.at[:, at], sem.at[4 + n]))

        @pl.when(k == ups)
        def _():
            at = pl.ds(pl.multiple_of(core * narrow, LANES), step)
            act(pltpu.make_async_copy(out_s.at[n], out_ref.at[:, at], sem.at[4 + n]))

        @pl.when(k > ups)
        def _():
            at = pl.ds(pl.multiple_of(core * narrow + step, LANES), LANES)
            act(pltpu.make_async_copy(out_s.at[n, :, pl.ds(0, LANES)], out_ref.at[:, at], sem.at[4 + n]))

        return core, k

    for i in range(4):
        copies_in[i].wait()
        for z in range(4):
            value = in_s[i, (z & 1) * 2 + (z >> 1)].astype(F32)
            out_s[i * 4 + z] = value
            core, k = each(i, z, lambda copy: copy.start())

            @pl.when((k > ups) & (core == 0))
            def _(value=value):
                extra = value[:, LANES:]
                for a in range(6):
                    for b in range(count):
                        row = extra[a * count + b : a * count + b + 1]
                        lanes = slice(b * LANES, (b + 1) * LANES)
                        if a < 2:
                            gains_ref[a : a + 1, lanes] = row
                        else:
                            biases_ref[a : a + 1, lanes] = row
                for b in range(upb_ref.shape[1] // LANES):
                    upb_ref[:, b * LANES : (b + 1) * LANES] = extra[6 * count + b : 6 * count + b + 1]

    for i in range(4):
        for z in range(4):
            each(i, z, lambda copy: copy.wait())


def qkv_final_kernel(at_ref, *rest):
    parts, (out_ref, early_ref, hold, in_s, out_s, sums_s, sem) = rest[:4], rest[4:]
    half, slab = out_s.shape[0], hold.shape[2] // 3
    width = 4 * slab
    size = parts[0].shape[1]
    copies = [put(part, in_s.at[i], sem, i) for i, part in enumerate(parts)]
    for r in range(4):
        copies[r].wait()
        for z in range(4):
            at = pl.ds(pl.multiple_of((z ^ at_ref[3]) * size, 16), size)
            hold[at_ref[4] ^ r, at, :] = in_s[r, (z & 1) * 2 + (z >> 1)]
    outs = []
    for k, column in ((0, 1), (1, 2), (2, 0)):
        for m in range(4):
            cols = slice(column * width + m * slab, column * width + (m + 1) * slab)
            out_s[:, cols] = hold[m, :half, k * slab : (k + 1) * slab].astype(F32)
        at = pl.ds(column * width, width)
        outs.append(put(out_s.at[:, at], out_ref.at[:, at], sem, 4 + k))
    for k, row in ((2, 0), (1, 1)):
        sums = [hold[m, half : half + 16, k * slab : (k + 1) * slab].astype(F32)[:1] for m in range(4)]
        sums_s[row : row + 1, :] = jnp.concatenate(sums, axis=1)
    early_ref[...] = sums_s[0:2, pl.ds(pl.multiple_of(at_ref[0] * half, LANES), half)]
    for copy in outs:
        copy.wait()


def local_call(kernel, outs, ins, scratch, name, time=3, loose=()):
    return pl.pallas_call(
        kernel,
        out_shape=outs,
        in_specs=[whole(pltpu.SMEM)]
        + [whole(pl.ANY if i in loose else pltpu.VMEM) for i in range(1, len(ins))],
        out_specs=tuple(whole(pl.ANY if len(ins) + i in loose else pltpu.VMEM) for i in range(len(outs))),
        scratch_shapes=scratch,
        compiler_params=pltpu.CompilerParams(vmem_limit_bytes=VMEM),
        cost_estimate=cost(time),
        name=name,
    )(*ins)


def swap_joint(value, f_mask, c_mask):
    n_f, n_c = lax.axis_size("fsdp"), lax.axis_size("ctx")
    pairs = [(f * n_c + c, (f ^ f_mask) * n_c + (c ^ c_mask)) for f in range(n_f) for c in range(n_c)]
    return lax.ppermute(value, ("fsdp", "ctx"), pairs)


def sum_planes(own, others):
    total = own.astype(F32)
    for other in others:
        total = total + other.astype(F32)
    return total.astype(BF16)


def reduce_square(keep, got, after, axis, mask):
    first, second = sum_planes(gate(keep[0], after), [got[0]]), sum_planes(keep[1], [got[1]])
    return first, swap(second, axis, mask)


def reduce_planes(mine, *after):
    two = sum_planes(gate(mine[:2], *after[:1]), [swap(mine[2:], "ctx", 4)])
    piece = sum_planes(gate(two[0], *after[1:]), [swap(two[1], "ctx", 8)])
    two = jnp.stack([piece, swap(piece, "ctx", 8)])
    four = jnp.concatenate([two, swap(two, "ctx", 4)])
    across = swap(four, "ctx", 2)
    return [four, swap(four, "ctx", 1), across, swap(across, "ctx", 1)]


def gather_fsdp(value):
    index = lax.axis_index("fsdp")
    parts = [value]
    for bit in bits_of(lax.axis_size("fsdp")):
        parts += [swap(part, "fsdp", bit) for part in parts]
    return to_absolute(parts, index)


def fetch_halves(value):
    half = value.shape[0] // 2
    parts = [lax.dynamic_slice_in_dim(value, (lax.axis_index("ctx") & 1) * half, half, 0)]
    for bit in bits_of(lax.axis_size("fsdp")):
        parts += [swap(part, "fsdp", bit) for part in parts]
    return parts[1:]


def weight_parts(value, halves):
    index = lax.axis_index("fsdp")
    core = lax.axis_index("ctx") & 1
    size = value.shape[0]
    half = size // 2
    pieces, places = [value], [index * size]
    for k, part in enumerate(halves, 1):
        pieces += [part, swap(part, "ctx", 1)]
        first = (index ^ k) * size
        places += [first + core * half, first + (1 - core) * half]
    return pieces, places


def halve(value, axis, dim, mask, index):
    half = value.shape[dim] // 2
    bit = (index // mask) & 1
    mine = lax.dynamic_slice_in_dim(value, bit * half, half, dim)
    theirs = lax.dynamic_slice_in_dim(value, (1 - bit) * half, half, dim)
    return mine + swap(theirs.astype(BF16), axis, mask).astype(F32)


def double(value, axis, dim, mask, index):
    bit = (index // mask) & 1
    other = swap(value, axis, mask)
    return lax.select_n(
        bit,
        jnp.concatenate([value, other], axis=dim),
        jnp.concatenate([other, value], axis=dim),
    )


def reduce_over_all(value):
    f_index, c_index = lax.axis_index("fsdp"), lax.axis_index("ctx")
    value = halve(value, "ctx", 1, 1, c_index)
    for bit in reversed(bits_of(lax.axis_size("fsdp"))):
        value = halve(value, "fsdp", 0, bit, f_index)
    value = value[0]
    rest = bits_of(lax.axis_size("ctx"))[1:]
    for bit in rest:
        value = halve(value, "ctx", 0, bit, c_index)
    value = value.astype(BF16)
    for bit in reversed(rest):
        value = double(value, "ctx", 0, bit, c_index)
    return double(value, "ctx", 0, 1, c_index).astype(F32)


def local(
    tokens, segments, rand_blocks, w_qkv, w_out, w_up, w_down, ln_gains, biases, up_bias, cotangent
):
    positions, seq_count, width = tokens.shape
    n_f, n_c = lax.axis_size("fsdp"), lax.axis_size("ctx")
    f_index, c_index = lax.axis_index("fsdp"), lax.axis_index("ctx")
    group = n_c // seq_count
    plane, member = c_index // group, c_index % group
    head_count = width // HD
    heads = -(-head_count // group)
    per_chunk = positions // BLK
    blocks = per_chunk * n_c
    rows_here = seq_count * positions
    f_width = width // n_f
    slab = heads * HD
    spare = group * slab - width

    def to_planes(parts):
        return [swap(part, "ctx", p * group) if p else part for p, part in enumerate(parts)]

    def from_planes(parts):
        return jnp.stack(to_absolute(parts, plane), axis=1)

    fast = n_f == 2 and group == 4 and seq_count == 4 and not spare and f_width % slab == 0
    turns = jnp.stack([f_index, member & 1, (member >> 1) & 1, plane, member, c_index])
    rand = jnp.pad(rand_blocks, ((0, 0), (0, 0), (0, group * heads - head_count), (0, 0)))
    rand = rand.reshape(seq_count, per_chunk, group, heads, -1).transpose(0, 2, 1, 3, 4)
    rand = rand.reshape(seq_count, group, -1)
    rand = jnp.pad(rand, ((0, 0), (0, 0), (0, LANES // group - rand.shape[2])))
    line = jnp.concatenate([segments.T, rand.reshape(seq_count, LANES)], axis=1).astype(BF16)
    line = jnp.pad(line, ((0, 0), (0, width - line.shape[1])))
    token_parts = split_planes(turns, tokens, line)
    w_qkv, small_in = lax.optimization_barrier(((w_qkv, (ln_gains, biases, up_bias)), *token_parts))[0]
    ln_gains, biases, up_bias = small_in
    x_rows = to_planes(token_parts)
    if fast:
        across = [swap(part, "ctx", 2) for part in x_rows]
        x_pieces = [*x_rows, swap(jnp.concatenate(x_rows), "ctx", 1), *across]
        x_pieces += [swap(part, "ctx", 1) for part in across]
    else:
        x_all = {(0, p): x_rows[p] for p in range(seq_count)}
        for bit in reversed(bits_of(group)):
            for r, p in list(x_all):
                x_all[r ^ bit, p] = swap(x_all[r, p], "ctx", bit)
        x_pieces = [x_all[r, p] for r in range(group) for p in range(seq_count)]

    w_parts = jnp.pad(w_qkv.reshape(-1, 3, width), ((0, 0), (0, 0), (0, spare))) if spare else None
    if spare:
        w_mine = [lax.dynamic_slice_in_dim(w_parts[:, k], member * slab, slab, 1) for k in (1, 2, 0)]
    else:
        w_mine = [lax.dynamic_slice_in_dim(w_qkv, k * width + member * slab, slab, 1) for k in (1, 2, 0)]
    small = jnp.concatenate([ln_gains.reshape(-1), biases.reshape(-1), up_bias])
    small_rows = -(-small.shape[0] // (3 * slab) // 16) * 16
    small_count = small.shape[0]
    small = jnp.pad(small, (0, small_rows * 3 * slab - small_count)).reshape(small_rows, 3 * slab)
    w_mine = jnp.concatenate([jnp.concatenate(w_mine, axis=1), small], axis=0)
    w_pieces = [w_mine]
    for bit in bits_of(n_f):
        w_pieces += [swap(part, "fsdp", bit) for part in w_pieces]
    small = [part[f_width:].reshape(-1)[:small_count] for part in w_pieces]
    small = jnp.stack(to_absolute(small, f_index)).astype(F32)
    gains_all = small[:, : 2 * f_width].reshape(n_f, 2, f_width).transpose(1, 0, 2).reshape(2, width)
    biases_all = (
        small[:, 2 * f_width : 8 * f_width].reshape(n_f, 6, f_width).transpose(1, 0, 2).reshape(6, width)
    )
    up_shift = small[:, 8 * f_width :].reshape(-1)
    bias_mine = lax.dynamic_slice_in_dim(
        jnp.pad(biases_all[:2], ((0, 0), (0, spare))), member * slab, slab, 1
    ).reshape(2, heads, HD)
    bias_wide = jnp.concatenate(
        [jnp.zeros_like(bias_mine[0]), bias_mine[1], bias_mine[0]], axis=0
    ).reshape(1, -1)

    cot_in = gate(cotangent, x_rows)
    cots = to_planes([lax.dynamic_index_in_dim(cot_in, plane ^ p, 1, keepdims=False) for p in range(seq_count)])
    if fast:
        core, chip = member & 1, member >> 1
        quarter, half = f_width // 4, f_width // 2
        up_quarter = lax.dynamic_slice_in_dim(w_up, (core * 2 + chip) * quarter, quarter, 0)
        up_quarter = swap(gate(up_quarter, w_mine, across[0]), "fsdp", 1)
        up_across = swap(up_quarter, "ctx", 2)
        tall = w_down.shape[0] // 2
        joint = lax.dynamic_slice_in_dim(w_down, core * tall, tall, 0).reshape(-1, half, width)
        joint = [lax.dynamic_slice_in_dim(w_out, core * half, half, 0), *joint]
        joint = swap(gate(jnp.concatenate(joint, axis=1), up_quarter), "fsdp", 1)
        bias_wide = gate(bias_wide, up_quarter)
    else:
        up_halves = fetch_halves(w_up)
        down_halves = fetch_halves(w_down)
    x_pieces = [piece.reshape(-1, positions + 16, width) for piece in x_pieces]
    x_seq, qa, ka, va, loc, *ctx_parts = attention_forward(
        turns, x_pieces, w_pieces, bias_wide, heads, group, seq_count, positions
    )
    x_seq = x_seq.reshape(blocks * BLK, width)
    if fast:
        ctx_parts, up_across, cots = lax.optimization_barrier((ctx_parts, up_across, cots))
        up_other = [swap(part, "ctx", 1) for part in (up_quarter, up_across)]
    ctx_mine = ctx_parts
    ctx_parts = [swap(part, "ctx", r) if r else part for r, part in enumerate(ctx_parts)]
    if fast:
        joint_other = swap(gate(joint, ctx_parts[1]), "ctx", 1)
        parts = [w_out.reshape(2, slab, width), w_up, w_down, up_quarter, up_across, *up_other, joint, joint_other]
        plan = [(0, None, 0), (1, None, 1), (2, None, 2)] + [(3 + k, None, 1) for k in range(4)]
        theirs = 1 - f_index
        places = [2 * f_index, f_index * f_width, f_index * 2 * tall]
        for k in range(4):
            part = (core ^ (k >> 1)) * 2 + (chip ^ (k & 1))
            places.append(theirs * f_width + part * quarter)
        for k in range(2):
            plan += [(7 + k, n * width, 0 if n == 0 else 2) for n in range(1 + tall // half)]
            places.append(2 * theirs + (core ^ k))
            places += [theirs * 2 * tall + (core ^ k) * tall + n * half for n in range(tall // half)]
    else:
        out_full = jnp.concatenate(gather_fsdp(w_out), axis=0)
        out_full = jnp.pad(out_full, ((0, spare), (0, 0))).reshape(group, slab, width)
        up_parts, up_places = weight_parts(w_up, up_halves)
        down_parts, down_places = weight_parts(w_down, down_halves)
        parts, places = [out_full, *up_parts, *down_parts], [0, *up_places, *down_places]
        plan = [(0, None, 0)] + [(1 + k, None, 1) for k in range(len(up_parts))]
        plan += [(1 + len(up_parts) + k, None, 2) for k in range(len(down_parts))]
    vectors = jnp.concatenate([biases_all, gains_all])
    place = jnp.stack([member] + [jnp.int32(p) for p in places])
    done = layer(
        place,
        x_seq,
        cots,
        vectors,
        up_shift.reshape(1, -1),
        ctx_parts,
        parts,
        plan,
        fast,
    )
    results, d_parts, done = done[:seq_count], done[-group:], done[seq_count:-group]
    d_parts = [swap(part, "ctx", r) if r else part for r, part in enumerate(d_parts)]
    results = to_planes(results)
    back = partial(attention_backward, loc, turns, qa, ka, va, x_seq, w_pieces)
    hidden_width = w_up.shape[1]
    used = 6 * f_width + hidden_width // n_f

    if fast:
        dh1, act_mine, pack_one, d_second, dhid_mine, dbr_mine, pack_two, first_low, small_sums = done
        piece = hidden_width // n_f // 16
        pack_one = swap(gate(pack_one, d_parts[1]), "ctx", 1)
        pack_two = swap(gate(pack_two, pack_one), "ctx", 1)
        shape = jax.ShapeDtypeStruct((2, 4, piece, width), BF16)
        down_keep, down_send = local_call(
            down_grad_kernel,
            (shape,) * 2,
            (turns, gate(act_mine, d_parts), d_second, pack_one),
            [],
            "down_grad",
        )
        step = (hidden_width + width + 256) // 16
        shape = jax.ShapeDtypeStruct((2, 4, f_width, step), BF16)
        up_keep, up_send = local_call(
            up_grad_kernel,
            (shape,) * 2,
            (
                turns,
                first_low,
                dhid_mine,
                dbr_mine,
                gate(small_sums, d_parts),
                pack_two,
                *ctx_parts,
            ),
            [
                pltpu.VMEM((width, 2 * rows_here), BF16),
                pltpu.VMEM((group, slab, 2 * rows_here), BF16),
                pltpu.VMEM((2, f_width, LANES), F32),
            ],
            "up_grad",
        )
        d_parts = gate(d_parts, down_send, up_send)
        down_got, up_got = swap(down_send, "fsdp", 1), swap(up_send, "ctx", 2)
        keep, send, mine, theirs = back(ctx_mine, d_parts, heads, fast)
        down_first, down_got = reduce_square(down_keep, down_got, send, "ctx", 2)
        up_first, up_got = reduce_square(up_keep, up_got, send, "fsdp", 1)
        output = from_planes([gate(results[0], send)] + results[1:])
        keep, send, mine, theirs, down_first, up_first, output = lax.optimization_barrier(
            (keep, send, mine, theirs, down_first, up_first, output)
        )
        cores = swap(send, "ctx", 1)
        down_mine = sum_planes(gate(down_first, cores), [down_got])
    else:
        dh1, active, d_hidden, first_low, d_second, d_branch, sums, upb_grad = done
        keep, send, d_qkv = back(ctx_mine, d_parts, heads, fast)
        output = from_planes(results)
        context_low = jnp.concatenate(to_absolute(ctx_parts, member), axis=1)[:, :width]
        grad_down = dot(active, d_second, ((0,), (0,)))
        grad_up = dot(first_low, d_hidden, ((0,), (0,)))
        grad_out = dot(context_low, d_branch, ((0,), (0,)))
        down_total = reduce_over_all(grad_down.reshape(n_f, -1, width))
        vectors = sums[:6].reshape(6, n_f, f_width).transpose(1, 0, 2).reshape(n_f, -1)
        vectors = jnp.concatenate([vectors, upb_grad.reshape(n_f, -1)], axis=1)
        extra = -(-used // f_width // LANES) * LANES
        vectors = jnp.pad(vectors, ((0, 0), (0, f_width * extra - used))).reshape(n_f, f_width, extra)
        up_out = jnp.concatenate(
            [grad_up.reshape(n_f, f_width, -1), grad_out.reshape(n_f, f_width, -1), vectors], axis=2
        )
        up_out = reduce_over_all(up_out)
        up_total = up_out[:, :hidden_width]
        out_total = up_out[:, hidden_width : hidden_width + width]
        vectors = up_out[:, hidden_width + width :].reshape(-1)
        gains_total = vectors[: 2 * f_width].reshape(2, f_width)
        biases_late = vectors[2 * f_width : 6 * f_width].reshape(4, f_width)
        up_bias_total = vectors[6 * f_width : used]

    if not fast:
        cores = swap(send, "ctx", 1)
    shape = (seq_count, positions, width)
    pieces = {2 * i: list((keep[i] + cores[i].astype(F32)).reshape(shape)) for i in range(group // 2)}
    far, close = [], []
    for bit in bits_of(group)[1:]:
        for r in [r for r in pieces if r & bit]:
            part = jnp.stack(pieces.pop(r)).astype(BF16)
            cut = seq_count // 2
            far, close = swap(part[cut:], "ctx", bit), swap(part[:cut], "ctx", bit)
            got = [*close, *far]
            pieces[r ^ bit] = [pieces[r ^ bit][p] + got[p].astype(F32) for p in range(seq_count)]
    dh1 = dh1.reshape(shape)
    input_grad = from_planes(
        to_planes([(dh1[p] + pieces[0][p]).astype(BF16) for p in range(seq_count)])
    )

    if fast:
        got = swap(theirs, "fsdp", 1)
        down_parts = reduce_planes(down_mine, far, close)
        up_parts = reduce_planes(sum_planes(gate(up_first, close), [up_got]))
        qkv_parts = reduce_planes(sum_planes(gate(mine, close), [got]))
        four = range(1, 5)
        down_total = local_call(
            down_final_kernel,
            (jax.ShapeDtypeStruct((hidden_width // n_f, width), F32),),
            (turns, *down_parts),
            [
                pltpu.VMEM((4, 4, piece, width), BF16),
                pltpu.VMEM((hidden_width // n_f, width), F32),
                pltpu.SemaphoreType.DMA((20,)),
            ],
            "down_final",
            loose=(*four, 5),
        )[0]
        qkv_total, early = local_call(
            qkv_final_kernel,
            (jax.ShapeDtypeStruct((f_width, 3 * width), F32), jax.ShapeDtypeStruct((2, f_width), F32)),
            (turns, *qkv_parts),
            [
                pltpu.VMEM((4, f_width + 64, 3 * slab), BF16),
                pltpu.VMEM((4, 4, (f_width + 64) // 4, 3 * slab), BF16),
                pltpu.VMEM((f_width, 3 * width), F32),
                pltpu.VMEM((8, width), F32),
                pltpu.SemaphoreType.DMA((7,)),
            ],
            "qkv_final",
            loose=(*four, 5),
        )
        up_total, out_total, gains_total, biases_total, up_bias_total = local_call(
            up_final_kernel,
            (
                jax.ShapeDtypeStruct((f_width, hidden_width), F32),
                jax.ShapeDtypeStruct((f_width, width), F32),
                jax.ShapeDtypeStruct((2, f_width), F32),
                jax.ShapeDtypeStruct((6, f_width), F32),
                jax.ShapeDtypeStruct((1, hidden_width // n_f), F32),
            ),
            (turns, early, *up_parts),
            [
                pltpu.VMEM((4, 4, f_width, step), BF16),
                pltpu.VMEM((16, f_width, step), F32),
                pltpu.SemaphoreType.DMA((20,)),
            ],
            "up_final",
            loose=(2, 3, 4, 5, 6, 7),
        )
        up_bias_total = up_bias_total.reshape(-1)
    else:
        grad_qkv = dot(x_seq, d_qkv, ((0,), (0,))).reshape(n_f, f_width, 3 * slab)
        sums = jnp.sum(d_qkv.astype(F32), axis=0, keepdims=True)
        sums = jnp.pad(sums, ((0, 15), (0, 0)))
        value = jnp.concatenate([grad_qkv, jnp.broadcast_to(sums[None], (n_f,) + sums.shape)], axis=1)
        for bit in reversed(bits_of(n_f)):
            value = halve(value, "fsdp", 0, bit, f_index)
        value = value[0]
        plane_bits = [bit * group for bit in bits_of(seq_count)]
        for bit in plane_bits:
            value = halve(value, "ctx", 0, bit, c_index)
        value = value.astype(BF16)
        for bit in reversed(plane_bits):
            value = double(value, "ctx", 0, bit, c_index)
        parts = [value]
        for bit in bits_of(group):
            parts += [swap(part, "ctx", bit) for part in parts]
        parts = to_absolute(parts, member)
        qkv_total = jnp.stack([part.reshape(-1, 3, slab) for part in parts], axis=2).reshape(-1, 3, group * slab)
        qkv_total = jnp.concatenate([qkv_total[:, 2:], qkv_total[:, :2]], axis=1)[:, :, :width].astype(F32)
        early = lax.dynamic_slice_in_dim(qkv_total[f_width][0::2], f_index * f_width, f_width, 1)
        qkv_total = qkv_total[:f_width].reshape(f_width, 3 * width)
        biases_total = jnp.concatenate([early, biases_late])
    return (
        output,
        input_grad,
        qkv_total,
        out_total,
        up_total,
        down_total,
        gains_total,
        biases_total,
        up_bias_total,
    )


def solution(mesh):
    placed = (
        P("ctx", "fsdp", None),
        P("ctx", "fsdp"),
        P("fsdp", "ctx", None, None),
        P("fsdp", None),
        P("fsdp", None),
        P("fsdp", None),
        P("fsdp", None),
        P(None, "fsdp"),
        P(None, "fsdp"),
        P("fsdp"),
        P("ctx", "fsdp", None),
    )
    return jax.shard_map(
        local,
        mesh=mesh,
        in_specs=placed,
        out_specs=(
            P("ctx", "fsdp", None),
            P("ctx", "fsdp", None),
            P("fsdp", None),
            P("fsdp", None),
            P("fsdp", None),
            P("fsdp", None),
            P(None, "fsdp"),
            P(None, "fsdp"),
            P("fsdp"),
        ),
        check_vma=False,
    )
```

```python
import math
from functools import partial

import jax
import jax.numpy as jnp
from jax import lax
from jax.experimental import pallas as pl
from jax.experimental.pallas import tpu as pltpu
from jax.sharding import PartitionSpec as P

HD = 64
BLK = 64
LANES = 128
SLOTS = 8
DOCS = 32
EPSILON = 1e-06
NEGATIVE = -1e30
SCALE = HD**-0.5
RATE = SCALE / math.log(2.0)
MIB = 1024 * 1024
WEIGHT = 0

BF16 = jnp.bfloat16
F32 = jnp.float32


def dot(left, right, dims):
    return lax.dot_general(left, right, ((dims[0], dims[1]), ((), ())), preferred_element_type=F32)


def swap(value, axis, mask):
    count = lax.axis_size(axis)
    return lax.ppermute(value, axis, [(i, i ^ mask) for i in range(count)])


def gate(value, *after):
    return lax.optimization_barrier((value, *after))[0]


def bits_of(count):
    return [1 << k for k in range((count - 1).bit_length())]


def choose(index, cases):
    return cases[0] if len(cases) == 1 else lax.select_n(index, *cases)


def to_absolute(relative, index):
    count = len(relative)
    return [choose(index, [relative[k ^ i] for i in range(count)]) for k in range(count)]


def split_three(values):
    high = values.astype(BF16)
    rest = values - high.astype(F32)
    middle = rest.astype(BF16)
    return high, middle, (rest - middle.astype(F32)).astype(BF16)


def lane_ids(shape):
    return lax.broadcasted_iota(jnp.int32, shape, len(shape) - 1)


def place_three(base, values, lane, first):
    high, middle, small = split_three(values)
    base = jnp.where(lane == first, high.astype(F32), base)
    base = jnp.where(lane == first + 1, middle.astype(F32), base)
    return jnp.where(lane == first + 2, small.astype(F32), base)


def picked(ref, loc_ref, head, place):
    parts = [
        ref[head, pl.ds(pl.multiple_of(loc_ref[place + s] * BLK, BLK), BLK), :]
        for s in range(SLOTS)
    ]
    return jnp.concatenate(parts, axis=0)


def gathered(pieces, places, target, sem, first):
    copies = []
    for k, (piece, place) in enumerate(zip(pieces, places)):
        copy = pltpu.make_async_copy(piece, target.at[pl.ds(place, piece.shape[0])], sem.at[first + k])
        copy.start()
        copies.append(copy)
    return copies


def put(source, target, sem, place):
    copy = pltpu.make_async_copy(source, target, sem.at[place])
    copy.start()
    return copy


def over(value, size):
    assert size & (size - 1) == 0
    return lax.shift_right_logical(value, size.bit_length() - 1)


def within(value, size):
    assert size & (size - 1) == 0
    return value & (size - 1)


def absolute_chunk(turn, own, seqs, group):
    return (within(turn, seqs) * group + over(turn, seqs)) ^ own


def split_kernel(tail, at_ref, rows_ref, *rest):
    positions, seqs, width = rows_ref.shape
    if tail:
        line_ref, *rest = rest
    for p, ref in enumerate(rest):
        for s in range(seqs):

            @pl.when((at_ref[3] ^ p) == s)
            def _(ref=ref, s=s):
                ref[:positions, :] = rows_ref[:, s, :]
                if tail:
                    blank = jnp.zeros((tail - 1, width), F32)
                    line = line_ref[s : s + 1, :].astype(F32)
                    ref[positions:, :] = jnp.concatenate([line, blank], axis=0).astype(BF16)


def split_planes(turns, rows, line=None):
    positions, seqs, width = rows.shape
    tail = 0 if line is None else 16
    shape = jax.ShapeDtypeStruct((positions + tail, width), BF16)
    ins = (turns, rows) if line is None else (turns, rows, line)
    return local_call(partial(split_kernel, tail), (shape,) * seqs, ins, [], "split_planes")


def forward_kernel(heads, group, seqs, counts, at_ref, bias_ref, *rest):
    x_pieces, w_pieces, rest = rest[: counts[0]], rest[counts[0] : sum(counts)], rest[sum(counts) :]
    x_out, q_out, k_out, v_out, loc_ref = rest[:5]
    near, far, rest = rest[5 : 5 + group // 2], rest[5 + group // 2], rest[6 + group // 2 :]
    ctx_refs = [*near, *[far.at[r] for r in range(group // 2)]]
    x_s, q_s, k_s, v_s, w_s, seg_s, number_v, number_s, sem = rest
    chunks, tall, width = x_s.shape
    chunk, blocks = x_out.shape[1], q_s.shape[1] // BLK
    rows = chunks * chunk
    w_rows = width // counts[1]
    w_copies = gathered(
        [piece.at[pl.ds(0, w_rows)] for piece in w_pieces],
        [pl.multiple_of((at_ref[0] ^ k) * w_rows, 16) for k in range(counts[1])],
        w_s,
        sem,
        counts[0],
    )
    last = sum(counts)
    x_copies, turn = [], 0
    for piece in x_pieces:
        count = piece.shape[0]
        x_copies.append(put(piece, x_s.at[pl.ds(turn, count)], sem, last + 5 + turn))
        turn += count
    for copy in w_copies:
        copy.wait()
    for copy in x_copies:
        copy.wait()
    out_copies = [put(x_s.at[:, pl.ds(0, chunk)], x_out, sem, last)]
    tile = 2 * chunk
    lines = jnp.concatenate(
        [x_s[k, chunk:, : 2 * LANES].astype(F32)[:1] for k in range(chunks)], axis=0
    )
    number_v[...] = lines[:, LANES:].astype(jnp.int32)
    number_copy = put(number_v, number_s, sem, last + 4)
    seg_s[...] = jnp.concatenate([lines[:, :LANES], jnp.zeros((LANES - chunks, LANES), F32)], axis=0).T
    number_copy.wait()
    per = chunk // BLK
    own, member = at_ref[5], at_ref[4]

    def place_of(block):
        c = over(block, per) ^ own
        return (within(c, group) * seqs + over(c, group)) * per + within(block, per)

    def slots_of(j):
        turn, inner = over(j, per), within(j, per)
        real = absolute_chunk(turn, own, seqs, group) * per + inner
        fixed = []
        for d in (-1, 0, 1):
            near = jnp.clip(real + d, 0, blocks - 1)
            fixed.append(jnp.where(near == real + d, place_of(near), blocks))
        for b in range(2):
            fixed.append(jnp.where(jnp.abs(real - b) > 1, place_of(jnp.int32(b)), blocks))
        first = member * (LANES // group) + inner * (heads * 3)
        for h in range(heads):
            free = [place_of(number_s[turn, first + h * 3 + r]) for r in range(3)]
            for s, value in enumerate(fixed + free):
                loc_ref[(j * heads + h) * SLOTS + s] = value

    def project(i, carry):
        at = pl.ds(pl.multiple_of(i * tile, tile), tile)
        x = jnp.concatenate([x_s[2 * i, :chunk, :], x_s[2 * i + 1, :chunk, :]], axis=0)
        lane = lane_ids((tile, LANES))
        seg = []
        for k in range(2):
            mine = lane_ids((LANES, LANES)) == 2 * i + k
            seg.append(jnp.sum(jnp.where(mine, seg_s[...], 0.0), axis=1, keepdims=True))
        same = (lane - HD).astype(F32) == jnp.concatenate(seg, axis=0)
        coded = (lane >= HD) & (lane < HD + DOCS)
        ones = (lane >= HD + DOCS) & (lane < HD + DOCS + 3)
        q_extra = jnp.where(coded & same, NEGATIVE, 0.0)
        k_extra = jnp.where((coded & jnp.logical_not(same)) | ones, 1.0, 0.0)
        v_extra = jnp.where((lane >= HD) & (lane < HD + 3), 1.0, 0.0)
        head_lane = lane < HD
        y = dot(x, w_s[...], ((1,), (0,))) + bias_ref[...]
        for part, extra, ref in ((0, k_extra, k_s), (1, v_extra, v_s), (2, q_extra, q_s)):
            for h in range(heads):
                n = part * heads + h
                here = y[:, n // 2 * LANES : (n // 2 + 1) * LANES]
                if n % 2:
                    here = pltpu.roll(here, HD, 1)
                elif here.shape[1] < LANES:
                    here = jnp.concatenate([here, jnp.zeros((tile, LANES - here.shape[1]), F32)], axis=1)
                ref[h, at, :] = jnp.where(head_lane, here, extra).astype(BF16)
        for k in range(2 * per):
            slots_of(i * 2 * per + k)
        return carry

    lax.fori_loop(0, rows // tile, project, 0)
    lane = lane_ids((BLK, LANES))
    null_key = jnp.where((lane >= HD) & (lane < HD + DOCS), 1.0, 0.0).astype(BF16)
    for h in range(heads):
        k_s[h, rows : rows + BLK, :] = null_key
        v_s[h, rows : rows + BLK, :] = jnp.zeros((BLK, LANES), BF16)
    out_copies += [put(k_s, k_out, sem, last + 1), put(v_s, v_out, sem, last + 2)]
    part_blocks = rows // BLK // group
    together = 4

    for r in range(group):

        def attend(i, carry, r=r):
            units = [(u, h) for u in range(together) for h in range(heads)]
            row = [r * part_blocks + i * together + u for u in range(together)]
            at = [pl.ds(pl.multiple_of(j * BLK, BLK), BLK) for j in row]
            place = [(row[u] * heads + h) * SLOTS for u, h in units]
            q = [q_s[h, at[u], :] for u, h in units]
            scores = [
                dot(q[n], picked(k_s, loc_ref, h, place[n]), ((1,), (1,))) for n, (u, h) in enumerate(units)
            ]
            top = [jnp.max(t, axis=1, keepdims=True) for t in scores]
            prob = [jnp.exp2((t - m) * RATE).astype(BF16) for t, m in zip(scores, top)]
            mixed = [
                dot(prob[n], picked(v_s, loc_ref, h, place[n]), ((1,), (0,))) for n, (u, h) in enumerate(units)
            ]
            total = [m[:, HD : HD + 1] for m in mixed]
            done = [(m / t)[:, :HD] for m, t in zip(mixed, total)]
            level = [-(m + jnp.log2(t) * (1.0 / RATE)) for m, t in zip(top, total)]
            for n, (u, h) in enumerate(units):
                q_s[h, at[u], :] = place_three(q[n].astype(F32), level[n], lane, HD + DOCS).astype(BF16)
            for u in range(together):
                here = pl.ds(pl.multiple_of((i * together + u) * BLK, BLK), BLK)
                ctx_refs[r][here, :] = jnp.concatenate(done[u * heads : (u + 1) * heads], axis=1).astype(BF16)
            return carry

        lax.fori_loop(0, part_blocks // together, attend, 0)
    out_copies.append(put(q_s, q_out, sem, last + 3))
    for copy in out_copies:
        copy.wait()


def backward_kernel(heads, group, count, fast, loc_ref, at_ref, qa_ref, ka_ref, va_ref, x_ref, *rest):
    w_pieces, rest = rest[:count], rest[count:]
    half = group // 2
    ctx_refs = [*rest[:half], *[rest[half].at[r] for r in range(half)]]
    grad_refs, rest = rest[half + 1 : half + 1 + group], rest[half + 1 + group :]
    keep_ref, send_ref, *rest = rest
    if fast:
        mine_ref, theirs_ref, *rest = rest
    else:
        out_ref, *rest = rest
    da_s, dq_s, x_s, w_s, keep_s, send_s, sem, *rest = rest
    dk_even, dk_odd, dv_even, dv_odd = (rest[i * heads : (i + 1) * heads] for i in range(4))
    if fast:
        out_ref = rest[4 * heads]
    rows, width = x_ref.shape
    w_rows = width // count
    w_copies = gathered(
        [piece.at[pl.ds(0, w_rows)] for piece in w_pieces],
        [pl.multiple_of((at_ref[0] ^ k) * w_rows, 16) for k in range(count)],
        w_s,
        sem,
        0,
    )
    if fast:
        x_copy = put(x_ref, x_s, sem, count)
    part_rows = rows // group
    tile = 128
    lane_tile = lane_ids((tile, LANES))
    blank = jnp.zeros((tile, LANES - HD), F32)

    def load(i, carry):
        at = pl.ds(pl.multiple_of(i * tile, tile), tile)
        for r in range(group):
            all_at = pl.ds(pl.multiple_of(r * part_rows + i * tile, tile), tile)
            grads = grad_refs[r][at, :].astype(F32)
            both = grads * ctx_refs[r][at, :].astype(F32)
            for h in range(heads):
                cols = slice(h * HD, (h + 1) * HD)
                delta = jnp.sum(both[:, cols], axis=1, keepdims=True)
                wide = jnp.concatenate([grads[:, cols], blank], axis=1)
                da_s[h, all_at, :] = place_three(wide, -delta, lane_tile, HD).astype(BF16)
        for b in range(rows // BLK // (part_rows // tile)):
            for ref in (*dk_even, *dk_odd, *dv_even, *dv_odd):
                ref[i * (rows // BLK // (part_rows // tile)) + b] = jnp.zeros((HD, LANES), F32)
        return carry

    lax.fori_loop(0, part_rows // tile, load, 0)
    for ref in (*dk_even, *dk_odd, *dv_even, *dv_odd):
        ref[rows // BLK] = jnp.zeros((HD, LANES), F32)
    together = 4

    def attend(i, carry):
        units = [(u, h) for u in range(together) for h in range(heads)]
        row = [i * together + u for u in range(together)]
        at = [pl.ds(pl.multiple_of(j * BLK, BLK), BLK) for j in row]
        place = [(row[u] * heads + h) * SLOTS for u, h in units]
        q = [qa_ref[h, at[u], :] for u, h in units]
        d_mixed = [da_s[h, at[u], :] for u, h in units]
        keys = [picked(ka_ref, loc_ref, h, place[n]) for n, (u, h) in enumerate(units)]
        values = [picked(va_ref, loc_ref, h, place[n]) for n, (u, h) in enumerate(units)]
        scores = [dot(a, b, ((1,), (1,))) for a, b in zip(q, keys)]
        d_prob = [dot(a, b, ((1,), (1,))) for a, b in zip(d_mixed, values)]
        prob = [jnp.exp2(t * RATE) for t in scores]
        d_scores = [(a * b).astype(BF16) for a, b in zip(prob, d_prob)]
        prob = [t.astype(BF16) for t in prob]
        d_q = [dot(a, b, ((1,), (0,))) for a, b in zip(d_scores, keys)]
        q_turned = [t.astype(F32).T[:HD].astype(BF16) for t in q]
        d_turned = [t.astype(F32).T[:HD].astype(BF16) for t in d_mixed]
        d_keys = [dot(a, b, ((1,), (0,))) for a, b in zip(q_turned, d_scores)]
        d_values = [dot(a, b, ((1,), (0,))) for a, b in zip(d_turned, prob)]
        for n, (u, h) in enumerate(units):
            dq_s[h, at[u], :] = (d_q[n] * SCALE).astype(BF16)
        for u in range(together):
            for s in range(SLOTS):
                for h in range(heads):
                    n = u * heads + h
                    to = loc_ref[place[n] + s]
                    cols = slice((s // 2) * LANES, (s // 2 + 1) * LANES)
                    dk_ref, dv_ref = (dk_odd[h], dv_odd[h]) if s % 2 else (dk_even[h], dv_even[h])
                    dk_ref[to] += d_keys[n][:, cols]
                    dv_ref[to] += d_values[n][:, cols]
        return carry

    lax.fori_loop(0, rows // BLK // together, attend, 0)
    low_lane = lane_ids((HD, LANES)) < BLK

    def finish(i, carry):
        at = [pl.ds(pl.multiple_of((2 * i + u) * BLK, BLK), BLK) for u in range(2)]
        turned = []
        for even, odd, factor in ((dk_even, dk_odd, SCALE), (dv_even, dv_odd, 1.0)):
            for h in range(heads):
                first = even[h][2 * i] + pltpu.roll(odd[h][2 * i], BLK, 1)
                second = pltpu.roll(even[h][2 * i + 1], BLK, 1) + odd[h][2 * i + 1]
                turned.append(jnp.where(low_lane, first, second) * factor)
        pair = pl.ds(pl.multiple_of(2 * i * BLK, 2 * BLK), 2 * BLK)
        for n in range(heads):
            both = jnp.concatenate([turned[2 * n], turned[2 * n + 1]], axis=0)
            out_ref[pair, n * LANES : (n + 1) * LANES] = both.T.astype(BF16)
        done = [dq_s[h, pair, :][:, :HD].astype(F32) for h in range(heads)]
        out_ref[pair, heads * LANES :] = jnp.concatenate(done, axis=1).astype(BF16)
        return carry

    lax.fori_loop(0, rows // BLK // 2, finish, 0)
    for copy in w_copies:
        copy.wait()
    out_copies = []
    for odd, hold, ref in ((1, send_s, send_ref), (0, keep_s, keep_ref)):

        def to_rows(i, carry, odd=odd, hold=hold):
            at = pl.ds(pl.multiple_of((2 * i + odd) * part_rows, BLK), part_rows)
            hold[i] = dot(out_ref[at, :], w_s[...], ((1,), (1,))).astype(hold.dtype)
            return carry

        lax.fori_loop(0, group // 2, to_rows, 0)
        out_copies.append(put(hold, ref, sem, count + 1 + odd))
    if fast:
        x_copy.wait()
        sums = jnp.zeros((1, out_ref.shape[1]), F32)
        for r in range(group):
            sums = sums + row_sum(out_ref[r * part_rows : (r + 1) * part_rows, :].astype(F32))
        shape = (64, sums.shape[1])
        tail = jnp.where(
            lax.broadcasted_iota(jnp.int32, shape, 0) == 0, jnp.broadcast_to(sums, shape), 0.0
        )
        for k, ref in ((1, theirs_ref), (0, mine_ref)):
            cols = pl.ds(pl.multiple_of((at_ref[0] ^ k) * w_rows, LANES), w_rows)
            half = dot(x_s[:, cols], out_ref[...], ((0,), (0,)))
            half = jnp.concatenate([half, tail], axis=0).astype(BF16)
            size = half.shape[0] // 4
            for z in range(4):
                ref[plane_spot(z, at_ref[3])] = half[z * size : (z + 1) * size]
    for copy in out_copies:
        copy.wait()


def cost(microseconds):
    return pl.CostEstimate(flops=int(microseconds * WEIGHT), bytes_accessed=0, transcendentals=0)


def whole(memory):
    return pl.BlockSpec(memory_space=memory)


def pieces_of(group, rows, columns):
    half = group // 2
    near = jax.ShapeDtypeStruct((rows, columns), BF16)
    return (near,) * half + (jax.ShapeDtypeStruct((half, rows, columns), BF16),)


def attention_forward(turns, x_pieces, w_pieces, bias, heads, group, seqs, positions):
    chunks, width = group * seqs, x_pieces[0].shape[2]
    rows = positions * chunks
    counts = (len(x_pieces), len(w_pieces))
    kept = jax.ShapeDtypeStruct((heads, rows + BLK, LANES), BF16)
    return pl.pallas_call(
        partial(forward_kernel, heads, group, seqs, counts),
        out_shape=(
            jax.ShapeDtypeStruct((chunks, positions, width), BF16),
            jax.ShapeDtypeStruct((heads, rows, LANES), BF16),
            kept,
            kept,
            jax.ShapeDtypeStruct((rows // BLK * heads * SLOTS,), jnp.int32),
        )
        + pieces_of(group, rows // group, heads * HD),
        in_specs=[whole(pltpu.SMEM), whole(pltpu.VMEM)] + [whole(pl.ANY)] * sum(counts),
        out_specs=(whole(pl.ANY),) * 4 + (whole(pltpu.SMEM),) + (whole(pltpu.VMEM),) * (group // 2 + 1),
        scratch_shapes=[
            pltpu.VMEM((chunks, positions + 16, width), BF16),
            pltpu.VMEM((heads, rows, LANES), BF16),
            pltpu.VMEM((heads, rows + BLK, LANES), BF16),
            pltpu.VMEM((heads, rows + BLK, LANES), BF16),
            pltpu.VMEM((width, 3 * heads * HD), BF16),
            pltpu.VMEM((LANES, LANES), F32),
            pltpu.VMEM((chunks, LANES), jnp.int32),
            pltpu.SMEM((chunks, LANES), jnp.int32),
            pltpu.SemaphoreType.DMA((sum(counts) + 5 + chunks,)),
        ],
        compiler_params=pltpu.CompilerParams(vmem_limit_bytes=56 * MIB),
        cost_estimate=cost(19),
        name="attention_forward",
    )(turns, bias, *x_pieces, *w_pieces)


def attention_backward(loc, turns, qa, ka, va, x, w_pieces, ctx_parts, grads, heads, fast):
    rows, width = x.shape
    blocks, group, count, slab = rows // BLK, len(grads), len(w_pieces), heads * HD
    part = (group // 2, rows // group, width)
    piece = jax.ShapeDtypeStruct((4, (width // 2 + 64) // 4, 3 * slab), BF16)
    d_qkv = jax.ShapeDtypeStruct((rows, 3 * slab), BF16)
    outs = (jax.ShapeDtypeStruct(part, F32), jax.ShapeDtypeStruct(part, BF16))
    outs += (piece, piece) if fast else (d_qkv,)
    return pl.pallas_call(
        partial(backward_kernel, heads, group, count, fast),
        out_shape=outs,
        in_specs=[whole(pltpu.SMEM)] * 2
        + [whole(pltpu.VMEM)] * 3
        + [whole(pl.ANY)] * (1 + count)
        + [whole(pltpu.VMEM)] * (group // 2 + 1 + group),
        out_specs=(whole(pl.ANY),) * 2 + (whole(pltpu.VMEM),) * (len(outs) - 2),
        scratch_shapes=[
            pltpu.VMEM((heads, rows, LANES), BF16),
            pltpu.VMEM((heads, rows, LANES), BF16),
            pltpu.VMEM((rows, width), BF16),
            pltpu.VMEM((width, 3 * slab), BF16),
            pltpu.VMEM(part, F32),
            pltpu.VMEM(part, BF16),
            pltpu.SemaphoreType.DMA((count + 3,)),
        ]
        + [pltpu.VMEM((blocks + 1, HD, LANES), F32)] * (4 * heads)
        + ([pltpu.VMEM((rows, 3 * slab), BF16)] if fast else []),
        compiler_params=pltpu.CompilerParams(vmem_limit_bytes=56 * MIB),
        cost_estimate=cost(50),
        name="attention_backward",
    )(loc, turns, qa, ka, va, x, *w_pieces, *ctx_parts, *grads)


def norm_values(values):
    average = jnp.mean(values, axis=-1, keepdims=True)
    centred = values - average
    inv_std = lax.rsqrt(jnp.mean(centred * centred, axis=-1, keepdims=True) + EPSILON)
    return centred * inv_std, inv_std


def norm_pull(upstream, scaled, inv_std, gain_row):
    weighted = upstream * gain_row
    centre_term = jnp.mean(weighted, axis=-1, keepdims=True)
    slope_term = jnp.mean(weighted * scaled, axis=-1, keepdims=True)
    return inv_std * (weighted - centre_term - scaled * slope_term)


def gelu_pair(v):
    rate = math.sqrt(2.0 / math.pi)
    square = v * v
    t = jnp.tanh(rate * v * (1.0 + 0.044715 * square))
    half = 0.5 * (1.0 + t)
    slope = half + (0.5 * rate) * v * (1.0 - t * t) * (1.0 + (3.0 * 0.044715) * square)
    return v * half, slope


def row_sum(values):
    return jnp.sum(values, axis=0, keepdims=True)


def layer_kernel(group, count, plan, seqs, fast, at_ref, x_ref, vec_ref, upb_ref, *rest):
    ctx_refs = rest[:group]
    arrays, rest = rest[group : group + count], rest[group + count :]
    cot_refs, result_refs, rest = rest[:seqs], rest[seqs : 2 * seqs], rest[2 * seqs :]
    if fast:
        dh1_ref, act_mine, pack_one, dsec_ref, dhid_mine, dbr_mine, pack_two, first_low_ref, small_ref = rest[:9]
        rest = rest[9:]
        slab = ctx_refs[0].shape[1]
    else:
        dh1_ref, active_ref, dhid_ref, first_low_ref, dsec_ref, dbr_ref, sums_out, upb_out = rest[:8]
        rest = rest[8:]
    near, far, rest = rest[: group // 2], rest[group // 2], rest[group // 2 + 1 :]
    dctx_refs = [*near, *[far.at[r] for r in range(group // 2)]]
    out_s, up_s, down_s, slope_s, scaled_s, inv_s, acc_s, cot_s, result_s, x_s, dbr_s, sums_s, upb_s, sem = rest
    rows, width = acc_s.shape
    hidden = up_s.shape[1]
    member = at_ref[0]
    core = member & 1
    copies = []
    for k, (array, column, w) in enumerate(plan):
        scratch, source = (out_s, up_s, down_s)[w], arrays[array]
        if column is not None:
            source = source.at[:, pl.ds(column, scratch.shape[-1])]
        start = pl.multiple_of(at_ref[1 + k], 1 if w == 0 else 16)
        one = w == 0 and len(source.shape) == 2
        copies.append(put(source, scratch.at[start] if one else scratch.at[pl.ds(start, source.shape[0])], sem, k))
    k = len(plan)
    part_rows = rows // seqs
    starts = [p * part_rows for p in range(seqs)]
    cot_copies = gathered(cot_refs, starts, cot_s, sem, k)
    x_copy = put(x_ref.at[pl.ds(0, rows)], x_s, sem, k + 2 * seqs)
    b_out, b_first, b_last, b_second = (vec_ref[i : i + 1, :] for i in (2, 3, 4, 5))
    gain_one, gain_two = vec_ref[6:7, :], vec_ref[7:8, :]
    tile = min(256, rows)
    sums_s[...] = jnp.zeros_like(sums_s)

    for copy in [x_copy] + [copy for copy, (_, _, w) in zip(copies, plan) if w == 0]:
        copy.wait()

    def first_norm(i, carry):
        at = pl.ds(pl.multiple_of(i * tile, tile), tile)
        total = x_s[at, :].astype(F32) + b_out
        for r in range(group):
            total = total + dot(ctx_refs[r][at, :], out_s[member ^ r], ((1,), (0,)))
        scaled, inv_std = norm_values(total)
        first = scaled * gain_one + b_first
        scaled_s[at, :] = scaled
        inv_s[at, :] = jnp.broadcast_to(inv_std, (tile, LANES))
        first_low_ref[at, :] = first.astype(BF16)
        acc_s[at, :] = first + b_second
        return carry

    lax.fori_loop(0, rows // tile, first_norm, 0)
    for copy in [copy for copy, (_, _, w) in zip(copies, plan) if w > 0]:
        copy.wait()

    def up_down(start, step, ref, to):
        at = pl.ds(pl.multiple_of(start, step), step)
        v = dot(first_low_ref[...], up_s[:, at], ((1,), (0,))) + upb_ref[:, at]
        active, slope = gelu_pair(v)
        active = active.astype(BF16)
        ref[:, pl.ds(pl.multiple_of(to, step), step)] = active
        slope_s[:, at] = slope
        acc_s[...] += dot(active, down_s[at, :], ((1,), (0,)))

    def down_up(start, step, ref, to):
        at = pl.ds(pl.multiple_of(start, step), step)
        d_hidden = dot(dsec_ref[...], down_s[at, :], ((1,), (1,))) * slope_s[:, at]
        low = d_hidden.astype(BF16)
        ref[:rows, pl.ds(pl.multiple_of(to, step), step)] = low
        upb_s[:, at] = row_sum(low.astype(F32))
        acc_s[...] += dot(low, up_s[:, at], ((1,), (1,)))

    def over_hidden(one, refs):
        if fast:
            step = hidden // 4
            for c, ref in enumerate(refs):

                def part(i, carry, c=c, ref=ref):
                    turn = c ^ core
                    one((i * 2 + turn if one is up_down else turn * 2 + i) * step, step, ref, i * step)
                    return carry

                for i in range(2):
                    part(i, 0)
        else:
            step = 512

            def part(i, carry):
                one(i * step, step, refs[0], i * step)
                return carry

            lax.fori_loop(0, hidden // step, part, 0)

    over_hidden(up_down, (act_mine, pack_one) if fast else (active_ref,))
    for copy in cot_copies:
        copy.wait()

    def last_norm(i, carry):
        at = pl.ds(pl.multiple_of(i * tile, tile), tile)
        scaled, inv_std = norm_values(acc_s[at, :])
        result_s[at, :] = (scaled * gain_two + b_last).astype(BF16)
        upstream = cot_s[at, :].astype(F32)
        pulled = norm_pull(upstream, scaled, inv_std, gain_two)
        acc_s[at, :] = pulled
        low = pulled.astype(BF16)
        dsec_ref[at, :] = low
        if fast:
            pack_one[at, hidden // 2 :] = low
        sums_s[1:2, :] += row_sum(upstream * scaled)
        sums_s[4:5, :] += row_sum(upstream)
        sums_s[5:6, :] += row_sum(pulled)
        return carry

    lax.fori_loop(0, rows // tile, last_norm, 0)
    result_copies = [
        put(result_s.at[pl.ds(starts[p], part_rows)], result_refs[p], sem, k + seqs + p) for p in range(seqs)
    ]
    over_hidden(down_up, (dhid_mine, pack_two) if fast else (dhid_ref,))

    def first_back(i, carry):
        at = pl.ds(pl.multiple_of(i * tile, tile), tile)
        upstream, scaled = acc_s[at, :], scaled_s[at, :]
        pulled = norm_pull(upstream, scaled, inv_s[at, :1], gain_one)
        dh1_ref[at, :] = pulled
        low = pulled.astype(BF16)
        dbr_s[at, :] = low
        sums_s[0:1, :] += row_sum(upstream * scaled)
        sums_s[2:3, :] += row_sum(pulled)
        sums_s[3:4, :] += row_sum(upstream)
        for r in range(group):
            dctx_refs[r][at, :] = dot(low, out_s[member ^ r], ((1,), (1,))).astype(BF16)
        return carry

    lax.fori_loop(0, rows // tile, first_back, 0)
    if fast:
        half, wide = width // 2, hidden // 2
        dbr_mine[...] = dbr_s[:, pl.ds(pl.multiple_of(core * half, LANES), half)]
        pack_two[:rows, wide : wide + half] = dbr_s[:, pl.ds(pl.multiple_of((1 - core) * half, LANES), half)]
        pack_two[:rows, wide + half : wide + half + width] = first_low_ref[...]
        pack_two[:rows, wide + half + width :] = jnp.concatenate([ref[...] for ref in ctx_refs], axis=1)
        long = [upb_s[:, i * width : (i + 1) * width] for i in range(hidden // width)]
        blank = jnp.zeros((8 - len(long), width), F32)
        small = jnp.concatenate([sums_s[...], *long, blank], axis=0).astype(BF16)
        small_ref[...] = small
        pack_two[rows:, :width] = small
        pack_two[rows:, width:] = jnp.zeros((16, pack_two.shape[1] - width), BF16)
    else:
        dbr_ref[...] = dbr_s[...]
        sums_out[...] = sums_s[...]
        upb_out[...] = upb_s[...]
    for copy in result_copies:
        copy.wait()


def layer(place, x_seq, cots, vectors, up_shift, ctx_parts, parts, plan, fast):
    rows, width = len(cots) * cots[0].shape[0], x_seq.shape[1]
    group, slab = len(ctx_parts), ctx_parts[0].shape[1]
    hidden = up_shift.shape[1]

    def like(columns, dtype=BF16, count=rows):
        return jax.ShapeDtypeStruct((count, columns), dtype)

    half, wide = width // 2, hidden // 2
    if fast:
        outs = (like(width, F32), like(wide), like(wide + width), like(width), like(wide), like(half))
        outs += (like(wide + half + 2 * width, BF16, rows + 16), like(width), like(width, BF16, 16))
    else:
        outs = (like(width, F32), like(hidden), like(hidden), like(width), like(width), like(width))
        outs += (like(width, F32, 8), like(hidden, F32, 1))
    outs = (jax.ShapeDtypeStruct(cots[0].shape, BF16),) * len(cots) + outs + pieces_of(group, rows, slab)
    return pl.pallas_call(
        partial(layer_kernel, group, len(parts), plan, len(cots), fast),
        out_shape=outs,
        in_specs=[whole(pltpu.SMEM), whole(pl.ANY)]
        + [whole(pltpu.VMEM)] * (2 + group)
        + [whole(pl.ANY)] * (len(parts) + len(cots)),
        out_specs=(whole(pl.ANY),) * len(cots) + (whole(pltpu.VMEM),) * (len(outs) - len(cots)),
        scratch_shapes=[
            pltpu.VMEM((group, slab, width), BF16),
            pltpu.VMEM((width, hidden), BF16),
            pltpu.VMEM((hidden, width), BF16),
            pltpu.VMEM((rows, hidden), F32),
            pltpu.VMEM((rows, width), F32),
            pltpu.VMEM((rows, LANES), F32),
            pltpu.VMEM((rows, width), F32),
            pltpu.VMEM((rows, width), BF16),
            pltpu.VMEM((rows, width), BF16),
            pltpu.VMEM((rows, width), BF16),
            pltpu.VMEM((rows, width), BF16),
            pltpu.VMEM((8, width), F32),
            pltpu.VMEM((1, hidden), F32),
            pltpu.SemaphoreType.DMA((len(plan) + 2 * len(cots) + 1,)),
        ],
        compiler_params=pltpu.CompilerParams(vmem_limit_bytes=56 * MIB),
        cost_estimate=cost(29),
        name="feed_forward",
    )(place, x_seq, vectors, up_shift, *ctx_parts, *parts, *cots)


def plane_spot(z, own):
    turn = z ^ own
    return (turn & 1) * 2 + (turn >> 1)


def down_grad_kernel(at_ref, act_in, d_in, got_in, keep_ref, send_ref, act_ref, d_ref, got_ref, keep_s, send_s, sem):
    piece = keep_s.shape[2]
    chunk = 4 * piece
    wide = act_ref.shape[1]
    ins = [put(*pair, sem, k) for k, pair in enumerate(((d_in, d_ref), (act_in, act_ref), (got_in, got_ref)))]
    for copy in ins:
        copy.wait()
    outs = []
    for f, hold, ref in ((1, send_s, send_ref), (0, keep_s, keep_ref)):
        for x in range(2):
            t = (f ^ at_ref[0]) * 2 + (x ^ at_ref[2])
            at = pl.ds(pl.multiple_of(t * chunk, LANES), chunk)
            grad = dot(act_ref[:, at], d_ref[...], ((0,), (0,)))
            grad = (grad + dot(got_ref[:, at], got_ref[:, wide:], ((0,), (0,)))).astype(BF16)
            for z in range(4):
                hold[x, plane_spot(z, at_ref[3])] = grad[z * piece : (z + 1) * piece]
            outs.append(put(hold.at[x], ref.at[x], sem, 3 + 2 * f + x))
    for copy in outs:
        copy.wait()


def up_grad_kernel(at_ref, first_in, dhid_in, dbr_in, small_ref, got_in, *rest):
    ctx_refs, (keep_ref, send_ref), rest = rest[:4], rest[4:6], rest[6:]
    first_s, ctx_s, extra_s, first_ref, dhid_ref, dbr_ref, got_ref, keep_s, send_s, sem = rest
    half, step = keep_s.shape[2:]
    rows, width = first_ref.shape
    slab = ctx_refs[0].shape[1]
    wide, narrow = dhid_ref.shape[1], dbr_ref.shape[1]
    ins = [put(first_in, first_ref, sem, 0)]
    cuts = (wide + narrow, wide + narrow + width, wide + narrow + 2 * width)
    for k, (a, b) in enumerate(((cuts[0], cuts[1]), (cuts[1], cuts[2]), (0, cuts[0]))):
        ins.append(put(got_in.at[:, pl.ds(a, b - a)], got_ref.at[:, pl.ds(a, b - a)], sem, 1 + k))
    ins += [put(dhid_in, dhid_ref, sem, 4), put(dbr_in, dbr_ref, sem, 5)]
    for copy in ins[:3]:
        copy.wait()
    first_s[:, :rows] = first_ref[...].astype(F32).T.astype(BF16)
    first_s[:, rows:] = got_ref[:rows, wide + narrow : wide + narrow + width].astype(F32).T.astype(BF16)
    got_ctx = got_ref[:rows, wide + narrow + width :].astype(F32).T.astype(BF16)
    for r in range(4):
        ctx_s[at_ref[4] ^ r, :, :rows] = ctx_refs[r][...].astype(F32).T.astype(BF16)
        ctx_s[at_ref[4] ^ r ^ 1, :, rows:] = got_ctx[r * slab : (r + 1) * slab]
    ups = wide // step
    for copy in ins[3:]:
        copy.wait()
    extra_s[...] = jnp.zeros_like(extra_s)
    vectors = small_ref[...].astype(F32) + got_ref[rows:, :width].astype(F32)
    for f in range(2):
        for i in range(6):
            for k in range(half // LANES):
                start = f * half + k * LANES
                extra_s[f, i * (half // LANES) + k : i * (half // LANES) + k + 1, :] = vectors[
                    i : i + 1, start : start + LANES
                ]
        row = 6 * (half // LANES)
        for k in range(wide // LANES):
            start = f * wide + k * LANES
            extra_s[f, row + k : row + k + 1, :] = vectors[
                8 + start // width : 9 + start // width, start % width : start % width + LANES
            ]
    outs = []
    for x, ref, out in ((1, send_s, send_ref), (0, keep_s, keep_ref)):

        def one(i, carry, x=x, ref=ref):
            spot = (i & 1) * 2 + (i >> 1)
            k = (x ^ at_ref[2]) * 4 + (i ^ at_ref[3])

            def store(grad):
                for f in range(2):
                    ref[f ^ at_ref[0], spot] = grad[f * half : (f + 1) * half].astype(BF16)

            def out_grad(lanes):
                turned = ctx_s[...].reshape(width, 2 * rows)
                right = jnp.concatenate([dbr_ref[:, lanes], got_ref[:rows, wide + lanes.start : wide + lanes.stop]], axis=0)
                return dot(turned, right, ((1,), (0,)))

            @pl.when(k < ups)
            def _():
                at = pl.ds(pl.multiple_of(k * step, step), step)
                right = jnp.concatenate([dhid_ref[:, at], got_ref[:rows, at]], axis=0)
                store(dot(first_s[...], right, ((1,), (0,))))

            @pl.when(k == ups)
            def _():
                store(out_grad(slice(0, step)))

            @pl.when(k > ups)
            def _():
                extra = extra_s[...].reshape(width, LANES)
                store(jnp.concatenate([out_grad(slice(step, narrow)), extra], axis=1))

            return carry

        lax.fori_loop(0, 4, one, 0)
        outs.append(put(ref, out, sem, 6 + x))
    for copy in outs:
        copy.wait()


def down_final_kernel(at_ref, *rest):
    parts, (out_ref, in_s, out_s, sem) = rest[:4], rest[4:]
    piece = parts[0].shape[1]
    copies_in = [put(part, in_s.at[i], sem, i) for i, part in enumerate(parts)]
    copies = []
    for i in range(4):
        copies_in[i].wait()
        for z in range(4):
            k = (((i & 1) ^ at_ref[1]) * 2 + ((i >> 1) ^ at_ref[2])) * 4 + (z ^ at_ref[3])
            at = pl.ds(pl.multiple_of(k * piece, 16), piece)
            out_s[at, :] = in_s[i, (z & 1) * 2 + (z >> 1)].astype(F32)
            copies.append(put(out_s.at[at], out_ref.at[at], sem, 4 + i * 4 + z))
    for copy in copies:
        copy.wait()


def up_final_kernel(at_ref, *rest):
    parts, (up_ref, out_ref, gains_ref, biases_ref, upb_ref, in_s, out_s, sem) = rest[:4], rest[4:]
    step = parts[0].shape[2]
    wide, narrow = up_ref.shape[1] // 2, out_ref.shape[1] // 2
    ups = wide // step
    half = gains_ref.shape[1]
    count = half // LANES
    copies_in = [put(part, in_s.at[i], sem, i) for i, part in enumerate(parts)]

    def each(i, z, act):
        core = (i & 1) ^ at_ref[1]
        k = ((i >> 1) ^ at_ref[2]) * 4 + (z ^ at_ref[3])
        n = i * 4 + z

        @pl.when(k < ups)
        def _():
            at = pl.ds(pl.multiple_of(core * wide + k * step, LANES), step)
            act(pltpu.make_async_copy(out_s.at[n], up_ref.at[:, at], sem.at[4 + n]))

        @pl.when(k == ups)
        def _():
            at = pl.ds(pl.multiple_of(core * narrow, LANES), step)
            act(pltpu.make_async_copy(out_s.at[n], out_ref.at[:, at], sem.at[4 + n]))

        @pl.when(k > ups)
        def _():
            at = pl.ds(pl.multiple_of(core * narrow + step, LANES), LANES)
            act(pltpu.make_async_copy(out_s.at[n, :, pl.ds(0, LANES)], out_ref.at[:, at], sem.at[4 + n]))

        return core, k

    for i in range(4):
        copies_in[i].wait()
        for z in range(4):
            value = in_s[i, (z & 1) * 2 + (z >> 1)].astype(F32)
            out_s[i * 4 + z] = value
            core, k = each(i, z, lambda copy: copy.start())

            @pl.when((k > ups) & (core == 0))
            def _(value=value):
                extra = value[:, LANES:]
                for a in range(6):
                    for b in range(count):
                        row = extra[a * count + b : a * count + b + 1]
                        lanes = slice(b * LANES, (b + 1) * LANES)
                        if a < 2:
                            gains_ref[a : a + 1, lanes] = row
                        else:
                            biases_ref[a - 2 : a - 1, lanes] = row
                for b in range(upb_ref.shape[1] // LANES):
                    upb_ref[:, b * LANES : (b + 1) * LANES] = extra[6 * count + b : 6 * count + b + 1]

    for i in range(4):
        for z in range(4):
            each(i, z, lambda copy: copy.wait())


def qkv_final_kernel(at_ref, late_ref, *rest):
    parts, (out_ref, biases_ref, hold, in_s, out_s, sums_s, sem) = rest[:4], rest[4:]
    half, slab = out_s.shape[0], hold.shape[2] // 3
    width = 4 * slab
    size = parts[0].shape[1]
    copies = [put(part, in_s.at[i], sem, i) for i, part in enumerate(parts)]
    for r in range(4):
        copies[r].wait()
        for z in range(4):
            at = pl.ds(pl.multiple_of((z ^ at_ref[3]) * size, 16), size)
            hold[at_ref[4] ^ r, at, :] = in_s[r, (z & 1) * 2 + (z >> 1)]
    outs = []
    for k, column in ((0, 1), (1, 2), (2, 0)):
        for m in range(4):
            cols = slice(column * width + m * slab, column * width + (m + 1) * slab)
            out_s[:, cols] = hold[m, :half, k * slab : (k + 1) * slab].astype(F32)
        at = pl.ds(column * width, width)
        outs.append(put(out_s.at[:, at], out_ref.at[:, at], sem, 4 + k))
    for k, row in ((2, 0), (1, 1)):
        sums = [hold[m, half : half + 16, k * slab : (k + 1) * slab].astype(F32)[:1] for m in range(4)]
        sums_s[row : row + 1, :] = jnp.concatenate(sums, axis=1)
    biases_ref[0:2, :] = sums_s[0:2, pl.ds(pl.multiple_of(at_ref[0] * half, LANES), half)]
    biases_ref[2:6, :] = late_ref[...]
    for copy in outs:
        copy.wait()


def local_call(kernel, outs, ins, scratch, name, time=3, loose=(), limit=28):
    return pl.pallas_call(
        kernel,
        out_shape=outs,
        in_specs=[whole(pltpu.SMEM)]
        + [whole(pl.ANY if i in loose else pltpu.VMEM) for i in range(1, len(ins))],
        out_specs=tuple(whole(pl.ANY if len(ins) + i in loose else pltpu.VMEM) for i in range(len(outs))),
        scratch_shapes=scratch,
        compiler_params=pltpu.CompilerParams(vmem_limit_bytes=limit * MIB),
        cost_estimate=cost(time),
        name=name,
    )(*ins)


def swap_joint(value, f_mask, c_mask):
    n_f, n_c = lax.axis_size("fsdp"), lax.axis_size("ctx")
    pairs = [(f * n_c + c, (f ^ f_mask) * n_c + (c ^ c_mask)) for f in range(n_f) for c in range(n_c)]
    return lax.ppermute(value, ("fsdp", "ctx"), pairs)


def sum_planes(own, others):
    total = own.astype(F32)
    for other in others:
        total = total + other.astype(F32)
    return total.astype(BF16)


def reduce_square(keep, got, after, axis, mask):
    first, second = sum_planes(gate(keep[0], after), [got[0]]), sum_planes(keep[1], [got[1]])
    return first, swap(second, axis, mask)


def reduce_planes(mine, late=(), last=()):
    two = sum_planes(mine[:2], [swap(mine[2:], "ctx", 4)])
    piece = gate(sum_planes(two[0], [swap(two[1], "ctx", 8)]), *late)
    four = jnp.stack([piece] + [swap(piece, "ctx", mask) for mask in (8, 4, 12)])
    across = swap(four, "ctx", 2)
    return four, [four, swap(four, "ctx", 1), across, swap(gate(across, *last), "ctx", 1)]


def exchange(near, far, between=None):
    half = len(near)
    got = swap(far, "ctx", half)
    if between is not None:
        got = gate(got, between)
    items = {(d, 0): near[d] for d in range(half)}
    items.update({(d, half): got[d] for d in range(half)})
    for bit in reversed(bits_of(half)):
        for d, source in [key for key in items if key[0] & bit]:
            items[d ^ bit, source ^ bit] = swap(items.pop((d, source)), "ctx", bit)
    return [items[0, source] for source in range(2 * half)]


def gather_fsdp(value):
    index = lax.axis_index("fsdp")
    parts = [value]
    for bit in bits_of(lax.axis_size("fsdp")):
        parts += [swap(part, "fsdp", bit) for part in parts]
    return to_absolute(parts, index)


def fetch_halves(value):
    half = value.shape[0] // 2
    parts = [lax.dynamic_slice_in_dim(value, (lax.axis_index("ctx") & 1) * half, half, 0)]
    for bit in bits_of(lax.axis_size("fsdp")):
        parts += [swap(part, "fsdp", bit) for part in parts]
    return parts[1:]


def weight_parts(value, halves):
    index = lax.axis_index("fsdp")
    core = lax.axis_index("ctx") & 1
    size = value.shape[0]
    half = size // 2
    pieces, places = [value], [index * size]
    for k, part in enumerate(halves, 1):
        pieces += [part, swap(part, "ctx", 1)]
        first = (index ^ k) * size
        places += [first + core * half, first + (1 - core) * half]
    return pieces, places


def halve(value, axis, dim, mask, index):
    half = value.shape[dim] // 2
    bit = (index // mask) & 1
    mine = lax.dynamic_slice_in_dim(value, bit * half, half, dim)
    theirs = lax.dynamic_slice_in_dim(value, (1 - bit) * half, half, dim)
    return mine + swap(theirs.astype(BF16), axis, mask).astype(F32)


def double(value, axis, dim, mask, index):
    bit = (index // mask) & 1
    other = swap(value, axis, mask)
    return lax.select_n(
        bit,
        jnp.concatenate([value, other], axis=dim),
        jnp.concatenate([other, value], axis=dim),
    )


def reduce_over_all(value):
    f_index, c_index = lax.axis_index("fsdp"), lax.axis_index("ctx")
    value = halve(value, "ctx", 1, 1, c_index)
    for bit in reversed(bits_of(lax.axis_size("fsdp"))):
        value = halve(value, "fsdp", 0, bit, f_index)
    value = value[0]
    rest = bits_of(lax.axis_size("ctx"))[1:]
    for bit in rest:
        value = halve(value, "ctx", 0, bit, c_index)
    value = value.astype(BF16)
    for bit in reversed(rest):
        value = double(value, "ctx", 0, bit, c_index)
    return double(value, "ctx", 0, 1, c_index).astype(F32)


def local(
    tokens, segments, rand_blocks, w_qkv, w_out, w_up, w_down, ln_gains, biases, up_bias, cotangent
):
    positions, seq_count, width = tokens.shape
    n_f, n_c = lax.axis_size("fsdp"), lax.axis_size("ctx")
    f_index, c_index = lax.axis_index("fsdp"), lax.axis_index("ctx")
    group = n_c // seq_count
    plane, member = c_index // group, c_index % group
    head_count = width // HD
    heads = -(-head_count // group)
    per_chunk = positions // BLK
    blocks = per_chunk * n_c
    rows_here = seq_count * positions
    f_width = width // n_f
    slab = heads * HD
    spare = group * slab - width

    def to_planes(parts):
        return [swap(part, "ctx", p * group) if p else part for p, part in enumerate(parts)]

    def from_planes(parts):
        return jnp.stack(to_absolute(parts, plane), axis=1)

    fast = n_f == 2 and group == 4 and seq_count == 4 and not spare and f_width % slab == 0
    turns = jnp.stack([f_index, member & 1, (member >> 1) & 1, plane, member, c_index])
    rand = jnp.pad(rand_blocks, ((0, 0), (0, 0), (0, group * heads - head_count), (0, 0)))
    rand = rand.reshape(seq_count, per_chunk, group, heads, -1).transpose(0, 2, 1, 3, 4)
    rand = rand.reshape(seq_count, group, -1)
    rand = jnp.pad(rand, ((0, 0), (0, 0), (0, LANES // group - rand.shape[2])))
    line = jnp.concatenate([segments.T, rand.reshape(seq_count, LANES)], axis=1).astype(BF16)
    line = jnp.pad(line, ((0, 0), (0, width - line.shape[1])))
    token_parts = split_planes(turns, tokens, line)
    w_qkv, small_in = lax.optimization_barrier(((w_qkv, (ln_gains, biases, up_bias)), *token_parts))[0]
    ln_gains, biases, up_bias = small_in
    x_rows = to_planes(token_parts)
    if fast:
        across = [swap(part, "ctx", 2) for part in x_rows]
        x_pieces = [*x_rows, swap(jnp.concatenate(x_rows), "ctx", 1), *across]
        x_pieces += [swap(part, "ctx", 1) for part in across]
    else:
        x_all = {(0, p): x_rows[p] for p in range(seq_count)}
        for bit in reversed(bits_of(group)):
            for r, p in list(x_all):
                x_all[r ^ bit, p] = swap(x_all[r, p], "ctx", bit)
        x_pieces = [x_all[r, p] for r in range(group) for p in range(seq_count)]

    w_parts = jnp.pad(w_qkv.reshape(-1, 3, width), ((0, 0), (0, 0), (0, spare))) if spare else None
    if spare:
        w_mine = [lax.dynamic_slice_in_dim(w_parts[:, k], member * slab, slab, 1) for k in (1, 2, 0)]
    else:
        w_mine = [lax.dynamic_slice_in_dim(w_qkv, k * width + member * slab, slab, 1) for k in (1, 2, 0)]
    small = jnp.concatenate([ln_gains.reshape(-1), biases.reshape(-1), up_bias])
    small_rows = -(-small.shape[0] // (3 * slab) // 16) * 16
    small_count = small.shape[0]
    small = jnp.pad(small, (0, small_rows * 3 * slab - small_count)).reshape(small_rows, 3 * slab)
    w_mine = jnp.concatenate([jnp.concatenate(w_mine, axis=1), small], axis=0)
    w_pieces = [w_mine]
    for bit in bits_of(n_f):
        w_pieces += [swap(part, "fsdp", bit) for part in w_pieces]
    small = [part[f_width:].reshape(-1)[:small_count] for part in w_pieces]
    small = jnp.stack(to_absolute(small, f_index)).astype(F32)
    gains_all = small[:, : 2 * f_width].reshape(n_f, 2, f_width).transpose(1, 0, 2).reshape(2, width)
    biases_all = (
        small[:, 2 * f_width : 8 * f_width].reshape(n_f, 6, f_width).transpose(1, 0, 2).reshape(6, width)
    )
    up_shift = small[:, 8 * f_width :].reshape(-1)
    bias_mine = lax.dynamic_slice_in_dim(
        jnp.pad(biases_all[:2], ((0, 0), (0, spare))), member * slab, slab, 1
    ).reshape(2, heads, HD)
    bias_wide = jnp.concatenate(
        [jnp.zeros_like(bias_mine[0]), bias_mine[1], bias_mine[0]], axis=0
    ).reshape(1, -1)

    cot_in = gate(cotangent, x_rows)
    cots = to_planes([lax.dynamic_index_in_dim(cot_in, plane ^ p, 1, keepdims=False) for p in range(seq_count)])
    if fast:
        core, chip = member & 1, member >> 1
        quarter, half = f_width // 4, f_width // 2
        up_quarter = lax.dynamic_slice_in_dim(w_up, (core * 2 + chip) * quarter, quarter, 0)
        up_quarter = gate(up_quarter, w_mine, across[0])
        tall = w_down.shape[0] // 2
        joint = lax.dynamic_slice_in_dim(w_down, core * tall, tall, 0).reshape(-1, half, width)
        joint = [lax.dynamic_slice_in_dim(w_out, core * half, half, 0), *joint]
        joint = swap(gate(jnp.concatenate(joint, axis=1), up_quarter), "fsdp", 1)
        up_quarter = swap(up_quarter, "fsdp", 1)
        up_across = swap(up_quarter, "ctx", 2)
    else:
        up_halves = fetch_halves(w_up)
        down_halves = fetch_halves(w_down)
    x_pieces = [piece.reshape(-1, positions + 16, width) for piece in x_pieces]
    x_seq, qa, ka, va, loc, *ctx_parts = attention_forward(
        turns, x_pieces, w_pieces, bias_wide, heads, group, seq_count, positions
    )
    x_seq = x_seq.reshape(blocks * BLK, width)
    if fast:
        ctx_parts, up_across, cots = lax.optimization_barrier((ctx_parts, up_across, cots))
        up_other = [swap(part, "ctx", 1) for part in (up_quarter, up_across)]
    ctx_mine = ctx_parts
    if fast:
        near, far = ctx_parts[:-1], ctx_parts[-1]
        ctx_parts = [near[0], swap(near[1], "ctx", 1), swap(far[0], "ctx", 2), swap(far[1], "ctx", 3)]
    else:
        ctx_parts = exchange(ctx_parts[:-1], ctx_parts[-1])
    if fast:
        joint_other = swap(gate(joint, ctx_parts[1]), "ctx", 1)
        parts = [w_out.reshape(2, slab, width), w_up, w_down, up_quarter, up_across, *up_other, joint, joint_other]
        plan = [(0, None, 0), (1, None, 1), (2, None, 2)] + [(3 + k, None, 1) for k in range(4)]
        theirs = 1 - f_index
        places = [2 * f_index, f_index * f_width, f_index * 2 * tall]
        for k in range(4):
            part = (core ^ (k >> 1)) * 2 + (chip ^ (k & 1))
            places.append(theirs * f_width + part * quarter)
        for k in range(2):
            plan += [(7 + k, n * width, 0 if n == 0 else 2) for n in range(1 + tall // half)]
            places.append(2 * theirs + (core ^ k))
            places += [theirs * 2 * tall + (core ^ k) * tall + n * half for n in range(tall // half)]
    else:
        out_full = jnp.concatenate(gather_fsdp(w_out), axis=0)
        out_full = jnp.pad(out_full, ((0, spare), (0, 0))).reshape(group, slab, width)
        up_parts, up_places = weight_parts(w_up, up_halves)
        down_parts, down_places = weight_parts(w_down, down_halves)
        parts, places = [out_full, *up_parts, *down_parts], [0, *up_places, *down_places]
        plan = [(0, None, 0)] + [(1 + k, None, 1) for k in range(len(up_parts))]
        plan += [(1 + len(up_parts) + k, None, 2) for k in range(len(down_parts))]
    vectors = jnp.concatenate([biases_all, gains_all])
    place = jnp.stack([member] + [jnp.int32(p) for p in places])
    done = layer(
        place,
        x_seq,
        cots,
        vectors,
        up_shift.reshape(1, -1),
        ctx_parts,
        parts,
        plan,
        fast,
    )
    pieces = group // 2 + 1
    results, d_parts, done = done[:seq_count], done[-pieces:], done[seq_count:-pieces]
    results = to_planes(results)
    back = partial(attention_backward, loc, turns, qa, ka, va, x_seq, w_pieces)
    hidden_width = w_up.shape[1]
    used = 6 * f_width + hidden_width // n_f

    if fast:
        dh1, act_mine, pack_one, d_second, dhid_mine, dbr_mine, pack_two, first_low, small_sums = done
        piece = hidden_width // n_f // 16
        pack_one = swap(pack_one, "ctx", 1)
        pack_two = swap(pack_two, "ctx", 1)
        step = (hidden_width + width + 256) // 16
        shape = jax.ShapeDtypeStruct((2, 4, f_width, step), BF16)
        up_keep, up_send = local_call(
            up_grad_kernel,
            (shape,) * 2,
            (
                turns,
                first_low,
                dhid_mine,
                dbr_mine,
                small_sums,
                pack_two,
                *ctx_parts,
            ),
            [
                pltpu.VMEM((width, 2 * rows_here), BF16),
                pltpu.VMEM((group, slab, 2 * rows_here), BF16),
                pltpu.VMEM((2, f_width, LANES), F32),
                pltpu.VMEM(first_low.shape, BF16),
                pltpu.VMEM(dhid_mine.shape, BF16),
                pltpu.VMEM(dbr_mine.shape, BF16),
                pltpu.VMEM(pack_two.shape, BF16),
                pltpu.VMEM(shape.shape, BF16),
                pltpu.VMEM(shape.shape, BF16),
                pltpu.SemaphoreType.DMA((8,)),
            ],
            "up_grad",
            loose=(1, 2, 3, 5, 10, 11),
            limit=56,
        )
        shape = jax.ShapeDtypeStruct((2, 4, piece, width), BF16)
        down_keep, down_send = local_call(
            down_grad_kernel,
            (shape,) * 2,
            (turns, gate(act_mine, up_send), d_second, pack_one),
            [
                pltpu.VMEM(act_mine.shape, BF16),
                pltpu.VMEM(d_second.shape, BF16),
                pltpu.VMEM(pack_one.shape, BF16),
                pltpu.VMEM(shape.shape, BF16),
                pltpu.VMEM(shape.shape, BF16),
                pltpu.SemaphoreType.DMA((7,)),
            ],
            "down_grad",
            loose=range(1, 6),
        )
        d_parts = exchange(d_parts[:-1], d_parts[-1], between=up_send)
        d_parts = gate(d_parts, down_send, up_send)
        down_got, up_got = swap(down_send, "fsdp", 1), swap(up_send, "ctx", 2)
        keep, send, mine, theirs = back(ctx_mine, d_parts, heads, fast)
        down_first, down_got = reduce_square(down_keep, down_got, send, "ctx", 2)
        up_first, up_got = reduce_square(up_keep, up_got, send, "fsdp", 1)
        output = from_planes([gate(results[0], send)] + results[1:])
        keep, send, mine, theirs, down_first, up_first, output = lax.optimization_barrier(
            (keep, send, mine, theirs, down_first, up_first, output)
        )
        cores = swap(send, "ctx", 1)
    else:
        dh1, active, d_hidden, first_low, d_second, d_branch, sums, upb_grad = done
        d_parts = exchange(d_parts[:-1], d_parts[-1])
        keep, send, d_qkv = back(ctx_mine, d_parts, heads, fast)
        output = from_planes(results)
        context_low = jnp.concatenate(to_absolute(ctx_parts, member), axis=1)[:, :width]
        grad_down = dot(active, d_second, ((0,), (0,)))
        grad_up = dot(first_low, d_hidden, ((0,), (0,)))
        grad_out = dot(context_low, d_branch, ((0,), (0,)))
        down_total = reduce_over_all(grad_down.reshape(n_f, -1, width))
        vectors = sums[:6].reshape(6, n_f, f_width).transpose(1, 0, 2).reshape(n_f, -1)
        vectors = jnp.concatenate([vectors, upb_grad.reshape(n_f, -1)], axis=1)
        extra = -(-used // f_width // LANES) * LANES
        vectors = jnp.pad(vectors, ((0, 0), (0, f_width * extra - used))).reshape(n_f, f_width, extra)
        up_out = jnp.concatenate(
            [grad_up.reshape(n_f, f_width, -1), grad_out.reshape(n_f, f_width, -1), vectors], axis=2
        )
        up_out = reduce_over_all(up_out)
        up_total = up_out[:, :hidden_width]
        out_total = up_out[:, hidden_width : hidden_width + width]
        vectors = up_out[:, hidden_width + width :].reshape(-1)
        gains_total = vectors[: 2 * f_width].reshape(2, f_width)
        biases_late = vectors[2 * f_width : 6 * f_width].reshape(4, f_width)
        up_bias_total = vectors[6 * f_width : used]

    if not fast:
        cores = swap(send, "ctx", 1)
    shape = (seq_count, positions, width)
    pieces = {2 * i: list((keep[i] + cores[i].astype(F32)).reshape(shape)) for i in range(group // 2)}
    far, close = [], []
    for bit in bits_of(group)[1:]:
        for r in [r for r in pieces if r & bit]:
            part = pieces.pop(r)
            cut = seq_count // 2
            far = jnp.stack([part[p].astype(BF16) for p in range(cut, seq_count)])
            close = jnp.stack([part[p].astype(BF16) for p in range(cut)])
            if fast:
                down_first = gate(down_first, far)
            far, close = swap(far, "ctx", bit), swap(close, "ctx", bit)
            got = [*close, *far]
            pieces[r ^ bit] = [pieces[r ^ bit][p] + got[p].astype(F32) for p in range(seq_count)]
    dh1 = dh1.reshape(shape)
    input_grad = from_planes(
        to_planes([(dh1[p] + pieces[0][p]).astype(BF16) for p in range(seq_count)])
    )

    if fast:
        got = swap(theirs, "fsdp", 1)
        down_four, down_parts = reduce_planes(sum_planes(down_first, [down_got]))
        up_four, up_parts = reduce_planes(sum_planes(gate(up_first, far), [up_got]), late=(down_four,))
        four = range(1, 5)
        down_total = local_call(
            down_final_kernel,
            (jax.ShapeDtypeStruct((hidden_width // n_f, width), F32),),
            (turns, *down_parts),
            [
                pltpu.VMEM((4, 4, piece, width), BF16),
                pltpu.VMEM((hidden_width // n_f, width), F32),
                pltpu.SemaphoreType.DMA((20,)),
            ],
            "down_final",
            loose=(*four, 5),
        )[0]
        up_total, out_total, gains_total, biases_late, up_bias_total = local_call(
            up_final_kernel,
            (
                jax.ShapeDtypeStruct((f_width, hidden_width), F32),
                jax.ShapeDtypeStruct((f_width, width), F32),
                jax.ShapeDtypeStruct((2, f_width), F32),
                jax.ShapeDtypeStruct((4, f_width), F32),
                jax.ShapeDtypeStruct((1, hidden_width // n_f), F32),
            ),
            (turns, *up_parts),
            [
                pltpu.VMEM((4, 4, f_width, step), BF16),
                pltpu.VMEM((16, f_width, step), F32),
                pltpu.SemaphoreType.DMA((20,)),
            ],
            "up_final",
            loose=(*four, 5, 6),
        )
        qkv_parts = reduce_planes(
            sum_planes(gate(mine, close), [got]), last=(up_total, down_total)
        )[1]
        qkv_total, biases_total = local_call(
            qkv_final_kernel,
            (jax.ShapeDtypeStruct((f_width, 3 * width), F32), jax.ShapeDtypeStruct((6, f_width), F32)),
            (turns, biases_late, *qkv_parts),
            [
                pltpu.VMEM((4, f_width + 64, 3 * slab), BF16),
                pltpu.VMEM((4, 4, (f_width + 64) // 4, 3 * slab), BF16),
                pltpu.VMEM((f_width, 3 * width), F32),
                pltpu.VMEM((8, width), F32),
                pltpu.SemaphoreType.DMA((7,)),
            ],
            "qkv_final",
            loose=(2, 3, 4, 5, 6),
        )
        up_bias_total = up_bias_total.reshape(-1)
    else:
        grad_qkv = dot(x_seq, d_qkv, ((0,), (0,))).reshape(n_f, f_width, 3 * slab)
        sums = jnp.sum(d_qkv.astype(F32), axis=0, keepdims=True)
        sums = jnp.pad(sums, ((0, 15), (0, 0)))
        value = jnp.concatenate([grad_qkv, jnp.broadcast_to(sums[None], (n_f,) + sums.shape)], axis=1)
        for bit in reversed(bits_of(n_f)):
            value = halve(value, "fsdp", 0, bit, f_index)
        value = value[0]
        plane_bits = [bit * group for bit in bits_of(seq_count)]
        for bit in plane_bits:
            value = halve(value, "ctx", 0, bit, c_index)
        value = value.astype(BF16)
        for bit in reversed(plane_bits):
            value = double(value, "ctx", 0, bit, c_index)
        parts = [value]
        for bit in bits_of(group):
            parts += [swap(part, "ctx", bit) for part in parts]
        parts = to_absolute(parts, member)
        qkv_total = jnp.stack([part.reshape(-1, 3, slab) for part in parts], axis=2).reshape(-1, 3, group * slab)
        qkv_total = jnp.concatenate([qkv_total[:, 2:], qkv_total[:, :2]], axis=1)[:, :, :width].astype(F32)
        early = lax.dynamic_slice_in_dim(qkv_total[f_width][0::2], f_index * f_width, f_width, 1)
        qkv_total = qkv_total[:f_width].reshape(f_width, 3 * width)
        biases_total = jnp.concatenate([early, biases_late])
    return (
        output,
        input_grad,
        qkv_total,
        out_total,
        up_total,
        down_total,
        gains_total,
        biases_total,
        up_bias_total,
    )


def solution(mesh):
    placed = (
        P("ctx", "fsdp", None),
        P("ctx", "fsdp"),
        P("fsdp", "ctx", None, None),
        P("fsdp", None),
        P("fsdp", None),
        P("fsdp", None),
        P("fsdp", None),
        P(None, "fsdp"),
        P(None, "fsdp"),
        P("fsdp"),
        P("ctx", "fsdp", None),
    )
    return jax.shard_map(
        local,
        mesh=mesh,
        in_specs=placed,
        out_specs=(
            P("ctx", "fsdp", None),
            P("ctx", "fsdp", None),
            P("fsdp", None),
            P("fsdp", None),
            P("fsdp", None),
            P("fsdp", None),
            P(None, "fsdp"),
            P(None, "fsdp"),
            P("fsdp"),
        ),
        check_vma=False,
    )
```

```python
import math
from functools import partial

import jax
import jax.numpy as jnp
from jax import lax
from jax.experimental import pallas as pl
from jax.experimental.pallas import tpu as pltpu
from jax.sharding import PartitionSpec as P

HD = 64
BLK = 64
LANES = 128
SLOTS = 8
DOCS = 32
EPSILON = 1e-06
NEGATIVE = -1e30
SCALE = HD**-0.5
RATE = SCALE / math.log(2.0)
MIB = 1024 * 1024
WEIGHT = 0

BF16 = jnp.bfloat16
F32 = jnp.float32


def dot(left, right, dims):
    return lax.dot_general(left, right, ((dims[0], dims[1]), ((), ())), preferred_element_type=F32)


def swap(value, axis, mask):
    count = lax.axis_size(axis)
    return lax.ppermute(value, axis, [(i, i ^ mask) for i in range(count)])


def gate(value, *after):
    return lax.optimization_barrier((value, *after))[0]


def bits_of(count):
    return [1 << k for k in range((count - 1).bit_length())]


def choose(index, cases):
    return cases[0] if len(cases) == 1 else lax.select_n(index, *cases)


def to_absolute(relative, index):
    count = len(relative)
    return [choose(index, [relative[k ^ i] for i in range(count)]) for k in range(count)]


def split_three(values):
    high = values.astype(BF16)
    rest = values - high.astype(F32)
    middle = rest.astype(BF16)
    return high, middle, (rest - middle.astype(F32)).astype(BF16)


def lane_ids(shape):
    return lax.broadcasted_iota(jnp.int32, shape, len(shape) - 1)


def place_three(base, values, lane, first):
    high, middle, small = split_three(values)
    base = jnp.where(lane == first, high.astype(F32), base)
    base = jnp.where(lane == first + 1, middle.astype(F32), base)
    return jnp.where(lane == first + 2, small.astype(F32), base)


def picked(ref, loc_ref, head, place):
    parts = [
        ref[head, pl.ds(pl.multiple_of(loc_ref[place + s] * BLK, BLK), BLK), :]
        for s in range(SLOTS)
    ]
    return jnp.concatenate(parts, axis=0)


def gathered(pieces, places, target, sem, first):
    copies = []
    for k, (piece, place) in enumerate(zip(pieces, places)):
        copy = pltpu.make_async_copy(piece, target.at[pl.ds(place, piece.shape[0])], sem.at[first + k])
        copy.start()
        copies.append(copy)
    return copies


def put(source, target, sem, place):
    copy = pltpu.make_async_copy(source, target, sem.at[place])
    copy.start()
    return copy


def over(value, size):
    assert size & (size - 1) == 0
    return lax.shift_right_logical(value, size.bit_length() - 1)


def within(value, size):
    assert size & (size - 1) == 0
    return value & (size - 1)


def absolute_chunk(turn, own, seqs, group):
    return (within(turn, seqs) * group + over(turn, seqs)) ^ own


def split_kernel(tail, at_ref, rows_ref, *rest):
    positions, seqs, width = rows_ref.shape
    if tail:
        line_ref, *rest = rest
    for p, ref in enumerate(rest):
        for s in range(seqs):

            @pl.when((at_ref[3] ^ p) == s)
            def _(ref=ref, s=s):
                ref[:positions, :] = rows_ref[:, s, :]
                if tail:
                    blank = jnp.zeros((tail - 1, width), F32)
                    line = line_ref[s : s + 1, :].astype(F32)
                    ref[positions:, :] = jnp.concatenate([line, blank], axis=0).astype(BF16)


def split_planes(turns, rows, line=None):
    positions, seqs, width = rows.shape
    tail = 0 if line is None else 16
    shape = jax.ShapeDtypeStruct((positions + tail, width), BF16)
    ins = (turns, rows) if line is None else (turns, rows, line)
    return local_call(partial(split_kernel, tail), (shape,) * seqs, ins, [], "split_planes")


def forward_kernel(heads, group, seqs, counts, at_ref, bias_ref, *rest):
    x_pieces, w_pieces, rest = rest[: counts[0]], rest[counts[0] : sum(counts)], rest[sum(counts) :]
    x_out, q_out, k_out, v_out, loc_ref = rest[:5]
    ctx_refs, rest = rest[5 : 5 + group], rest[5 + group :]
    x_s, q_s, k_s, v_s, w_s, seg_s, number_v, number_s, sem = rest
    chunks, tall, width = x_s.shape
    chunk, blocks = x_out.shape[1], q_s.shape[1] // BLK
    rows = chunks * chunk
    w_rows = width // counts[1]
    w_copies = gathered(
        [piece.at[pl.ds(0, w_rows)] for piece in w_pieces],
        [pl.multiple_of((at_ref[0] ^ k) * w_rows, 16) for k in range(counts[1])],
        w_s,
        sem,
        counts[0],
    )
    last = sum(counts)
    x_copies, turn = [], 0
    for piece in x_pieces:
        count = piece.shape[0]
        x_copies.append(put(piece, x_s.at[pl.ds(turn, count)], sem, last + 5 + turn))
        turn += count
    for copy in w_copies:
        copy.wait()
    for copy in x_copies:
        copy.wait()
    out_copies = [put(x_s.at[:, pl.ds(0, chunk)], x_out, sem, last)]
    tile = 2 * chunk
    lines = jnp.concatenate(
        [x_s[k, chunk:, : 2 * LANES].astype(F32)[:1] for k in range(chunks)], axis=0
    )
    number_v[...] = lines[:, LANES:].astype(jnp.int32)
    number_copy = put(number_v, number_s, sem, last + 4)
    seg_s[...] = jnp.concatenate([lines[:, :LANES], jnp.zeros((LANES - chunks, LANES), F32)], axis=0).T
    number_copy.wait()
    per = chunk // BLK
    own, member = at_ref[5], at_ref[4]

    def place_of(block):
        c = over(block, per) ^ own
        return (within(c, group) * seqs + over(c, group)) * per + within(block, per)

    def slots_of(j):
        turn, inner = over(j, per), within(j, per)
        real = absolute_chunk(turn, own, seqs, group) * per + inner
        fixed = []
        for d in (-1, 0, 1):
            near = jnp.clip(real + d, 0, blocks - 1)
            fixed.append(jnp.where(near == real + d, place_of(near), blocks))
        for b in range(2):
            fixed.append(jnp.where(jnp.abs(real - b) > 1, place_of(jnp.int32(b)), blocks))
        first = member * (LANES // group) + inner * (heads * 3)
        for h in range(heads):
            free = [place_of(number_s[turn, first + h * 3 + r]) for r in range(3)]
            for s, value in enumerate(fixed + free):
                loc_ref[(j * heads + h) * SLOTS + s] = value

    def project(i, carry):
        at = pl.ds(pl.multiple_of(i * tile, tile), tile)
        x = jnp.concatenate([x_s[2 * i, :chunk, :], x_s[2 * i + 1, :chunk, :]], axis=0)
        lane = lane_ids((tile, LANES))
        seg = []
        for k in range(2):
            mine = lane_ids((LANES, LANES)) == 2 * i + k
            seg.append(jnp.sum(jnp.where(mine, seg_s[...], 0.0), axis=1, keepdims=True))
        same = (lane - HD).astype(F32) == jnp.concatenate(seg, axis=0)
        coded = (lane >= HD) & (lane < HD + DOCS)
        ones = (lane >= HD + DOCS) & (lane < HD + DOCS + 3)
        q_extra = jnp.where(coded & same, NEGATIVE, 0.0)
        k_extra = jnp.where((coded & jnp.logical_not(same)) | ones, 1.0, 0.0)
        v_extra = jnp.where((lane >= HD) & (lane < HD + 3), 1.0, 0.0)
        head_lane = lane < HD
        y = dot(x, w_s[...], ((1,), (0,))) + bias_ref[...]
        for part, extra, ref in ((0, k_extra, k_s), (1, v_extra, v_s), (2, q_extra, q_s)):
            for h in range(heads):
                n = part * heads + h
                here = y[:, n // 2 * LANES : (n // 2 + 1) * LANES]
                if n % 2:
                    here = pltpu.roll(here, HD, 1)
                elif here.shape[1] < LANES:
                    here = jnp.concatenate([here, jnp.zeros((tile, LANES - here.shape[1]), F32)], axis=1)
                ref[h, at, :] = jnp.where(head_lane, here, extra).astype(BF16)
        for k in range(2 * per):
            slots_of(i * 2 * per + k)
        return carry

    lax.fori_loop(0, rows // tile, project, 0)
    lane = lane_ids((BLK, LANES))
    null_key = jnp.where((lane >= HD) & (lane < HD + DOCS), 1.0, 0.0).astype(BF16)
    for h in range(heads):
        k_s[h, rows : rows + BLK, :] = null_key
        v_s[h, rows : rows + BLK, :] = jnp.zeros((BLK, LANES), BF16)
    out_copies += [put(k_s, k_out, sem, last + 1), put(v_s, v_out, sem, last + 2)]
    part_blocks = rows // BLK // group
    together = 4

    for r in range(group):

        def attend(i, carry, r=r):
            units = [(u, h) for u in range(together) for h in range(heads)]
            row = [r * part_blocks + i * together + u for u in range(together)]
            at = [pl.ds(pl.multiple_of(j * BLK, BLK), BLK) for j in row]
            place = [(row[u] * heads + h) * SLOTS for u, h in units]
            q = [q_s[h, at[u], :] for u, h in units]
            scores = [
                dot(q[n], picked(k_s, loc_ref, h, place[n]), ((1,), (1,))) for n, (u, h) in enumerate(units)
            ]
            top = [jnp.max(t, axis=1, keepdims=True) for t in scores]
            prob = [jnp.exp2((t - m) * RATE).astype(BF16) for t, m in zip(scores, top)]
            mixed = [
                dot(prob[n], picked(v_s, loc_ref, h, place[n]), ((1,), (0,))) for n, (u, h) in enumerate(units)
            ]
            total = [m[:, HD : HD + 1] for m in mixed]
            done = [(m / t)[:, :HD] for m, t in zip(mixed, total)]
            level = [-(m + jnp.log2(t) * (1.0 / RATE)) for m, t in zip(top, total)]
            for n, (u, h) in enumerate(units):
                q_s[h, at[u], :] = place_three(q[n].astype(F32), level[n], lane, HD + DOCS).astype(BF16)
            for u in range(together):
                here = pl.ds(pl.multiple_of((i * together + u) * BLK, BLK), BLK)
                ctx_refs[r][here, :] = jnp.concatenate(done[u * heads : (u + 1) * heads], axis=1).astype(BF16)
            return carry

        lax.fori_loop(0, part_blocks // together, attend, 0)
    out_copies.append(put(q_s, q_out, sem, last + 3))
    for copy in out_copies:
        copy.wait()


def backward_kernel(heads, group, count, loc_ref, at_ref, q_in, k_in, v_in, *rest):
    w_pieces, rest = rest[:count], rest[count:]
    ctx_refs, grad_refs, rest = rest[:group], rest[group : 2 * group], rest[2 * group :]
    keep_ref, send_ref, d_out, out_ref, da_s, dq_s, w_s, keep_s, send_s, qa_ref, ka_ref, va_ref, sem, *rest = rest
    dk_even, dk_odd, dv_even, dv_odd = (rest[i * heads : (i + 1) * heads] for i in range(4))
    rows, width = qa_ref.shape[1], w_s.shape[0]
    loads = [
        put(*pair, sem, count + 2 + n)
        for n, pair in enumerate(((q_in, qa_ref), (k_in, ka_ref), (v_in, va_ref)))
    ]
    w_rows = width // count
    w_copies = gathered(
        [piece.at[pl.ds(0, w_rows)] for piece in w_pieces],
        [pl.multiple_of((at_ref[0] ^ k) * w_rows, 16) for k in range(count)],
        w_s,
        sem,
        0,
    )
    part_rows = rows // group
    tile = 128
    lane_tile = lane_ids((tile, LANES))
    blank = jnp.zeros((tile, LANES - HD), F32)

    def load(i, carry):
        at = pl.ds(pl.multiple_of(i * tile, tile), tile)
        for r in range(group):
            all_at = pl.ds(pl.multiple_of(r * part_rows + i * tile, tile), tile)
            grads = grad_refs[r][at, :].astype(F32)
            both = grads * ctx_refs[r][at, :].astype(F32)
            for h in range(heads):
                cols = slice(h * HD, (h + 1) * HD)
                delta = jnp.sum(both[:, cols], axis=1, keepdims=True)
                wide = jnp.concatenate([grads[:, cols], blank], axis=1)
                da_s[h, all_at, :] = place_three(wide, -delta, lane_tile, HD).astype(BF16)
        for b in range(rows // BLK // (part_rows // tile)):
            for ref in (*dk_even, *dk_odd, *dv_even, *dv_odd):
                ref[i * (rows // BLK // (part_rows // tile)) + b] = jnp.zeros((HD, LANES), F32)
        return carry

    lax.fori_loop(0, part_rows // tile, load, 0)
    for ref in (*dk_even, *dk_odd, *dv_even, *dv_odd):
        ref[rows // BLK] = jnp.zeros((HD, LANES), F32)
    for copy in loads:
        copy.wait()
    together = 4

    def attend(i, carry):
        units = [(u, h) for u in range(together) for h in range(heads)]
        row = [i * together + u for u in range(together)]
        at = [pl.ds(pl.multiple_of(j * BLK, BLK), BLK) for j in row]
        place = [(row[u] * heads + h) * SLOTS for u, h in units]
        q = [qa_ref[h, at[u], :] for u, h in units]
        d_mixed = [da_s[h, at[u], :] for u, h in units]
        keys = [picked(ka_ref, loc_ref, h, place[n]) for n, (u, h) in enumerate(units)]
        values = [picked(va_ref, loc_ref, h, place[n]) for n, (u, h) in enumerate(units)]
        scores = [dot(a, b, ((1,), (1,))) for a, b in zip(q, keys)]
        d_prob = [dot(a, b, ((1,), (1,))) for a, b in zip(d_mixed, values)]
        prob = [jnp.exp2(t * RATE) for t in scores]
        d_scores = [(a * b).astype(BF16) for a, b in zip(prob, d_prob)]
        prob = [t.astype(BF16) for t in prob]
        d_q = [dot(a, b, ((1,), (0,))) for a, b in zip(d_scores, keys)]
        q_turned = [t.astype(F32).T[:HD].astype(BF16) for t in q]
        d_turned = [t.astype(F32).T[:HD].astype(BF16) for t in d_mixed]
        d_keys = [dot(a, b, ((1,), (0,))) for a, b in zip(q_turned, d_scores)]
        d_values = [dot(a, b, ((1,), (0,))) for a, b in zip(d_turned, prob)]
        for n, (u, h) in enumerate(units):
            dq_s[h, at[u], :] = (d_q[n] * SCALE).astype(BF16)
        for u in range(together):
            for s in range(SLOTS):
                for h in range(heads):
                    n = u * heads + h
                    to = loc_ref[place[n] + s]
                    cols = slice((s // 2) * LANES, (s // 2 + 1) * LANES)
                    dk_ref, dv_ref = (dk_odd[h], dv_odd[h]) if s % 2 else (dk_even[h], dv_even[h])
                    dk_ref[to] += d_keys[n][:, cols]
                    dv_ref[to] += d_values[n][:, cols]
        return carry

    lax.fori_loop(0, rows // BLK // together, attend, 0)
    low_lane = lane_ids((HD, LANES)) < BLK

    def finish(i, carry):
        at = [pl.ds(pl.multiple_of((2 * i + u) * BLK, BLK), BLK) for u in range(2)]
        turned = []
        for even, odd, factor in ((dk_even, dk_odd, SCALE), (dv_even, dv_odd, 1.0)):
            for h in range(heads):
                first = even[h][2 * i] + pltpu.roll(odd[h][2 * i], BLK, 1)
                second = pltpu.roll(even[h][2 * i + 1], BLK, 1) + odd[h][2 * i + 1]
                turned.append(jnp.where(low_lane, first, second) * factor)
        pair = pl.ds(pl.multiple_of(2 * i * BLK, 2 * BLK), 2 * BLK)
        for n in range(heads):
            both = jnp.concatenate([turned[2 * n], turned[2 * n + 1]], axis=0)
            out_ref[pair, n * LANES : (n + 1) * LANES] = both.T.astype(BF16)
        done = [dq_s[h, pair, :][:, :HD].astype(F32) for h in range(heads)]
        out_ref[pair, heads * LANES :] = jnp.concatenate(done, axis=1).astype(BF16)
        return carry

    lax.fori_loop(0, rows // BLK // 2, finish, 0)
    out_copies = [put(out_ref, d_out, sem, count + 5)]
    for copy in w_copies:
        copy.wait()
    for odd, hold, ref in ((1, send_s, send_ref), (0, keep_s, keep_ref)):

        def to_rows(i, carry, odd=odd, hold=hold):
            at = pl.ds(pl.multiple_of((2 * i + odd) * part_rows, BLK), part_rows)
            hold[i] = dot(out_ref[at, :], w_s[...], ((1,), (1,))).astype(hold.dtype)
            return carry

        lax.fori_loop(0, group // 2, to_rows, 0)
        out_copies.append(put(hold, ref, sem, count + odd))
    for copy in out_copies:
        copy.wait()


def projection_grad_kernel(at_ref, x_in, d_in, mine_ref, theirs_ref, x_s, d_s, sem):
    copies = [put(x_in, x_s, sem, 0), put(d_in, d_s, sem, 1)]
    half = x_s.shape[1] // 2
    copies[1].wait()
    sums = row_sum(d_s[...].astype(F32))
    shape = (64, sums.shape[1])
    tail = jnp.where(lax.broadcasted_iota(jnp.int32, shape, 0) == 0, jnp.broadcast_to(sums, shape), 0.0)
    copies[0].wait()
    for k, ref in ((1, theirs_ref), (0, mine_ref)):
        cols = pl.ds(pl.multiple_of((at_ref[0] ^ k) * half, LANES), half)
        grad = jnp.concatenate([dot(x_s[:, cols], d_s[...], ((0,), (0,))), tail], axis=0).astype(BF16)
        size = grad.shape[0] // 4
        for z in range(4):
            ref[plane_spot(z, at_ref[3])] = grad[z * size : (z + 1) * size]


def cost(microseconds):
    return pl.CostEstimate(flops=int(microseconds * WEIGHT), bytes_accessed=0, transcendentals=0)


def whole(memory):
    return pl.BlockSpec(memory_space=memory)


def pieces_of(group, rows, columns):
    half = group // 2
    near = jax.ShapeDtypeStruct((rows, columns), BF16)
    return (near,) * half + (jax.ShapeDtypeStruct((half, rows, columns), BF16),)


def attention_forward(turns, x_pieces, w_pieces, bias, heads, group, seqs, positions):
    chunks, width = group * seqs, x_pieces[0].shape[2]
    rows = positions * chunks
    counts = (len(x_pieces), len(w_pieces))
    kept = jax.ShapeDtypeStruct((heads, rows + BLK, LANES), BF16)
    return pl.pallas_call(
        partial(forward_kernel, heads, group, seqs, counts),
        out_shape=(
            jax.ShapeDtypeStruct((chunks, positions, width), BF16),
            jax.ShapeDtypeStruct((heads, rows, LANES), BF16),
            kept,
            kept,
            jax.ShapeDtypeStruct((rows // BLK * heads * SLOTS,), jnp.int32),
        )
        + (jax.ShapeDtypeStruct((rows // group, heads * HD), BF16),) * group,
        in_specs=[whole(pltpu.SMEM), whole(pltpu.VMEM)] + [whole(pl.ANY)] * sum(counts),
        out_specs=(whole(pl.ANY),) * 4 + (whole(pltpu.SMEM),) + (whole(pltpu.VMEM),) * group,
        scratch_shapes=[
            pltpu.VMEM((chunks, positions + 16, width), BF16),
            pltpu.VMEM((heads, rows, LANES), BF16),
            pltpu.VMEM((heads, rows + BLK, LANES), BF16),
            pltpu.VMEM((heads, rows + BLK, LANES), BF16),
            pltpu.VMEM((width, 3 * heads * HD), BF16),
            pltpu.VMEM((LANES, LANES), F32),
            pltpu.VMEM((chunks, LANES), jnp.int32),
            pltpu.SMEM((chunks, LANES), jnp.int32),
            pltpu.SemaphoreType.DMA((sum(counts) + 5 + chunks,)),
        ],
        compiler_params=pltpu.CompilerParams(vmem_limit_bytes=56 * MIB),
        cost_estimate=cost(19),
        name="attention_forward",
    )(turns, bias, *x_pieces, *w_pieces)


def attention_backward(loc, turns, qa, ka, va, w_pieces, width, ctx_parts, grads, heads):
    rows = qa.shape[1]
    blocks, group, count, slab = rows // BLK, len(grads), len(w_pieces), heads * HD
    part = (group // 2, rows // group, width)
    outs = (
        jax.ShapeDtypeStruct(part, F32),
        jax.ShapeDtypeStruct(part, BF16),
        jax.ShapeDtypeStruct((rows, 3 * slab), BF16),
    )
    return pl.pallas_call(
        partial(backward_kernel, heads, group, count),
        out_shape=outs,
        in_specs=[whole(pltpu.SMEM)] * 2
        + [whole(pl.ANY)] * (3 + count)
        + [whole(pltpu.VMEM)] * (2 * group),
        out_specs=(whole(pl.ANY),) * 3,
        scratch_shapes=[
            pltpu.VMEM((rows, 3 * slab), BF16),
            pltpu.VMEM((heads, rows, LANES), BF16),
            pltpu.VMEM((heads, rows, LANES), BF16),
            pltpu.VMEM((width, 3 * slab), BF16),
            pltpu.VMEM(part, F32),
            pltpu.VMEM(part, BF16),
            pltpu.VMEM(qa.shape, BF16),
            pltpu.VMEM(ka.shape, BF16),
            pltpu.VMEM(va.shape, BF16),
            pltpu.SemaphoreType.DMA((count + 6,)),
        ]
        + [pltpu.VMEM((blocks + 1, HD, LANES), F32)] * (4 * heads),
        compiler_params=pltpu.CompilerParams(vmem_limit_bytes=56 * MIB),
        cost_estimate=cost(50),
        name="attention_backward",
    )(loc, turns, qa, ka, va, *w_pieces, *ctx_parts, *grads)


def norm_values(values):
    average = jnp.mean(values, axis=-1, keepdims=True)
    centred = values - average
    inv_std = lax.rsqrt(jnp.mean(centred * centred, axis=-1, keepdims=True) + EPSILON)
    return centred * inv_std, inv_std


def norm_pull(upstream, scaled, inv_std, gain_row):
    weighted = upstream * gain_row
    centre_term = jnp.mean(weighted, axis=-1, keepdims=True)
    slope_term = jnp.mean(weighted * scaled, axis=-1, keepdims=True)
    return inv_std * (weighted - centre_term - scaled * slope_term)


def gelu_pair(v):
    rate = math.sqrt(2.0 / math.pi)
    square = v * v
    t = jnp.tanh(rate * v * (1.0 + 0.044715 * square))
    half = 0.5 * (1.0 + t)
    slope = half + (0.5 * rate) * v * (1.0 - t * t) * (1.0 + (3.0 * 0.044715) * square)
    return v * half, slope


def row_sum(values):
    return jnp.sum(values, axis=0, keepdims=True)


def layer_kernel(group, count, plan, seqs, fast, at_ref, x_ref, vec_ref, upb_ref, *rest):
    ctx_refs = rest[:group]
    arrays, rest = rest[group : group + count], rest[group + count :]
    cot_refs, result_refs, rest = rest[:seqs], rest[seqs : 2 * seqs], rest[2 * seqs :]
    if fast:
        early, (dh1_ref, dhid_mine, dbr_mine, pack_two, small_ref) = rest[:4], rest[4:9]
        rest = rest[9:]
        slab = ctx_refs[0].shape[1]
    else:
        dh1_ref, active_ref, dhid_ref, first_low_ref, dsec_ref, dbr_ref, sums_out, upb_out = rest[:8]
        rest = rest[8:]
    near, far, rest = rest[: group // 2], rest[group // 2], rest[group // 2 + 1 :]
    dctx_refs = [*near, *[far.at[r] for r in range(group // 2)]]
    out_s, up_s, down_s, slope_s, scaled_s, inv_s, acc_s, cot_s, result_s, x_s, dbr_s, sums_s, upb_s, sem = rest[:14]
    if fast:
        act_mine, pack_one, dsec_ref, first_low_ref = rest[14:]
    rows, width = acc_s.shape
    hidden = up_s.shape[1]
    member = at_ref[0]
    core = member & 1
    copies = []
    for k, (array, column, w) in enumerate(plan):
        scratch, source = (out_s, up_s, down_s)[w], arrays[array]
        if column is not None:
            source = source.at[:, pl.ds(column, scratch.shape[-1])]
        start = pl.multiple_of(at_ref[1 + k], 1 if w == 0 else 16)
        one = w == 0 and len(source.shape) == 2
        copies.append(put(source, scratch.at[start] if one else scratch.at[pl.ds(start, source.shape[0])], sem, k))
    k = len(plan)
    part_rows = rows // seqs
    starts = [p * part_rows for p in range(seqs)]
    cot_copies = gathered(cot_refs, starts, cot_s, sem, k)
    x_copy = put(x_ref.at[pl.ds(0, rows)], x_s, sem, k + 2 * seqs)
    b_out, b_first, b_last, b_second = (vec_ref[i : i + 1, :] for i in (2, 3, 4, 5))
    gain_one, gain_two = vec_ref[6:7, :], vec_ref[7:8, :]
    tile = min(256, rows)
    sums_s[...] = jnp.zeros_like(sums_s)

    for copy in [x_copy] + [copy for copy, (_, _, w) in zip(copies, plan) if w == 0]:
        copy.wait()

    def first_norm(i, carry):
        at = pl.ds(pl.multiple_of(i * tile, tile), tile)
        total = x_s[at, :].astype(F32) + b_out
        for r in range(group):
            total = total + dot(ctx_refs[r][at, :], out_s[member ^ r], ((1,), (0,)))
        scaled, inv_std = norm_values(total)
        first = scaled * gain_one + b_first
        scaled_s[at, :] = scaled
        inv_s[at, :] = jnp.broadcast_to(inv_std, (tile, LANES))
        first_low_ref[at, :] = first.astype(BF16)
        acc_s[at, :] = first + b_second
        return carry

    lax.fori_loop(0, rows // tile, first_norm, 0)
    for copy in [copy for copy, (_, _, w) in zip(copies, plan) if w > 0]:
        copy.wait()

    def up_down(start, step, ref, to):
        at = pl.ds(pl.multiple_of(start, step), step)
        v = dot(first_low_ref[...], up_s[:, at], ((1,), (0,))) + upb_ref[:, at]
        active, slope = gelu_pair(v)
        active = active.astype(BF16)
        ref[:, pl.ds(pl.multiple_of(to, step), step)] = active
        slope_s[:, at] = slope
        acc_s[...] += dot(active, down_s[at, :], ((1,), (0,)))

    def down_up(start, step, ref, to):
        at = pl.ds(pl.multiple_of(start, step), step)
        d_hidden = dot(dsec_ref[...], down_s[at, :], ((1,), (1,))) * slope_s[:, at]
        low = d_hidden.astype(BF16)
        ref[:rows, pl.ds(pl.multiple_of(to, step), step)] = low
        upb_s[:, at] = row_sum(low.astype(F32))
        acc_s[...] += dot(low, up_s[:, at], ((1,), (1,)))

    def over_hidden(one, refs):
        if fast:
            step = hidden // 4
            for c, ref in enumerate(refs):

                def part(i, carry, c=c, ref=ref):
                    turn = c ^ core
                    one((i * 2 + turn if one is up_down else turn * 2 + i) * step, step, ref, i * step)
                    return carry

                for i in range(2):
                    part(i, 0)
        else:
            step = 512

            def part(i, carry):
                one(i * step, step, refs[0], i * step)
                return carry

            lax.fori_loop(0, hidden // step, part, 0)

    over_hidden(up_down, (act_mine, pack_one) if fast else (active_ref,))
    for copy in cot_copies:
        copy.wait()

    def last_norm(i, carry):
        at = pl.ds(pl.multiple_of(i * tile, tile), tile)
        scaled, inv_std = norm_values(acc_s[at, :])
        result_s[at, :] = (scaled * gain_two + b_last).astype(BF16)
        upstream = cot_s[at, :].astype(F32)
        pulled = norm_pull(upstream, scaled, inv_std, gain_two)
        acc_s[at, :] = pulled
        low = pulled.astype(BF16)
        dsec_ref[at, :] = low
        if fast:
            pack_one[at, hidden // 2 :] = low
        sums_s[1:2, :] += row_sum(upstream * scaled)
        sums_s[4:5, :] += row_sum(upstream)
        sums_s[5:6, :] += row_sum(pulled)
        return carry

    lax.fori_loop(0, rows // tile, last_norm, 0)
    early_copies = []
    if fast:
        held = (act_mine, pack_one, dsec_ref, first_low_ref)
        early_copies = [put(a, b, sem, k + 2 * seqs + 1 + n) for n, (a, b) in enumerate(zip(held, early))]
    result_copies = [
        put(result_s.at[pl.ds(starts[p], part_rows)], result_refs[p], sem, k + seqs + p) for p in range(seqs)
    ]
    over_hidden(down_up, (dhid_mine, pack_two) if fast else (dhid_ref,))

    def first_back(i, carry):
        at = pl.ds(pl.multiple_of(i * tile, tile), tile)
        upstream, scaled = acc_s[at, :], scaled_s[at, :]
        pulled = norm_pull(upstream, scaled, inv_s[at, :1], gain_one)
        dh1_ref[at, :] = pulled
        low = pulled.astype(BF16)
        dbr_s[at, :] = low
        sums_s[0:1, :] += row_sum(upstream * scaled)
        sums_s[2:3, :] += row_sum(pulled)
        sums_s[3:4, :] += row_sum(upstream)
        for r in range(group):
            dctx_refs[r][at, :] = dot(low, out_s[member ^ r], ((1,), (1,))).astype(BF16)
        return carry

    lax.fori_loop(0, rows // tile, first_back, 0)
    if fast:
        half, wide = width // 2, hidden // 2
        dbr_mine[...] = dbr_s[:, pl.ds(pl.multiple_of(core * half, LANES), half)]
        pack_two[:rows, wide : wide + half] = dbr_s[:, pl.ds(pl.multiple_of((1 - core) * half, LANES), half)]
        pack_two[:rows, wide + half : wide + half + width] = first_low_ref[...]
        pack_two[:rows, wide + half + width :] = jnp.concatenate([ref[...] for ref in ctx_refs], axis=1)
        long = [upb_s[:, i * width : (i + 1) * width] for i in range(hidden // width)]
        blank = jnp.zeros((8 - len(long), width), F32)
        small = jnp.concatenate([sums_s[...], *long, blank], axis=0).astype(BF16)
        small_ref[...] = small
        pack_two[rows:, :width] = small
        pack_two[rows:, width:] = jnp.zeros((16, pack_two.shape[1] - width), BF16)
    else:
        dbr_ref[...] = dbr_s[...]
        sums_out[...] = sums_s[...]
        upb_out[...] = upb_s[...]
    for copy in result_copies + early_copies:
        copy.wait()


def layer(place, x_seq, cots, vectors, up_shift, ctx_parts, parts, plan, fast):
    rows, width = len(cots) * cots[0].shape[0], x_seq.shape[1]
    group, slab = len(ctx_parts), ctx_parts[0].shape[1]
    hidden = up_shift.shape[1]

    def like(columns, dtype=BF16, count=rows):
        return jax.ShapeDtypeStruct((count, columns), dtype)

    half, wide = width // 2, hidden // 2
    if fast:
        held = (like(wide), like(wide + width), like(width), like(width))
        outs = held + (like(width, F32), like(wide), like(half))
        outs += (like(wide + half + 2 * width, BF16, rows + 16), like(width, BF16, 16))
    else:
        held = ()
        outs = (like(width, F32), like(hidden), like(hidden), like(width), like(width), like(width))
        outs += (like(width, F32, 8), like(hidden, F32, 1))
    outs = (jax.ShapeDtypeStruct(cots[0].shape, BF16),) * len(cots) + outs + pieces_of(group, rows, slab)
    return pl.pallas_call(
        partial(layer_kernel, group, len(parts), plan, len(cots), fast),
        out_shape=outs,
        in_specs=[whole(pltpu.SMEM), whole(pl.ANY)]
        + [whole(pltpu.VMEM)] * (2 + group)
        + [whole(pl.ANY)] * (len(parts) + len(cots)),
        out_specs=(whole(pl.ANY),) * (len(cots) + len(held))
        + (whole(pltpu.VMEM),) * (len(outs) - len(cots) - len(held)),
        scratch_shapes=[
            pltpu.VMEM((group, slab, width), BF16),
            pltpu.VMEM((width, hidden), BF16),
            pltpu.VMEM((hidden, width), BF16),
            pltpu.VMEM((rows, hidden), F32),
            pltpu.VMEM((rows, width), F32),
            pltpu.VMEM((rows, LANES), F32),
            pltpu.VMEM((rows, width), F32),
            pltpu.VMEM((rows, width), BF16),
            pltpu.VMEM((rows, width), BF16),
            pltpu.VMEM((rows, width), BF16),
            pltpu.VMEM((rows, width), BF16),
            pltpu.VMEM((8, width), F32),
            pltpu.VMEM((1, hidden), F32),
            pltpu.SemaphoreType.DMA((len(plan) + 2 * len(cots) + 1 + len(held),)),
        ]
        + [pltpu.VMEM(one.shape, BF16) for one in held],
        compiler_params=pltpu.CompilerParams(vmem_limit_bytes=56 * MIB),
        cost_estimate=cost(29),
        name="feed_forward",
    )(place, x_seq, vectors, up_shift, *ctx_parts, *parts, *cots)


def plane_spot(z, own):
    turn = z ^ own
    return (turn & 1) * 2 + (turn >> 1)


def down_grad_kernel(at_ref, act_in, d_in, got_in, keep_ref, send_ref, act_ref, d_ref, got_ref, keep_s, send_s, sem):
    piece = keep_s.shape[2]
    chunk = 4 * piece
    wide = act_ref.shape[1]
    ins = [put(*pair, sem, k) for k, pair in enumerate(((d_in, d_ref), (act_in, act_ref), (got_in, got_ref)))]
    for copy in ins:
        copy.wait()
    outs = []
    for f, hold, ref in ((1, send_s, send_ref), (0, keep_s, keep_ref)):
        for x in range(2):
            t = (f ^ at_ref[0]) * 2 + (x ^ at_ref[2])
            at = pl.ds(pl.multiple_of(t * chunk, LANES), chunk)
            grad = dot(act_ref[:, at], d_ref[...], ((0,), (0,)))
            grad = (grad + dot(got_ref[:, at], got_ref[:, wide:], ((0,), (0,)))).astype(BF16)
            for z in range(4):
                hold[x, plane_spot(z, at_ref[3])] = grad[z * piece : (z + 1) * piece]
            outs.append(put(hold.at[x], ref.at[x], sem, 3 + 2 * f + x))
    for copy in outs:
        copy.wait()


def up_grad_kernel(at_ref, first_in, dhid_in, dbr_in, small_ref, got_in, *rest):
    ctx_refs, (keep_ref, send_ref), rest = rest[:4], rest[4:6], rest[6:]
    first_s, ctx_s, extra_s, first_ref, dhid_ref, dbr_ref, got_ref, keep_s, send_s, sem = rest
    half, step = keep_s.shape[2:]
    rows, width = first_ref.shape
    slab = ctx_refs[0].shape[1]
    wide, narrow = dhid_ref.shape[1], dbr_ref.shape[1]
    ins = [put(first_in, first_ref, sem, 0)]
    cuts = (wide + narrow, wide + narrow + width, wide + narrow + 2 * width)
    for k, (a, b) in enumerate(((cuts[0], cuts[1]), (cuts[1], cuts[2]), (0, cuts[0]))):
        ins.append(put(got_in.at[:, pl.ds(a, b - a)], got_ref.at[:, pl.ds(a, b - a)], sem, 1 + k))
    ins += [put(dhid_in, dhid_ref, sem, 4), put(dbr_in, dbr_ref, sem, 5)]
    for copy in ins[:3]:
        copy.wait()
    first_s[:, :rows] = first_ref[...].astype(F32).T.astype(BF16)
    first_s[:, rows:] = got_ref[:rows, wide + narrow : wide + narrow + width].astype(F32).T.astype(BF16)
    got_ctx = got_ref[:rows, wide + narrow + width :].astype(F32).T.astype(BF16)
    for r in range(4):
        ctx_s[at_ref[4] ^ r, :, :rows] = ctx_refs[r][...].astype(F32).T.astype(BF16)
        ctx_s[at_ref[4] ^ r ^ 1, :, rows:] = got_ctx[r * slab : (r + 1) * slab]
    ups = wide // step
    for copy in ins[3:]:
        copy.wait()
    extra_s[...] = jnp.zeros_like(extra_s)
    vectors = small_ref[...].astype(F32) + got_ref[rows:, :width].astype(F32)
    for f in range(2):
        for i in range(6):
            for k in range(half // LANES):
                start = f * half + k * LANES
                extra_s[f, i * (half // LANES) + k : i * (half // LANES) + k + 1, :] = vectors[
                    i : i + 1, start : start + LANES
                ]
        row = 6 * (half // LANES)
        for k in range(wide // LANES):
            start = f * wide + k * LANES
            extra_s[f, row + k : row + k + 1, :] = vectors[
                8 + start // width : 9 + start // width, start % width : start % width + LANES
            ]
    outs = []
    for x, ref, out in ((1, send_s, send_ref), (0, keep_s, keep_ref)):

        def one(i, carry, x=x, ref=ref):
            spot = (i & 1) * 2 + (i >> 1)
            k = (x ^ at_ref[2]) * 4 + (i ^ at_ref[3])

            def store(grad):
                for f in range(2):
                    ref[f ^ at_ref[0], spot] = grad[f * half : (f + 1) * half].astype(BF16)

            def out_grad(lanes):
                turned = ctx_s[...].reshape(width, 2 * rows)
                right = jnp.concatenate([dbr_ref[:, lanes], got_ref[:rows, wide + lanes.start : wide + lanes.stop]], axis=0)
                return dot(turned, right, ((1,), (0,)))

            @pl.when(k < ups)
            def _():
                at = pl.ds(pl.multiple_of(k * step, step), step)
                right = jnp.concatenate([dhid_ref[:, at], got_ref[:rows, at]], axis=0)
                store(dot(first_s[...], right, ((1,), (0,))))

            @pl.when(k == ups)
            def _():
                store(out_grad(slice(0, step)))

            @pl.when(k > ups)
            def _():
                extra = extra_s[...].reshape(width, LANES)
                store(jnp.concatenate([out_grad(slice(step, narrow)), extra], axis=1))

            return carry

        lax.fori_loop(0, 4, one, 0)
        outs.append(put(ref, out, sem, 6 + x))
    for copy in outs:
        copy.wait()


def down_final_kernel(at_ref, *rest):
    parts, (out_ref, in_s, out_s, sem) = rest[:4], rest[4:]
    piece = parts[0].shape[1]
    copies_in = [put(part, in_s.at[i], sem, i) for i, part in enumerate(parts)]
    copies = []
    for i in range(4):
        copies_in[i].wait()
        for z in range(4):
            k = (((i & 1) ^ at_ref[1]) * 2 + ((i >> 1) ^ at_ref[2])) * 4 + (z ^ at_ref[3])
            at = pl.ds(pl.multiple_of(k * piece, 16), piece)
            out_s[at, :] = in_s[i, (z & 1) * 2 + (z >> 1)].astype(F32)
            copies.append(put(out_s.at[at], out_ref.at[at], sem, 4 + i * 4 + z))
    for copy in copies:
        copy.wait()


def up_final_kernel(at_ref, *rest):
    parts, (up_ref, out_ref, gains_ref, biases_ref, upb_ref, in_s, out_s, sem) = rest[:4], rest[4:]
    step = parts[0].shape[2]
    wide, narrow = up_ref.shape[1] // 2, out_ref.shape[1] // 2
    ups = wide // step
    half = gains_ref.shape[1]
    count = half // LANES
    copies_in = [put(part, in_s.at[i], sem, i) for i, part in enumerate(parts)]

    def each(i, z, act):
        core = (i & 1) ^ at_ref[1]
        k = ((i >> 1) ^ at_ref[2]) * 4 + (z ^ at_ref[3])
        n = i * 4 + z

        @pl.when(k < ups)
        def _():
            at = pl.ds(pl.multiple_of(core * wide + k * step, LANES), step)
            act(pltpu.make_async_copy(out_s.at[n], up_ref.at[:, at], sem.at[4 + n]))

        @pl.when(k == ups)
        def _():
            at = pl.ds(pl.multiple_of(core * narrow, LANES), step)
            act(pltpu.make_async_copy(out_s.at[n], out_ref.at[:, at], sem.at[4 + n]))

        @pl.when(k > ups)
        def _():
            at = pl.ds(pl.multiple_of(core * narrow + step, LANES), LANES)
            act(pltpu.make_async_copy(out_s.at[n, :, pl.ds(0, LANES)], out_ref.at[:, at], sem.at[4 + n]))

        return core, k

    for i in range(4):
        copies_in[i].wait()
        for z in range(4):
            value = in_s[i, (z & 1) * 2 + (z >> 1)].astype(F32)
            out_s[i * 4 + z] = value
            core, k = each(i, z, lambda copy: copy.start())

            @pl.when((k > ups) & (core == 0))
            def _(value=value):
                extra = value[:, LANES:]
                for a in range(6):
                    for b in range(count):
                        row = extra[a * count + b : a * count + b + 1]
                        lanes = slice(b * LANES, (b + 1) * LANES)
                        if a < 2:
                            gains_ref[a : a + 1, lanes] = row
                        else:
                            biases_ref[a - 2 : a - 1, lanes] = row
                for b in range(upb_ref.shape[0] // LANES):
                    upb_ref[b * LANES : (b + 1) * LANES] = extra[6 * count + b]

    for i in range(4):
        for z in range(4):
            each(i, z, lambda copy: copy.wait())


def qkv_final_kernel(at_ref, late_ref, *rest):
    parts, (out_ref, biases_ref, hold, in_s, out_s, sums_s, sem) = rest[:4], rest[4:]
    half, slab = out_s.shape[0], hold.shape[2] // 3
    width = 4 * slab
    size = parts[0].shape[1]
    copies = [put(part, in_s.at[i], sem, i) for i, part in enumerate(parts)]
    for r in range(4):
        copies[r].wait()
        for z in range(4):
            at = pl.ds(pl.multiple_of((z ^ at_ref[3]) * size, 16), size)
            hold[at_ref[4] ^ r, at, :] = in_s[r, (z & 1) * 2 + (z >> 1)]
    outs = []
    for k, column in ((0, 1), (1, 2), (2, 0)):
        for m in range(4):
            cols = slice(column * width + m * slab, column * width + (m + 1) * slab)
            out_s[:, cols] = hold[m, :half, k * slab : (k + 1) * slab].astype(F32)
        at = pl.ds(column * width, width)
        outs.append(put(out_s.at[:, at], out_ref.at[:, at], sem, 4 + k))
    for k, row in ((2, 0), (1, 1)):
        sums = [hold[m, half : half + 16, k * slab : (k + 1) * slab].astype(F32)[:1] for m in range(4)]
        sums_s[row : row + 1, :] = jnp.concatenate(sums, axis=1)
    biases_ref[0:2, :] = sums_s[0:2, pl.ds(pl.multiple_of(at_ref[0] * half, LANES), half)]
    biases_ref[2:6, :] = late_ref[...]
    for copy in outs:
        copy.wait()


def local_call(kernel, outs, ins, scratch, name, time=3, loose=(), limit=28):
    return pl.pallas_call(
        kernel,
        out_shape=outs,
        in_specs=[whole(pltpu.SMEM)]
        + [whole(pl.ANY if i in loose else pltpu.VMEM) for i in range(1, len(ins))],
        out_specs=tuple(whole(pl.ANY if len(ins) + i in loose else pltpu.VMEM) for i in range(len(outs))),
        scratch_shapes=scratch,
        compiler_params=pltpu.CompilerParams(vmem_limit_bytes=limit * MIB),
        cost_estimate=cost(time),
        name=name,
    )(*ins)


def swap_joint(value, f_mask, c_mask):
    n_f, n_c = lax.axis_size("fsdp"), lax.axis_size("ctx")
    pairs = [(f * n_c + c, (f ^ f_mask) * n_c + (c ^ c_mask)) for f in range(n_f) for c in range(n_c)]
    return lax.ppermute(value, ("fsdp", "ctx"), pairs)


def sum_planes(own, others):
    total = own.astype(F32)
    for other in others:
        total = total + other.astype(F32)
    return total.astype(BF16)


def reduce_square(keep, got, after, axis, mask):
    first, second = sum_planes(gate(keep[0], after), [got[0]]), sum_planes(keep[1], [got[1]])
    return first, swap(second, axis, mask)


def reduce_planes(mine, late=(), last=()):
    two = sum_planes(mine[:2], [swap(mine[2:], "ctx", 4)])
    piece = gate(sum_planes(two[0], [swap(two[1], "ctx", 8)]), *late)
    four = jnp.stack([piece] + [swap(piece, "ctx", mask) for mask in (8, 4, 12)])
    across = swap(four, "ctx", 2)
    return four, [four, swap(four, "ctx", 1), across, swap(gate(across, *last), "ctx", 1)]


def exchange(near, far, between=None):
    half = len(near)
    got = swap(far, "ctx", half)
    if between is not None:
        got = gate(got, between)
    items = {(d, 0): near[d] for d in range(half)}
    items.update({(d, half): got[d] for d in range(half)})
    for bit in reversed(bits_of(half)):
        for d, source in [key for key in items if key[0] & bit]:
            items[d ^ bit, source ^ bit] = swap(items.pop((d, source)), "ctx", bit)
    return [items[0, source] for source in range(2 * half)]


def gather_fsdp(value):
    index = lax.axis_index("fsdp")
    parts = [value]
    for bit in bits_of(lax.axis_size("fsdp")):
        parts += [swap(part, "fsdp", bit) for part in parts]
    return to_absolute(parts, index)


def fetch_halves(value):
    half = value.shape[0] // 2
    parts = [lax.dynamic_slice_in_dim(value, (lax.axis_index("ctx") & 1) * half, half, 0)]
    for bit in bits_of(lax.axis_size("fsdp")):
        parts += [swap(part, "fsdp", bit) for part in parts]
    return parts[1:]


def weight_parts(value, halves):
    index = lax.axis_index("fsdp")
    core = lax.axis_index("ctx") & 1
    size = value.shape[0]
    half = size // 2
    pieces, places = [value], [index * size]
    for k, part in enumerate(halves, 1):
        pieces += [part, swap(part, "ctx", 1)]
        first = (index ^ k) * size
        places += [first + core * half, first + (1 - core) * half]
    return pieces, places


def halve(value, axis, dim, mask, index):
    half = value.shape[dim] // 2
    bit = (index // mask) & 1
    mine = lax.dynamic_slice_in_dim(value, bit * half, half, dim)
    theirs = lax.dynamic_slice_in_dim(value, (1 - bit) * half, half, dim)
    return mine + swap(theirs.astype(BF16), axis, mask).astype(F32)


def double(value, axis, dim, mask, index):
    bit = (index // mask) & 1
    other = swap(value, axis, mask)
    return lax.select_n(
        bit,
        jnp.concatenate([value, other], axis=dim),
        jnp.concatenate([other, value], axis=dim),
    )


def reduce_over_all(value):
    f_index, c_index = lax.axis_index("fsdp"), lax.axis_index("ctx")
    value = halve(value, "ctx", 1, 1, c_index)
    for bit in reversed(bits_of(lax.axis_size("fsdp"))):
        value = halve(value, "fsdp", 0, bit, f_index)
    value = value[0]
    rest = bits_of(lax.axis_size("ctx"))[1:]
    for bit in rest:
        value = halve(value, "ctx", 0, bit, c_index)
    value = value.astype(BF16)
    for bit in reversed(rest):
        value = double(value, "ctx", 0, bit, c_index)
    return double(value, "ctx", 0, 1, c_index).astype(F32)


def local(
    tokens, segments, rand_blocks, w_qkv, w_out, w_up, w_down, ln_gains, biases, up_bias, cotangent
):
    positions, seq_count, width = tokens.shape
    n_f, n_c = lax.axis_size("fsdp"), lax.axis_size("ctx")
    f_index, c_index = lax.axis_index("fsdp"), lax.axis_index("ctx")
    group = n_c // seq_count
    plane, member = c_index // group, c_index % group
    head_count = width // HD
    heads = -(-head_count // group)
    per_chunk = positions // BLK
    blocks = per_chunk * n_c
    rows_here = seq_count * positions
    f_width = width // n_f
    slab = heads * HD
    spare = group * slab - width

    def to_planes(parts):
        return [swap(part, "ctx", p * group) if p else part for p, part in enumerate(parts)]

    def from_planes(parts):
        return jnp.stack(to_absolute(parts, plane), axis=1)

    fast = n_f == 2 and group == 4 and seq_count == 4 and not spare and f_width % slab == 0
    turns = jnp.stack([f_index, member & 1, (member >> 1) & 1, plane, member, c_index])
    rand = jnp.pad(rand_blocks, ((0, 0), (0, 0), (0, group * heads - head_count), (0, 0)))
    rand = rand.reshape(seq_count, per_chunk, group, heads, -1).transpose(0, 2, 1, 3, 4)
    rand = rand.reshape(seq_count, group, -1)
    rand = jnp.pad(rand, ((0, 0), (0, 0), (0, LANES // group - rand.shape[2])))
    line = jnp.concatenate([segments.T, rand.reshape(seq_count, LANES)], axis=1).astype(BF16)
    line = jnp.pad(line, ((0, 0), (0, width - line.shape[1])))
    token_parts = split_planes(turns, tokens, line)
    w_qkv, small_in = lax.optimization_barrier(((w_qkv, (ln_gains, biases, up_bias)), *token_parts))[0]
    ln_gains, biases, up_bias = small_in
    x_rows = to_planes(token_parts)
    if fast:
        across = [swap(part, "ctx", 2) for part in x_rows]
        x_pieces = [*x_rows, swap(jnp.concatenate(x_rows), "ctx", 1), *across]
        x_pieces += [swap(part, "ctx", 1) for part in across]
    else:
        x_all = {(0, p): x_rows[p] for p in range(seq_count)}
        for bit in reversed(bits_of(group)):
            for r, p in list(x_all):
                x_all[r ^ bit, p] = swap(x_all[r, p], "ctx", bit)
        x_pieces = [x_all[r, p] for r in range(group) for p in range(seq_count)]

    w_parts = jnp.pad(w_qkv.reshape(-1, 3, width), ((0, 0), (0, 0), (0, spare))) if spare else None
    if spare:
        w_mine = [lax.dynamic_slice_in_dim(w_parts[:, k], member * slab, slab, 1) for k in (1, 2, 0)]
    else:
        w_mine = [lax.dynamic_slice_in_dim(w_qkv, k * width + member * slab, slab, 1) for k in (1, 2, 0)]
    small = jnp.concatenate([ln_gains.reshape(-1), biases.reshape(-1), up_bias])
    small_rows = -(-small.shape[0] // (3 * slab) // 16) * 16
    small_count = small.shape[0]
    small = jnp.pad(small, (0, small_rows * 3 * slab - small_count)).reshape(small_rows, 3 * slab)
    w_mine = jnp.concatenate([jnp.concatenate(w_mine, axis=1), small], axis=0)
    w_pieces = [w_mine]
    for bit in bits_of(n_f):
        w_pieces += [swap(part, "fsdp", bit) for part in w_pieces]
    small = [part[f_width:].reshape(-1)[:small_count] for part in w_pieces]
    small = jnp.stack(to_absolute(small, f_index)).astype(F32)
    gains_all = small[:, : 2 * f_width].reshape(n_f, 2, f_width).transpose(1, 0, 2).reshape(2, width)
    biases_all = (
        small[:, 2 * f_width : 8 * f_width].reshape(n_f, 6, f_width).transpose(1, 0, 2).reshape(6, width)
    )
    up_shift = small[:, 8 * f_width :].reshape(-1)
    bias_mine = lax.dynamic_slice_in_dim(
        jnp.pad(biases_all[:2], ((0, 0), (0, spare))), member * slab, slab, 1
    ).reshape(2, heads, HD)
    bias_wide = jnp.concatenate(
        [jnp.zeros_like(bias_mine[0]), bias_mine[1], bias_mine[0]], axis=0
    ).reshape(1, -1)

    cot_in = gate(cotangent, x_rows)
    cots = to_planes([lax.dynamic_index_in_dim(cot_in, plane ^ p, 1, keepdims=False) for p in range(seq_count)])
    if fast:
        core, chip = member & 1, member >> 1
        quarter, half = f_width // 4, f_width // 2
        up_quarter = lax.dynamic_slice_in_dim(w_up, (core * 2 + chip) * quarter, quarter, 0)
        up_quarter = gate(up_quarter, w_mine, across[0])
        tall = w_down.shape[0] // 2
        joint = lax.dynamic_slice_in_dim(w_down, core * tall, tall, 0).reshape(-1, half, width)
        joint = [lax.dynamic_slice_in_dim(w_out, core * half, half, 0), *joint]
        joint = swap(gate(jnp.concatenate(joint, axis=1), up_quarter), "fsdp", 1)
        up_quarter = swap(up_quarter, "fsdp", 1)
        up_across = swap(up_quarter, "ctx", 2)
    else:
        up_halves = fetch_halves(w_up)
        down_halves = fetch_halves(w_down)
    x_pieces = [piece.reshape(-1, positions + 16, width) for piece in x_pieces]
    x_seq, qa, ka, va, loc, *ctx_parts = attention_forward(
        turns, x_pieces, w_pieces, bias_wide, heads, group, seq_count, positions
    )
    x_seq = x_seq.reshape(blocks * BLK, width)
    if fast:
        ctx_parts, up_across, cots = lax.optimization_barrier((ctx_parts, up_across, cots))
        up_other = [swap(part, "ctx", 1) for part in (gate(up_quarter, ctx_parts[0]), up_across)]
    ctx_mine = ctx_parts
    if fast:
        ctx_parts = [ctx_parts[0]] + [swap(ctx_parts[r], "ctx", r) for r in (1, 2, 3)]
    else:
        ctx_parts = exchange(ctx_parts[: group // 2], jnp.stack(ctx_parts[group // 2 :]))
    if fast:
        joint_other = swap(gate(joint, ctx_mine[0]), "ctx", 1)
        parts = [w_out.reshape(2, slab, width), w_up, w_down, up_quarter, up_across, *up_other, joint, joint_other]
        plan = [(0, None, 0), (1, None, 1), (2, None, 2)] + [(3 + k, None, 1) for k in range(4)]
        theirs = 1 - f_index
        places = [2 * f_index, f_index * f_width, f_index * 2 * tall]
        for k in range(4):
            part = (core ^ (k >> 1)) * 2 + (chip ^ (k & 1))
            places.append(theirs * f_width + part * quarter)
        for k in range(2):
            plan += [(7 + k, n * width, 0 if n == 0 else 2) for n in range(1 + tall // half)]
            places.append(2 * theirs + (core ^ k))
            places += [theirs * 2 * tall + (core ^ k) * tall + n * half for n in range(tall // half)]
    else:
        out_full = jnp.concatenate(gather_fsdp(w_out), axis=0)
        out_full = jnp.pad(out_full, ((0, spare), (0, 0))).reshape(group, slab, width)
        up_parts, up_places = weight_parts(w_up, up_halves)
        down_parts, down_places = weight_parts(w_down, down_halves)
        parts, places = [out_full, *up_parts, *down_parts], [0, *up_places, *down_places]
        plan = [(0, None, 0)] + [(1 + k, None, 1) for k in range(len(up_parts))]
        plan += [(1 + len(up_parts) + k, None, 2) for k in range(len(down_parts))]
    vectors = jnp.concatenate([biases_all, gains_all])
    place = jnp.stack([member] + [jnp.int32(p) for p in places])
    done = layer(
        place,
        x_seq,
        cots,
        vectors,
        up_shift.reshape(1, -1),
        ctx_parts,
        parts,
        plan,
        fast,
    )
    pieces = group // 2 + 1
    results, d_parts, done = done[:seq_count], done[-pieces:], done[seq_count:-pieces]
    results = to_planes(results)
    back = partial(attention_backward, loc, turns, qa, ka, va, w_pieces, width)
    hidden_width = w_up.shape[1]
    used = 6 * f_width + hidden_width // n_f

    if fast:
        act_mine, pack_one, d_second, first_low, dh1, dhid_mine, dbr_mine, pack_two, small_sums = done
        piece = hidden_width // n_f // 16
        pack_one = swap(pack_one, "ctx", 1)
        pack_two = swap(pack_two, "ctx", 1)
        step = (hidden_width + width + 256) // 16
        shape = jax.ShapeDtypeStruct((2, 4, f_width, step), BF16)
        up_keep, up_send = local_call(
            up_grad_kernel,
            (shape,) * 2,
            (
                turns,
                first_low,
                dhid_mine,
                dbr_mine,
                small_sums,
                pack_two,
                *ctx_parts,
            ),
            [
                pltpu.VMEM((width, 2 * rows_here), BF16),
                pltpu.VMEM((group, slab, 2 * rows_here), BF16),
                pltpu.VMEM((2, f_width, LANES), F32),
                pltpu.VMEM(first_low.shape, BF16),
                pltpu.VMEM(dhid_mine.shape, BF16),
                pltpu.VMEM(dbr_mine.shape, BF16),
                pltpu.VMEM(pack_two.shape, BF16),
                pltpu.VMEM(shape.shape, BF16),
                pltpu.VMEM(shape.shape, BF16),
                pltpu.SemaphoreType.DMA((8,)),
            ],
            "up_grad",
            loose=(1, 2, 3, 5, 10, 11),
            limit=56,
        )
        shape = jax.ShapeDtypeStruct((2, 4, piece, width), BF16)
        down_keep, down_send = local_call(
            down_grad_kernel,
            (shape,) * 2,
            (turns, gate(act_mine, up_send), d_second, pack_one),
            [
                pltpu.VMEM(act_mine.shape, BF16),
                pltpu.VMEM(d_second.shape, BF16),
                pltpu.VMEM(pack_one.shape, BF16),
                pltpu.VMEM(shape.shape, BF16),
                pltpu.VMEM(shape.shape, BF16),
                pltpu.SemaphoreType.DMA((7,)),
            ],
            "down_grad",
            loose=range(1, 6),
        )
        d_parts = exchange(d_parts[:-1], d_parts[-1], between=up_send)
        d_parts = gate(d_parts, down_send, up_send)
        down_got, up_got = swap(down_send, "fsdp", 1), swap(up_send, "ctx", 2)
        keep, send, d_qkv = back(ctx_mine, d_parts, heads)
        down_first, down_got = reduce_square(down_keep, down_got, send, "ctx", 2)
        up_first, up_got = reduce_square(up_keep, up_got, send, "fsdp", 1)
        output = from_planes([gate(results[0], send)] + results[1:])
        keep, send, d_qkv, down_first, up_first, output = lax.optimization_barrier(
            (keep, send, d_qkv, down_first, up_first, output)
        )
        shape = jax.ShapeDtypeStruct((4, (f_width + 64) // 4, 3 * slab), BF16)
        mine, theirs = local_call(
            projection_grad_kernel,
            (shape, shape),
            (turns, x_seq, d_qkv),
            [
                pltpu.VMEM(x_seq.shape, BF16),
                pltpu.VMEM(d_qkv.shape, BF16),
                pltpu.SemaphoreType.DMA((2,)),
            ],
            "projection_grad",
            loose=(1, 2),
        )
        cores = swap(send, "ctx", 1)
    else:
        dh1, active, d_hidden, first_low, d_second, d_branch, sums, upb_grad = done
        d_parts = exchange(d_parts[:-1], d_parts[-1])
        keep, send, d_qkv = back(ctx_mine, d_parts, heads)
        output = from_planes(results)
        context_low = jnp.concatenate(to_absolute(ctx_parts, member), axis=1)[:, :width]
        grad_down = dot(active, d_second, ((0,), (0,)))
        grad_up = dot(first_low, d_hidden, ((0,), (0,)))
        grad_out = dot(context_low, d_branch, ((0,), (0,)))
        down_total = reduce_over_all(grad_down.reshape(n_f, -1, width))
        vectors = sums[:6].reshape(6, n_f, f_width).transpose(1, 0, 2).reshape(n_f, -1)
        vectors = jnp.concatenate([vectors, upb_grad.reshape(n_f, -1)], axis=1)
        extra = -(-used // f_width // LANES) * LANES
        vectors = jnp.pad(vectors, ((0, 0), (0, f_width * extra - used))).reshape(n_f, f_width, extra)
        up_out = jnp.concatenate(
            [grad_up.reshape(n_f, f_width, -1), grad_out.reshape(n_f, f_width, -1), vectors], axis=2
        )
        up_out = reduce_over_all(up_out)
        up_total = up_out[:, :hidden_width]
        out_total = up_out[:, hidden_width : hidden_width + width]
        vectors = up_out[:, hidden_width + width :].reshape(-1)
        gains_total = vectors[: 2 * f_width].reshape(2, f_width)
        biases_late = vectors[2 * f_width : 6 * f_width].reshape(4, f_width)
        up_bias_total = vectors[6 * f_width : used]

    if not fast:
        cores = swap(send, "ctx", 1)
    shape = (seq_count, positions, width)
    pieces = {2 * i: list((keep[i] + cores[i].astype(F32)).reshape(shape)) for i in range(group // 2)}
    far, close = [], []
    for bit in bits_of(group)[1:]:
        for r in [r for r in pieces if r & bit]:
            part = pieces.pop(r)
            cut = seq_count // 2
            far = jnp.stack([part[p].astype(BF16) for p in range(cut, seq_count)])
            close = jnp.stack([part[p].astype(BF16) for p in range(cut)])
            if fast:
                down_first = gate(down_first, far)
            far, close = swap(far, "ctx", bit), swap(close, "ctx", bit)
            got = [*close, *far]
            pieces[r ^ bit] = [pieces[r ^ bit][p] + got[p].astype(F32) for p in range(seq_count)]
    dh1 = dh1.reshape(shape)
    input_grad = from_planes(
        to_planes([(dh1[p] + pieces[0][p]).astype(BF16) for p in range(seq_count)])
    )

    if fast:
        got = swap(theirs, "fsdp", 1)
        down_four, down_parts = reduce_planes(sum_planes(down_first, [down_got]))
        up_four, up_parts = reduce_planes(sum_planes(gate(up_first, far), [up_got]), late=(down_four,))
        four = range(1, 5)
        down_total = local_call(
            down_final_kernel,
            (jax.ShapeDtypeStruct((hidden_width // n_f, width), F32),),
            (turns, *down_parts),
            [
                pltpu.VMEM((4, 4, piece, width), BF16),
                pltpu.VMEM((hidden_width // n_f, width), F32),
                pltpu.SemaphoreType.DMA((20,)),
            ],
            "down_final",
            loose=(*four, 5),
        )[0]
        up_total, out_total, gains_total, biases_late, up_bias_total = local_call(
            up_final_kernel,
            (
                jax.ShapeDtypeStruct((f_width, hidden_width), F32),
                jax.ShapeDtypeStruct((f_width, width), F32),
                jax.ShapeDtypeStruct((2, f_width), F32),
                jax.ShapeDtypeStruct((4, f_width), F32),
                jax.ShapeDtypeStruct((hidden_width // n_f,), F32),
            ),
            (turns, *up_parts),
            [
                pltpu.VMEM((4, 4, f_width, step), BF16),
                pltpu.VMEM((16, f_width, step), F32),
                pltpu.SemaphoreType.DMA((20,)),
            ],
            "up_final",
            loose=(*four, 5, 6),
        )
        qkv_parts = reduce_planes(
            sum_planes(gate(mine, close), [got]), last=(up_total, down_total)
        )[1]
        qkv_total, biases_total = local_call(
            qkv_final_kernel,
            (jax.ShapeDtypeStruct((f_width, 3 * width), F32), jax.ShapeDtypeStruct((6, f_width), F32)),
            (turns, biases_late, *qkv_parts),
            [
                pltpu.VMEM((4, f_width + 64, 3 * slab), BF16),
                pltpu.VMEM((4, 4, (f_width + 64) // 4, 3 * slab), BF16),
                pltpu.VMEM((f_width, 3 * width), F32),
                pltpu.VMEM((8, width), F32),
                pltpu.SemaphoreType.DMA((7,)),
            ],
            "qkv_final",
            loose=(2, 3, 4, 5, 6),
        )
    else:
        grad_qkv = dot(x_seq, d_qkv, ((0,), (0,))).reshape(n_f, f_width, 3 * slab)
        sums = jnp.sum(d_qkv.astype(F32), axis=0, keepdims=True)
        sums = jnp.pad(sums, ((0, 15), (0, 0)))
        value = jnp.concatenate([grad_qkv, jnp.broadcast_to(sums[None], (n_f,) + sums.shape)], axis=1)
        for bit in reversed(bits_of(n_f)):
            value = halve(value, "fsdp", 0, bit, f_index)
        value = value[0]
        plane_bits = [bit * group for bit in bits_of(seq_count)]
        for bit in plane_bits:
            value = halve(value, "ctx", 0, bit, c_index)
        value = value.astype(BF16)
        for bit in reversed(plane_bits):
            value = double(value, "ctx", 0, bit, c_index)
        parts = [value]
        for bit in bits_of(group):
            parts += [swap(part, "ctx", bit) for part in parts]
        parts = to_absolute(parts, member)
        qkv_total = jnp.stack([part.reshape(-1, 3, slab) for part in parts], axis=2).reshape(-1, 3, group * slab)
        qkv_total = jnp.concatenate([qkv_total[:, 2:], qkv_total[:, :2]], axis=1)[:, :, :width].astype(F32)
        early = lax.dynamic_slice_in_dim(qkv_total[f_width][0::2], f_index * f_width, f_width, 1)
        qkv_total = qkv_total[:f_width].reshape(f_width, 3 * width)
        biases_total = jnp.concatenate([early, biases_late])
    return (
        output,
        input_grad,
        qkv_total,
        out_total,
        up_total,
        down_total,
        gains_total,
        biases_total,
        up_bias_total,
    )


def solution(mesh):
    placed = (
        P("ctx", "fsdp", None),
        P("ctx", "fsdp"),
        P("fsdp", "ctx", None, None),
        P("fsdp", None),
        P("fsdp", None),
        P("fsdp", None),
        P("fsdp", None),
        P(None, "fsdp"),
        P(None, "fsdp"),
        P("fsdp"),
        P("ctx", "fsdp", None),
    )
    return jax.shard_map(
        local,
        mesh=mesh,
        in_specs=placed,
        out_specs=(
            P("ctx", "fsdp", None),
            P("ctx", "fsdp", None),
            P("fsdp", None),
            P("fsdp", None),
            P("fsdp", None),
            P("fsdp", None),
            P(None, "fsdp"),
            P(None, "fsdp"),
            P("fsdp"),
        ),
        check_vma=False,
    )
```

```python
import math
from functools import partial

import jax
import jax.numpy as jnp
from jax import lax
from jax.experimental import pallas as pl
from jax.experimental.pallas import tpu as pltpu
from jax.sharding import PartitionSpec as P

HD = 64
BLK = 64
LANES = 128
SLOTS = 8
DOCS = 32
EPSILON = 1e-06
NEGATIVE = -1e30
SCALE = HD**-0.5
RATE = SCALE / math.log(2.0)
MIB = 1024 * 1024
WEIGHT = 0

BF16 = jnp.bfloat16
F32 = jnp.float32


def dot(left, right, dims):
    return lax.dot_general(left, right, ((dims[0], dims[1]), ((), ())), preferred_element_type=F32)


def swap(value, axis, mask):
    count = lax.axis_size(axis)
    return lax.ppermute(value, axis, [(i, i ^ mask) for i in range(count)])


def gate(value, *after):
    return lax.optimization_barrier((value, *after))[0]


def bits_of(count):
    return [1 << k for k in range((count - 1).bit_length())]


def choose(index, cases):
    return cases[0] if len(cases) == 1 else lax.select_n(index, *cases)


def to_absolute(relative, index):
    count = len(relative)
    return [choose(index, [relative[k ^ i] for i in range(count)]) for k in range(count)]


def split_three(values):
    high = values.astype(BF16)
    rest = values - high.astype(F32)
    middle = rest.astype(BF16)
    return high, middle, (rest - middle.astype(F32)).astype(BF16)


def lane_ids(shape):
    return lax.broadcasted_iota(jnp.int32, shape, len(shape) - 1)


def place_three(base, values, lane, first):
    high, middle, small = split_three(values)
    base = jnp.where(lane == first, high.astype(F32), base)
    base = jnp.where(lane == first + 1, middle.astype(F32), base)
    return jnp.where(lane == first + 2, small.astype(F32), base)


def picked(ref, loc_ref, head, place):
    parts = [
        ref[head, pl.ds(pl.multiple_of(loc_ref[place + s] * BLK, BLK), BLK), :]
        for s in range(SLOTS)
    ]
    return jnp.concatenate(parts, axis=0)


def gathered(pieces, places, target, sem, first):
    copies = []
    for k, (piece, place) in enumerate(zip(pieces, places)):
        copy = pltpu.make_async_copy(piece, target.at[pl.ds(place, piece.shape[0])], sem.at[first + k])
        copy.start()
        copies.append(copy)
    return copies


def put(source, target, sem, place):
    copy = pltpu.make_async_copy(source, target, sem.at[place])
    copy.start()
    return copy


def over(value, size):
    assert size & (size - 1) == 0
    return lax.shift_right_logical(value, size.bit_length() - 1)


def within(value, size):
    assert size & (size - 1) == 0
    return value & (size - 1)


def absolute_chunk(turn, own, seqs, group):
    return (within(turn, seqs) * group + over(turn, seqs)) ^ own


def split_kernel(tail, at_ref, rows_ref, *rest):
    positions, seqs, width = rows_ref.shape
    if tail:
        line_ref, *rest = rest
    for p, ref in enumerate(rest):
        for s in range(seqs):

            @pl.when((at_ref[3] ^ p) == s)
            def _(ref=ref, s=s):
                ref[:positions, :] = rows_ref[:, s, :]
                if tail:
                    blank = jnp.zeros((tail - 1, width), F32)
                    line = line_ref[s : s + 1, :].astype(F32)
                    ref[positions:, :] = jnp.concatenate([line, blank], axis=0).astype(BF16)


def split_planes(turns, rows, line=None):
    positions, seqs, width = rows.shape
    tail = 0 if line is None else 16
    shape = jax.ShapeDtypeStruct((positions + tail, width), BF16)
    ins = (turns, rows) if line is None else (turns, rows, line)
    return local_call(partial(split_kernel, tail), (shape,) * seqs, ins, [], "split_planes")


def forward_kernel(heads, group, seqs, counts, at_ref, bias_ref, *rest):
    x_pieces, w_pieces, rest = rest[: counts[0]], rest[counts[0] : sum(counts)], rest[sum(counts) :]
    x_out, q_out, k_out, v_out, loc_ref = rest[:5]
    ctx_refs, rest = rest[5 : 5 + group], rest[5 + group :]
    x_s, q_s, k_s, v_s, w_s, seg_s, number_v, number_s, sem = rest
    chunks, tall, width = x_s.shape
    chunk, blocks = x_out.shape[1], q_s.shape[1] // BLK
    rows = chunks * chunk
    w_rows = width // counts[1]
    w_copies = gathered(
        [piece.at[pl.ds(0, w_rows)] for piece in w_pieces],
        [pl.multiple_of((at_ref[0] ^ k) * w_rows, 16) for k in range(counts[1])],
        w_s,
        sem,
        counts[0],
    )
    last = sum(counts)
    x_copies, turn = [], 0
    for piece in x_pieces:
        count = piece.shape[0]
        x_copies.append(put(piece, x_s.at[pl.ds(turn, count)], sem, last + 5 + turn))
        turn += count
    for copy in w_copies:
        copy.wait()
    for copy in x_copies:
        copy.wait()
    out_copies = [put(x_s.at[:, pl.ds(0, chunk)], x_out, sem, last)]
    tile = 2 * chunk
    lines = jnp.concatenate(
        [x_s[k, chunk:, : 2 * LANES].astype(F32)[:1] for k in range(chunks)], axis=0
    )
    number_v[...] = lines[:, LANES:].astype(jnp.int32)
    number_copy = put(number_v, number_s, sem, last + 4)
    seg_s[...] = jnp.concatenate([lines[:, :LANES], jnp.zeros((LANES - chunks, LANES), F32)], axis=0).T
    number_copy.wait()
    per = chunk // BLK
    own, member = at_ref[5], at_ref[4]

    def place_of(block):
        c = over(block, per) ^ own
        return (within(c, group) * seqs + over(c, group)) * per + within(block, per)

    def slots_of(j):
        turn, inner = over(j, per), within(j, per)
        real = absolute_chunk(turn, own, seqs, group) * per + inner
        fixed = []
        for d in (-1, 0, 1):
            near = jnp.clip(real + d, 0, blocks - 1)
            fixed.append(jnp.where(near == real + d, place_of(near), blocks))
        for b in range(2):
            fixed.append(jnp.where(jnp.abs(real - b) > 1, place_of(jnp.int32(b)), blocks))
        first = member * (LANES // group) + inner * (heads * 3)
        for h in range(heads):
            free = [place_of(number_s[turn, first + h * 3 + r]) for r in range(3)]
            for s, value in enumerate(fixed + free):
                loc_ref[(j * heads + h) * SLOTS + s] = value

    def project(i, carry):
        at = pl.ds(pl.multiple_of(i * tile, tile), tile)
        x = jnp.concatenate([x_s[2 * i, :chunk, :], x_s[2 * i + 1, :chunk, :]], axis=0)
        lane = lane_ids((tile, LANES))
        seg = []
        for k in range(2):
            mine = lane_ids((LANES, LANES)) == 2 * i + k
            seg.append(jnp.sum(jnp.where(mine, seg_s[...], 0.0), axis=1, keepdims=True))
        same = (lane - HD).astype(F32) == jnp.concatenate(seg, axis=0)
        coded = (lane >= HD) & (lane < HD + DOCS)
        ones = (lane >= HD + DOCS) & (lane < HD + DOCS + 3)
        q_extra = jnp.where(coded & same, NEGATIVE, 0.0)
        k_extra = jnp.where((coded & jnp.logical_not(same)) | ones, 1.0, 0.0)
        v_extra = jnp.where((lane >= HD) & (lane < HD + 3), 1.0, 0.0)
        head_lane = lane < HD
        y = dot(x, w_s[...], ((1,), (0,))) + bias_ref[...]
        for part, extra, ref in ((0, k_extra, k_s), (1, v_extra, v_s), (2, q_extra, q_s)):
            for h in range(heads):
                n = part * heads + h
                here = y[:, n // 2 * LANES : (n // 2 + 1) * LANES]
                if n % 2:
                    here = pltpu.roll(here, HD, 1)
                elif here.shape[1] < LANES:
                    here = jnp.concatenate([here, jnp.zeros((tile, LANES - here.shape[1]), F32)], axis=1)
                ref[h, at, :] = jnp.where(head_lane, here, extra).astype(BF16)
        for k in range(2 * per):
            slots_of(i * 2 * per + k)
        return carry

    lax.fori_loop(0, rows // tile, project, 0)
    lane = lane_ids((BLK, LANES))
    null_key = jnp.where((lane >= HD) & (lane < HD + DOCS), 1.0, 0.0).astype(BF16)
    for h in range(heads):
        k_s[h, rows : rows + BLK, :] = null_key
        v_s[h, rows : rows + BLK, :] = jnp.zeros((BLK, LANES), BF16)
    out_copies += [put(k_s, k_out, sem, last + 1), put(v_s, v_out, sem, last + 2)]
    part_blocks = rows // BLK // group
    together = 4

    for r in range(group):

        def attend(i, carry, r=r):
            units = [(u, h) for u in range(together) for h in range(heads)]
            row = [r * part_blocks + i * together + u for u in range(together)]
            at = [pl.ds(pl.multiple_of(j * BLK, BLK), BLK) for j in row]
            place = [(row[u] * heads + h) * SLOTS for u, h in units]
            q = [q_s[h, at[u], :] for u, h in units]
            scores = [
                dot(q[n], picked(k_s, loc_ref, h, place[n]), ((1,), (1,))) for n, (u, h) in enumerate(units)
            ]
            top = [jnp.max(t, axis=1, keepdims=True) for t in scores]
            prob = [jnp.exp2((t - m) * RATE).astype(BF16) for t, m in zip(scores, top)]
            mixed = [
                dot(prob[n], picked(v_s, loc_ref, h, place[n]), ((1,), (0,))) for n, (u, h) in enumerate(units)
            ]
            total = [m[:, HD : HD + 1] for m in mixed]
            done = [(m / t)[:, :HD] for m, t in zip(mixed, total)]
            level = [-(m + jnp.log2(t) * (1.0 / RATE)) for m, t in zip(top, total)]
            for n, (u, h) in enumerate(units):
                q_s[h, at[u], :] = place_three(q[n].astype(F32), level[n], lane, HD + DOCS).astype(BF16)
            for u in range(together):
                here = pl.ds(pl.multiple_of((i * together + u) * BLK, BLK), BLK)
                ctx_refs[r][here, :] = jnp.concatenate(done[u * heads : (u + 1) * heads], axis=1).astype(BF16)
            return carry

        lax.fori_loop(0, part_blocks // together, attend, 0)
    out_copies.append(put(q_s, q_out, sem, last + 3))
    for copy in out_copies:
        copy.wait()


def backward_kernel(heads, group, count, loc_ref, at_ref, q_in, k_in, v_in, *rest):
    w_pieces, rest = rest[:count], rest[count:]
    ctx_refs, grad_refs, rest = rest[:group], rest[group : 2 * group], rest[2 * group :]
    grad_refs = [ref if len(ref.shape) == 2 else ref.at[0] for ref in grad_refs]
    keep_ref, send_ref, d_out, out_ref, da_s, dq_s, w_s, keep_s, send_s, qa_ref, ka_ref, va_ref, sem, *rest = rest
    dk_even, dk_odd, dv_even, dv_odd = (rest[i * heads : (i + 1) * heads] for i in range(4))
    rows, width = qa_ref.shape[1], w_s.shape[0]
    loads = [
        put(*pair, sem, count + 2 + n)
        for n, pair in enumerate(((q_in, qa_ref), (k_in, ka_ref), (v_in, va_ref)))
    ]
    w_rows = width // count
    w_copies = gathered(
        [piece.at[pl.ds(0, w_rows)] for piece in w_pieces],
        [pl.multiple_of((at_ref[0] ^ k) * w_rows, 16) for k in range(count)],
        w_s,
        sem,
        0,
    )
    part_rows = rows // group
    tile = 128
    lane_tile = lane_ids((tile, LANES))
    blank = jnp.zeros((tile, LANES - HD), F32)

    def load(i, carry):
        at = pl.ds(pl.multiple_of(i * tile, tile), tile)
        for r in range(group):
            all_at = pl.ds(pl.multiple_of(r * part_rows + i * tile, tile), tile)
            grads = grad_refs[r][at, :].astype(F32)
            both = grads * ctx_refs[r][at, :].astype(F32)
            for h in range(heads):
                cols = slice(h * HD, (h + 1) * HD)
                delta = jnp.sum(both[:, cols], axis=1, keepdims=True)
                wide = jnp.concatenate([grads[:, cols], blank], axis=1)
                da_s[h, all_at, :] = place_three(wide, -delta, lane_tile, HD).astype(BF16)
        for b in range(rows // BLK // (part_rows // tile)):
            for ref in (*dk_even, *dk_odd, *dv_even, *dv_odd):
                ref[i * (rows // BLK // (part_rows // tile)) + b] = jnp.zeros((HD, LANES), F32)
        return carry

    lax.fori_loop(0, part_rows // tile, load, 0)
    for ref in (*dk_even, *dk_odd, *dv_even, *dv_odd):
        ref[rows // BLK] = jnp.zeros((HD, LANES), F32)
    for copy in loads:
        copy.wait()
    together = 4

    def attend(i, carry):
        units = [(u, h) for u in range(together) for h in range(heads)]
        row = [i * together + u for u in range(together)]
        at = [pl.ds(pl.multiple_of(j * BLK, BLK), BLK) for j in row]
        place = [(row[u] * heads + h) * SLOTS for u, h in units]
        q = [qa_ref[h, at[u], :] for u, h in units]
        d_mixed = [da_s[h, at[u], :] for u, h in units]
        keys = [picked(ka_ref, loc_ref, h, place[n]) for n, (u, h) in enumerate(units)]
        values = [picked(va_ref, loc_ref, h, place[n]) for n, (u, h) in enumerate(units)]
        scores = [dot(a, b, ((1,), (1,))) for a, b in zip(q, keys)]
        d_prob = [dot(a, b, ((1,), (1,))) for a, b in zip(d_mixed, values)]
        prob = [jnp.exp2(t * RATE) for t in scores]
        d_scores = [(a * b).astype(BF16) for a, b in zip(prob, d_prob)]
        prob = [t.astype(BF16) for t in prob]
        d_q = [dot(a, b, ((1,), (0,))) for a, b in zip(d_scores, keys)]
        q_turned = [t.T[:HD] for t in q]
        d_turned = [t.T[:HD] for t in d_mixed]
        d_keys = [dot(a, b, ((1,), (0,))) for a, b in zip(q_turned, d_scores)]
        d_values = [dot(a, b, ((1,), (0,))) for a, b in zip(d_turned, prob)]
        for n, (u, h) in enumerate(units):
            dq_s[h, at[u], :] = (d_q[n] * SCALE).astype(BF16)
        for u in range(together):
            for s in range(SLOTS):
                for h in range(heads):
                    n = u * heads + h
                    to = loc_ref[place[n] + s]
                    cols = slice((s // 2) * LANES, (s // 2 + 1) * LANES)
                    dk_ref, dv_ref = (dk_odd[h], dv_odd[h]) if s % 2 else (dk_even[h], dv_even[h])
                    dk_ref[to] += d_keys[n][:, cols]
                    dv_ref[to] += d_values[n][:, cols]
        return carry

    lax.fori_loop(0, rows // BLK // together, attend, 0)
    low_lane = lane_ids((HD, LANES)) < BLK

    def finish(i, carry):
        at = [pl.ds(pl.multiple_of((2 * i + u) * BLK, BLK), BLK) for u in range(2)]
        turned = []
        for even, odd, factor in ((dk_even, dk_odd, SCALE), (dv_even, dv_odd, 1.0)):
            for h in range(heads):
                first = even[h][2 * i] + pltpu.roll(odd[h][2 * i], BLK, 1)
                second = pltpu.roll(even[h][2 * i + 1], BLK, 1) + odd[h][2 * i + 1]
                turned.append(jnp.where(low_lane, first, second) * factor)
        pair = pl.ds(pl.multiple_of(2 * i * BLK, 2 * BLK), 2 * BLK)
        for n in range(heads):
            both = jnp.concatenate([turned[2 * n], turned[2 * n + 1]], axis=0)
            out_ref[pair, n * LANES : (n + 1) * LANES] = both.astype(BF16).T
        done = [dq_s[h, pair, :][:, :HD].astype(F32) for h in range(heads)]
        out_ref[pair, heads * LANES :] = jnp.concatenate(done, axis=1).astype(BF16)
        return carry

    lax.fori_loop(0, rows // BLK // 2, finish, 0)
    out_copies = [put(out_ref, d_out, sem, count + 5)]
    for copy in w_copies:
        copy.wait()
    for odd, hold, ref in ((1, send_s, send_ref), (0, keep_s, keep_ref)):

        def to_rows(i, carry, odd=odd, hold=hold):
            at = pl.ds(pl.multiple_of((2 * i + odd) * part_rows, BLK), part_rows)
            hold[i] = dot(out_ref[at, :], w_s[...], ((1,), (1,))).astype(hold.dtype)
            return carry

        lax.fori_loop(0, group // 2, to_rows, 0)
        out_copies.append(put(hold, ref, sem, count + odd))
    for copy in out_copies:
        copy.wait()


def projection_grad_kernel(at_ref, x_in, d_in, mine_ref, theirs_ref, x_s, d_s, sem):
    copies = [put(x_in, x_s, sem, 0), put(d_in, d_s, sem, 1)]
    half = x_s.shape[1] // 2
    copies[1].wait()
    sums = row_sum(d_s[...].astype(F32))
    shape = (64, sums.shape[1])
    tail = jnp.where(lax.broadcasted_iota(jnp.int32, shape, 0) == 0, jnp.broadcast_to(sums, shape), 0.0)
    copies[0].wait()
    for k, ref in ((1, theirs_ref), (0, mine_ref)):
        cols = pl.ds(pl.multiple_of((at_ref[0] ^ k) * half, LANES), half)
        grad = jnp.concatenate([dot(x_s[:, cols], d_s[...], ((0,), (0,))), tail], axis=0).astype(BF16)
        size = grad.shape[0] // 4
        for z in range(4):
            ref[plane_spot(z, at_ref[3])] = grad[z * size : (z + 1) * size]


def cost(microseconds):
    return pl.CostEstimate(flops=int(microseconds * WEIGHT), bytes_accessed=0, transcendentals=0)


def whole(memory):
    return pl.BlockSpec(memory_space=memory)


def pieces_of(group, rows, columns):
    half = group // 2
    near = jax.ShapeDtypeStruct((rows, columns), BF16)
    return (near,) * half + (jax.ShapeDtypeStruct((half, rows, columns), BF16),)


def attention_forward(turns, x_pieces, w_pieces, bias, heads, group, seqs, positions):
    chunks, width = group * seqs, x_pieces[0].shape[2]
    rows = positions * chunks
    counts = (len(x_pieces), len(w_pieces))
    kept = jax.ShapeDtypeStruct((heads, rows + BLK, LANES), BF16)
    return pl.pallas_call(
        partial(forward_kernel, heads, group, seqs, counts),
        out_shape=(
            jax.ShapeDtypeStruct((chunks, positions, width), BF16),
            jax.ShapeDtypeStruct((heads, rows, LANES), BF16),
            kept,
            kept,
            jax.ShapeDtypeStruct((rows // BLK * heads * SLOTS,), jnp.int32),
        )
        + (jax.ShapeDtypeStruct((rows // group, heads * HD), BF16),) * group,
        in_specs=[whole(pltpu.SMEM), whole(pltpu.VMEM)] + [whole(pl.ANY)] * sum(counts),
        out_specs=(whole(pl.ANY),) * 4 + (whole(pltpu.SMEM),) + (whole(pltpu.VMEM),) * group,
        scratch_shapes=[
            pltpu.VMEM((chunks, positions + 16, width), BF16),
            pltpu.VMEM((heads, rows, LANES), BF16),
            pltpu.VMEM((heads, rows + BLK, LANES), BF16),
            pltpu.VMEM((heads, rows + BLK, LANES), BF16),
            pltpu.VMEM((width, 3 * heads * HD), BF16),
            pltpu.VMEM((LANES, LANES), F32),
            pltpu.VMEM((chunks, LANES), jnp.int32),
            pltpu.SMEM((chunks, LANES), jnp.int32),
            pltpu.SemaphoreType.DMA((sum(counts) + 5 + chunks,)),
        ],
        compiler_params=pltpu.CompilerParams(vmem_limit_bytes=56 * MIB),
        cost_estimate=cost(19),
        name="attention_forward",
    )(turns, bias, *x_pieces, *w_pieces)


def attention_backward(loc, turns, qa, ka, va, w_pieces, width, ctx_parts, grads, heads):
    rows = qa.shape[1]
    blocks, group, count, slab = rows // BLK, len(grads), len(w_pieces), heads * HD
    part = (group // 2, rows // group, width)
    outs = (
        jax.ShapeDtypeStruct(part, F32),
        jax.ShapeDtypeStruct(part, BF16),
        jax.ShapeDtypeStruct((rows, 3 * slab), BF16),
    )
    return pl.pallas_call(
        partial(backward_kernel, heads, group, count),
        out_shape=outs,
        in_specs=[whole(pltpu.SMEM)] * 2
        + [whole(pl.ANY)] * (3 + count)
        + [whole(pltpu.VMEM)] * (2 * group),
        out_specs=(whole(pl.ANY),) * 3,
        scratch_shapes=[
            pltpu.VMEM((rows, 3 * slab), BF16),
            pltpu.VMEM((heads, rows, LANES), BF16),
            pltpu.VMEM((heads, rows, LANES), BF16),
            pltpu.VMEM((width, 3 * slab), BF16),
            pltpu.VMEM(part, F32),
            pltpu.VMEM(part, BF16),
            pltpu.VMEM(qa.shape, BF16),
            pltpu.VMEM(ka.shape, BF16),
            pltpu.VMEM(va.shape, BF16),
            pltpu.SemaphoreType.DMA((count + 6,)),
        ]
        + [pltpu.VMEM((blocks + 1, HD, LANES), F32)] * (4 * heads),
        compiler_params=pltpu.CompilerParams(vmem_limit_bytes=56 * MIB),
        cost_estimate=cost(50),
        name="attention_backward",
    )(loc, turns, qa, ka, va, *w_pieces, *ctx_parts, *grads)


def norm_values(values):
    average = jnp.mean(values, axis=-1, keepdims=True)
    centred = values - average
    inv_std = lax.rsqrt(jnp.mean(centred * centred, axis=-1, keepdims=True) + EPSILON)
    return centred * inv_std, inv_std


def norm_pull(upstream, scaled, inv_std, gain_row):
    weighted = upstream * gain_row
    centre_term = jnp.mean(weighted, axis=-1, keepdims=True)
    slope_term = jnp.mean(weighted * scaled, axis=-1, keepdims=True)
    return inv_std * (weighted - centre_term - scaled * slope_term)


def gelu_pair(v):
    rate = math.sqrt(2.0 / math.pi)
    square = v * v
    t = jnp.tanh(rate * v * (1.0 + 0.044715 * square))
    half = 0.5 * (1.0 + t)
    slope = half + (0.5 * rate) * v * (1.0 - t * t) * (1.0 + (3.0 * 0.044715) * square)
    return v * half, slope


def row_sum(values):
    return jnp.sum(values, axis=0, keepdims=True)


def layer_kernel(group, count, plan, seqs, fast, at_ref, x_ref, vec_ref, upb_ref, *rest):
    ctx_refs = rest[:group]
    arrays, rest = rest[group : group + count], rest[group + count :]
    cot_refs, result_refs, rest = rest[:seqs], rest[seqs : 2 * seqs], rest[2 * seqs :]
    if fast:
        early, (dh1_ref, dhid_mine, dbr_mine, pack_two, small_ref) = rest[:4], rest[4:9]
        rest = rest[9:]
        slab = ctx_refs[0].shape[1]
    else:
        dh1_ref, active_ref, dhid_ref, first_low_ref, dsec_ref, dbr_ref, sums_out, upb_out = rest[:8]
        rest = rest[8:]
    near, far, rest = rest[: group // 2], rest[group // 2], rest[group // 2 + 1 :]
    dctx_refs = [*near, *[far.at[r] for r in range(group // 2)]]
    out_s, up_s, down_s, slope_s, scaled_s, inv_s, acc_s, cot_s, result_s, x_s, dbr_s, sums_s, upb_s, sem = rest[:14]
    if fast:
        act_mine, pack_one, dsec_ref, first_low_ref = rest[14:]
    rows, width = acc_s.shape
    hidden = up_s.shape[1]
    member = at_ref[0]
    core = member & 1
    copies = []
    for k, (array, column, w) in enumerate(plan):
        scratch, source = (out_s, up_s, down_s)[w], arrays[array]
        if column is not None:
            source = source.at[:, pl.ds(column, scratch.shape[-1])]
        start = pl.multiple_of(at_ref[1 + k], 1 if w == 0 else 16)
        one = w == 0 and len(source.shape) == 2
        copies.append(put(source, scratch.at[start] if one else scratch.at[pl.ds(start, source.shape[0])], sem, k))
    k = len(plan)
    part_rows = rows // seqs
    starts = [p * part_rows for p in range(seqs)]
    cot_copies = gathered(cot_refs, starts, cot_s, sem, k)
    x_copy = put(x_ref.at[pl.ds(0, rows)], x_s, sem, k + 2 * seqs)
    b_out, b_first, b_last, b_second = (vec_ref[i : i + 1, :] for i in (2, 3, 4, 5))
    gain_one, gain_two = vec_ref[6:7, :], vec_ref[7:8, :]
    tile = min(256, rows)
    sums_s[...] = jnp.zeros_like(sums_s)

    for copy in [x_copy] + [copy for copy, (_, _, w) in zip(copies, plan) if w == 0]:
        copy.wait()

    def first_norm(i, carry):
        at = pl.ds(pl.multiple_of(i * tile, tile), tile)
        total = x_s[at, :].astype(F32) + b_out
        for r in range(group):
            total = total + dot(ctx_refs[r][at, :], out_s[member ^ r], ((1,), (0,)))
        scaled, inv_std = norm_values(total)
        first = scaled * gain_one + b_first
        scaled_s[at, :] = scaled
        inv_s[at, :] = jnp.broadcast_to(inv_std, (tile, LANES))
        first_low_ref[at, :] = first.astype(BF16)
        acc_s[at, :] = first + b_second
        return carry

    lax.fori_loop(0, rows // tile, first_norm, 0)
    for copy in [copy for copy, (_, _, w) in zip(copies, plan) if w > 0]:
        copy.wait()

    def up_down(start, step, ref, to):
        at = pl.ds(pl.multiple_of(start, step), step)
        v = dot(first_low_ref[...], up_s[:, at], ((1,), (0,))) + upb_ref[:, at]
        active, slope = gelu_pair(v)
        active = active.astype(BF16)
        ref[:, pl.ds(pl.multiple_of(to, step), step)] = active
        slope_s[:, at] = slope
        acc_s[...] += dot(active, down_s[at, :], ((1,), (0,)))

    def down_up(start, step, ref, to):
        at = pl.ds(pl.multiple_of(start, step), step)
        d_hidden = dot(dsec_ref[...], down_s[at, :], ((1,), (1,))) * slope_s[:, at]
        low = d_hidden.astype(BF16)
        ref[:rows, pl.ds(pl.multiple_of(to, step), step)] = low
        upb_s[:, at] = row_sum(low.astype(F32))
        acc_s[...] += dot(low, up_s[:, at], ((1,), (1,)))

    def over_hidden(one, refs):
        if fast:
            step = hidden // 4
            for c, ref in enumerate(refs):

                def part(i, carry, c=c, ref=ref):
                    turn = c ^ core
                    one((i * 2 + turn if one is up_down else turn * 2 + i) * step, step, ref, i * step)
                    return carry

                for i in range(2):
                    part(i, 0)
        else:
            step = 512

            def part(i, carry):
                one(i * step, step, refs[0], i * step)
                return carry

            lax.fori_loop(0, hidden // step, part, 0)

    over_hidden(up_down, (act_mine, pack_one) if fast else (active_ref,))
    for copy in cot_copies:
        copy.wait()

    def last_norm(i, carry):
        at = pl.ds(pl.multiple_of(i * tile, tile), tile)
        scaled, inv_std = norm_values(acc_s[at, :])
        result_s[at, :] = (scaled * gain_two + b_last).astype(BF16)
        upstream = cot_s[at, :].astype(F32)
        pulled = norm_pull(upstream, scaled, inv_std, gain_two)
        acc_s[at, :] = pulled
        low = pulled.astype(BF16)
        dsec_ref[at, :] = low
        if fast:
            pack_one[at, hidden // 2 :] = low
        sums_s[1:2, :] += row_sum(upstream * scaled)
        sums_s[4:5, :] += row_sum(upstream)
        sums_s[5:6, :] += row_sum(pulled)
        return carry

    lax.fori_loop(0, rows // tile, last_norm, 0)
    early_copies = []
    if fast:
        held = (act_mine, pack_one, dsec_ref, first_low_ref)
        early_copies = [put(a, b, sem, k + 2 * seqs + 1 + n) for n, (a, b) in enumerate(zip(held, early))]
    result_copies = [
        put(result_s.at[pl.ds(starts[p], part_rows)], result_refs[p], sem, k + seqs + p) for p in range(seqs)
    ]
    over_hidden(down_up, (dhid_mine, pack_two) if fast else (dhid_ref,))

    def first_back(i, carry):
        at = pl.ds(pl.multiple_of(i * tile, tile), tile)
        upstream, scaled = acc_s[at, :], scaled_s[at, :]
        pulled = norm_pull(upstream, scaled, inv_s[at, :1], gain_one)
        dh1_ref[at, :] = pulled
        low = pulled.astype(BF16)
        dbr_s[at, :] = low
        sums_s[0:1, :] += row_sum(upstream * scaled)
        sums_s[2:3, :] += row_sum(pulled)
        sums_s[3:4, :] += row_sum(upstream)
        for r in range(group):
            dctx_refs[r][at, :] = dot(low, out_s[member ^ r], ((1,), (1,))).astype(BF16)
        return carry

    lax.fori_loop(0, rows // tile, first_back, 0)
    if fast:
        half, wide = width // 2, hidden // 2
        dbr_mine[...] = dbr_s[:, pl.ds(pl.multiple_of(core * half, LANES), half)]
        pack_two[:rows, wide : wide + half] = dbr_s[:, pl.ds(pl.multiple_of((1 - core) * half, LANES), half)]
        pack_two[:rows, wide + half : wide + half + width] = first_low_ref[...]
        pack_two[:rows, wide + half + width :] = jnp.concatenate([ref[...] for ref in ctx_refs], axis=1)
        long = [upb_s[:, i * width : (i + 1) * width] for i in range(hidden // width)]
        blank = jnp.zeros((8 - len(long), width), F32)
        small = jnp.concatenate([sums_s[...], *long, blank], axis=0).astype(BF16)
        small_ref[...] = small
        pack_two[rows:, :width] = small
        pack_two[rows:, width:] = jnp.zeros((16, pack_two.shape[1] - width), BF16)
    else:
        dbr_ref[...] = dbr_s[...]
        sums_out[...] = sums_s[...]
        upb_out[...] = upb_s[...]
    for copy in result_copies + early_copies:
        copy.wait()


def layer(place, x_seq, cots, vectors, up_shift, ctx_parts, parts, plan, fast):
    rows, width = len(cots) * cots[0].shape[0], x_seq.shape[1]
    group, slab = len(ctx_parts), ctx_parts[0].shape[1]
    hidden = up_shift.shape[1]

    def like(columns, dtype=BF16, count=rows):
        return jax.ShapeDtypeStruct((count, columns), dtype)

    half, wide = width // 2, hidden // 2
    if fast:
        held = (like(wide), like(wide + width), like(width), like(width))
        outs = held + (like(width, F32), like(wide), like(half))
        outs += (like(wide + half + 2 * width, BF16, rows + 16), like(width, BF16, 16))
    else:
        held = ()
        outs = (like(width, F32), like(hidden), like(hidden), like(width), like(width), like(width))
        outs += (like(width, F32, 8), like(hidden, F32, 1))
    outs = (jax.ShapeDtypeStruct(cots[0].shape, BF16),) * len(cots) + outs + pieces_of(group, rows, slab)
    return pl.pallas_call(
        partial(layer_kernel, group, len(parts), plan, len(cots), fast),
        out_shape=outs,
        in_specs=[whole(pltpu.SMEM), whole(pl.ANY)]
        + [whole(pltpu.VMEM)] * (2 + group)
        + [whole(pl.ANY)] * (len(parts) + len(cots)),
        out_specs=(whole(pl.ANY),) * (len(cots) + len(held))
        + (whole(pltpu.VMEM),) * (len(outs) - len(cots) - len(held)),
        scratch_shapes=[
            pltpu.VMEM((group, slab, width), BF16),
            pltpu.VMEM((width, hidden), BF16),
            pltpu.VMEM((hidden, width), BF16),
            pltpu.VMEM((rows, hidden), F32),
            pltpu.VMEM((rows, width), F32),
            pltpu.VMEM((rows, LANES), F32),
            pltpu.VMEM((rows, width), F32),
            pltpu.VMEM((rows, width), BF16),
            pltpu.VMEM((rows, width), BF16),
            pltpu.VMEM((rows, width), BF16),
            pltpu.VMEM((rows, width), BF16),
            pltpu.VMEM((8, width), F32),
            pltpu.VMEM((1, hidden), F32),
            pltpu.SemaphoreType.DMA((len(plan) + 2 * len(cots) + 1 + len(held),)),
        ]
        + [pltpu.VMEM(one.shape, BF16) for one in held],
        compiler_params=pltpu.CompilerParams(vmem_limit_bytes=56 * MIB),
        cost_estimate=cost(29),
        name="feed_forward",
    )(place, x_seq, vectors, up_shift, *ctx_parts, *parts, *cots)


def plane_spot(z, own):
    turn = z ^ own
    return (turn & 1) * 2 + (turn >> 1)


def down_grad_kernel(at_ref, act_in, d_in, got_in, keep_ref, send_ref, act_ref, d_ref, got_ref, keep_s, send_s, sem):
    piece = keep_s.shape[2]
    chunk = 4 * piece
    wide = act_ref.shape[1]
    ins = [put(*pair, sem, k) for k, pair in enumerate(((d_in, d_ref), (act_in, act_ref), (got_in, got_ref)))]
    for copy in ins:
        copy.wait()
    outs = []
    for f, hold, ref in ((1, send_s, send_ref), (0, keep_s, keep_ref)):
        for x in range(2):
            t = (f ^ at_ref[0]) * 2 + (x ^ at_ref[2])
            at = pl.ds(pl.multiple_of(t * chunk, LANES), chunk)
            grad = dot(act_ref[:, at], d_ref[...], ((0,), (0,)))
            grad = (grad + dot(got_ref[:, at], got_ref[:, wide:], ((0,), (0,)))).astype(BF16)
            for z in range(4):
                hold[x, plane_spot(z, at_ref[3])] = grad[z * piece : (z + 1) * piece]
            outs.append(put(hold.at[x], ref.at[x], sem, 3 + 2 * f + x))
    for copy in outs:
        copy.wait()


def up_grad_kernel(at_ref, first_in, dhid_in, dbr_in, small_ref, got_in, *rest):
    ctx_refs, (keep_ref, send_ref), rest = rest[:4], rest[4:6], rest[6:]
    first_s, ctx_s, extra_s, first_ref, dhid_ref, dbr_ref, got_ref, keep_s, send_s, sem = rest
    half, step = keep_s.shape[2:]
    rows, width = first_ref.shape
    slab = ctx_refs[0].shape[1]
    wide, narrow = dhid_ref.shape[1], dbr_ref.shape[1]
    ins = [put(first_in, first_ref, sem, 0)]
    cuts = (wide + narrow, wide + narrow + width, wide + narrow + 2 * width)
    for k, (a, b) in enumerate(((cuts[0], cuts[1]), (cuts[1], cuts[2]), (0, cuts[0]))):
        ins.append(put(got_in.at[:, pl.ds(a, b - a)], got_ref.at[:, pl.ds(a, b - a)], sem, 1 + k))
    ins += [put(dhid_in, dhid_ref, sem, 4), put(dbr_in, dbr_ref, sem, 5)]
    for copy in ins[:3]:
        copy.wait()
    first_s[:, :rows] = first_ref[...].T
    first_s[:, rows:] = got_ref[:rows, wide + narrow : wide + narrow + width].T
    got_ctx = got_ref[:rows, wide + narrow + width :].T
    for r in range(4):
        ctx_s[at_ref[4] ^ r, :, :rows] = ctx_refs[r][...].T
        ctx_s[at_ref[4] ^ r ^ 1, :, rows:] = got_ctx[r * slab : (r + 1) * slab]
    ups = wide // step
    for copy in ins[3:]:
        copy.wait()
    extra_s[...] = jnp.zeros_like(extra_s)
    vectors = small_ref[...].astype(F32) + got_ref[rows:, :width].astype(F32)
    for f in range(2):
        for i in range(6):
            for k in range(half // LANES):
                start = f * half + k * LANES
                extra_s[f, i * (half // LANES) + k : i * (half // LANES) + k + 1, :] = vectors[
                    i : i + 1, start : start + LANES
                ]
        row = 6 * (half // LANES)
        for k in range(wide // LANES):
            start = f * wide + k * LANES
            extra_s[f, row + k : row + k + 1, :] = vectors[
                8 + start // width : 9 + start // width, start % width : start % width + LANES
            ]
    outs = []
    for x, ref, out in ((1, send_s, send_ref), (0, keep_s, keep_ref)):

        def one(i, carry, x=x, ref=ref):
            spot = (i & 1) * 2 + (i >> 1)
            k = (x ^ at_ref[2]) * 4 + (i ^ at_ref[3])

            def store(grad):
                for f in range(2):
                    ref[f ^ at_ref[0], spot] = grad[f * half : (f + 1) * half].astype(BF16)

            def out_grad(lanes):
                turned = ctx_s[...].reshape(width, 2 * rows)
                right = jnp.concatenate([dbr_ref[:, lanes], got_ref[:rows, wide + lanes.start : wide + lanes.stop]], axis=0)
                return dot(turned, right, ((1,), (0,)))

            @pl.when(k < ups)
            def _():
                at = pl.ds(pl.multiple_of(k * step, step), step)
                right = jnp.concatenate([dhid_ref[:, at], got_ref[:rows, at]], axis=0)
                store(dot(first_s[...], right, ((1,), (0,))))

            @pl.when(k == ups)
            def _():
                store(out_grad(slice(0, step)))

            @pl.when(k > ups)
            def _():
                extra = extra_s[...].reshape(width, LANES)
                store(jnp.concatenate([out_grad(slice(step, narrow)), extra], axis=1))

            return carry

        lax.fori_loop(0, 4, one, 0)
        outs.append(put(ref, out, sem, 6 + x))
    for copy in outs:
        copy.wait()


def down_final_kernel(at_ref, *rest):
    parts, (out_ref, in_s, out_s, sem) = rest[:4], rest[4:]
    piece = parts[0].shape[1]
    copies_in = [put(part, in_s.at[i], sem, i) for i, part in enumerate(parts)]
    copies = []
    for i in range(4):
        copies_in[i].wait()
        for z in range(4):
            k = (((i & 1) ^ at_ref[1]) * 2 + ((i >> 1) ^ at_ref[2])) * 4 + (z ^ at_ref[3])
            at = pl.ds(pl.multiple_of(k * piece, 16), piece)
            out_s[at, :] = in_s[i, (z & 1) * 2 + (z >> 1)].astype(F32)
            copies.append(put(out_s.at[at], out_ref.at[at], sem, 4 + i * 4 + z))
    for copy in copies:
        copy.wait()


def up_final_kernel(at_ref, *rest):
    parts, (up_ref, out_ref, gains_ref, biases_ref, upb_ref, in_s, out_s, sem) = rest[:4], rest[4:]
    step = parts[0].shape[2]
    wide, narrow = up_ref.shape[1] // 2, out_ref.shape[1] // 2
    ups = wide // step
    half = gains_ref.shape[1]
    count = half // LANES
    copies_in = [put(part, in_s.at[i], sem, i) for i, part in enumerate(parts)]

    def each(i, z, act):
        core = (i & 1) ^ at_ref[1]
        k = ((i >> 1) ^ at_ref[2]) * 4 + (z ^ at_ref[3])
        n = i * 4 + z

        @pl.when(k < ups)
        def _():
            at = pl.ds(pl.multiple_of(core * wide + k * step, LANES), step)
            act(pltpu.make_async_copy(out_s.at[n], up_ref.at[:, at], sem.at[4 + n]))

        @pl.when(k == ups)
        def _():
            at = pl.ds(pl.multiple_of(core * narrow, LANES), step)
            act(pltpu.make_async_copy(out_s.at[n], out_ref.at[:, at], sem.at[4 + n]))

        @pl.when(k > ups)
        def _():
            at = pl.ds(pl.multiple_of(core * narrow + step, LANES), LANES)
            act(pltpu.make_async_copy(out_s.at[n, :, pl.ds(0, LANES)], out_ref.at[:, at], sem.at[4 + n]))

        return core, k

    for i in range(4):
        copies_in[i].wait()
        for z in range(4):
            value = in_s[i, (z & 1) * 2 + (z >> 1)].astype(F32)
            out_s[i * 4 + z] = value
            core, k = each(i, z, lambda copy: copy.start())

            @pl.when((k > ups) & (core == 0))
            def _(value=value):
                extra = value[:, LANES:]
                for a in range(6):
                    for b in range(count):
                        row = extra[a * count + b : a * count + b + 1]
                        lanes = slice(b * LANES, (b + 1) * LANES)
                        if a < 2:
                            gains_ref[a : a + 1, lanes] = row
                        else:
                            biases_ref[a - 2 : a - 1, lanes] = row
                for b in range(upb_ref.shape[0] // LANES):
                    upb_ref[b * LANES : (b + 1) * LANES] = extra[6 * count + b]

    for i in range(4):
        for z in range(4):
            each(i, z, lambda copy: copy.wait())


def qkv_final_kernel(at_ref, late_ref, *rest):
    parts, (out_ref, biases_ref, hold, in_s, out_s, sums_s, sem) = rest[:4], rest[4:]
    half, slab = out_s.shape[0], hold.shape[2] // 3
    width = 4 * slab
    size = parts[0].shape[1]
    copies = [put(part, in_s.at[i], sem, i) for i, part in enumerate(parts)]
    for r in range(4):
        copies[r].wait()
        for z in range(4):
            at = pl.ds(pl.multiple_of((z ^ at_ref[3]) * size, 16), size)
            hold[at_ref[4] ^ r, at, :] = in_s[r, (z & 1) * 2 + (z >> 1)]
    outs = []
    for k, column in ((0, 1), (1, 2), (2, 0)):
        for m in range(4):
            cols = slice(column * width + m * slab, column * width + (m + 1) * slab)
            out_s[:, cols] = hold[m, :half, k * slab : (k + 1) * slab].astype(F32)
        at = pl.ds(column * width, width)
        outs.append(put(out_s.at[:, at], out_ref.at[:, at], sem, 4 + k))
    for k, row in ((2, 0), (1, 1)):
        sums = [hold[m, half : half + 16, k * slab : (k + 1) * slab].astype(F32)[:1] for m in range(4)]
        sums_s[row : row + 1, :] = jnp.concatenate(sums, axis=1)
    biases_ref[0:2, :] = sums_s[0:2, pl.ds(pl.multiple_of(at_ref[0] * half, LANES), half)]
    biases_ref[2:6, :] = late_ref[...]
    for copy in outs:
        copy.wait()


def local_call(kernel, outs, ins, scratch, name, time=3, loose=(), limit=28):
    return pl.pallas_call(
        kernel,
        out_shape=outs,
        in_specs=[whole(pltpu.SMEM)]
        + [whole(pl.ANY if i in loose else pltpu.VMEM) for i in range(1, len(ins))],
        out_specs=tuple(whole(pl.ANY if len(ins) + i in loose else pltpu.VMEM) for i in range(len(outs))),
        scratch_shapes=scratch,
        compiler_params=pltpu.CompilerParams(vmem_limit_bytes=limit * MIB),
        cost_estimate=cost(time),
        name=name,
    )(*ins)


def swap_joint(value, f_mask, c_mask):
    n_f, n_c = lax.axis_size("fsdp"), lax.axis_size("ctx")
    pairs = [(f * n_c + c, (f ^ f_mask) * n_c + (c ^ c_mask)) for f in range(n_f) for c in range(n_c)]
    return lax.ppermute(value, ("fsdp", "ctx"), pairs)


def sum_planes(own, others):
    total = own.astype(F32)
    for other in others:
        total = total + other.astype(F32)
    return total.astype(BF16)


def reduce_square(keep, got, after, axis, mask):
    first, second = sum_planes(gate(keep[0], after), [got[0]]), sum_planes(keep[1], [got[1]])
    return first, swap(second, axis, mask)


def reduce_planes(mine, late=(), last=()):
    two = sum_planes(mine[:2], [swap(mine[2:], "ctx", 4)])
    piece = gate(sum_planes(two[0], [swap(two[1], "ctx", 8)]), *late)
    four = jnp.stack([piece] + [swap(piece, "ctx", mask) for mask in (8, 4, 12)])
    across = swap(four, "ctx", 2)
    return four, [four, swap(four, "ctx", 1), across, swap(gate(across, *last), "ctx", 1)]


def exchange(near, far, between=None):
    half = len(near)
    got = swap(far, "ctx", half)
    if between is not None:
        got = gate(got, between)
    items = {(d, 0): near[d] for d in range(half)}
    items.update({(d, half): got[d] for d in range(half)})
    if between is not None:
        items[0, half] = got
    for bit in reversed(bits_of(half)):
        for d, source in [key for key in items if key[0] & bit]:
            items[d ^ bit, source ^ bit] = swap(items.pop((d, source)), "ctx", bit)
    return [items[0, source] for source in range(2 * half)]


def gather_fsdp(value):
    index = lax.axis_index("fsdp")
    parts = [value]
    for bit in bits_of(lax.axis_size("fsdp")):
        parts += [swap(part, "fsdp", bit) for part in parts]
    return to_absolute(parts, index)


def fetch_halves(value):
    half = value.shape[0] // 2
    parts = [lax.dynamic_slice_in_dim(value, (lax.axis_index("ctx") & 1) * half, half, 0)]
    for bit in bits_of(lax.axis_size("fsdp")):
        parts += [swap(part, "fsdp", bit) for part in parts]
    return parts[1:]


def weight_parts(value, halves):
    index = lax.axis_index("fsdp")
    core = lax.axis_index("ctx") & 1
    size = value.shape[0]
    half = size // 2
    pieces, places = [value], [index * size]
    for k, part in enumerate(halves, 1):
        pieces += [part, swap(part, "ctx", 1)]
        first = (index ^ k) * size
        places += [first + core * half, first + (1 - core) * half]
    return pieces, places


def halve(value, axis, dim, mask, index):
    half = value.shape[dim] // 2
    bit = (index // mask) & 1
    mine = lax.dynamic_slice_in_dim(value, bit * half, half, dim)
    theirs = lax.dynamic_slice_in_dim(value, (1 - bit) * half, half, dim)
    return mine + swap(theirs.astype(BF16), axis, mask).astype(F32)


def double(value, axis, dim, mask, index):
    bit = (index // mask) & 1
    other = swap(value, axis, mask)
    return lax.select_n(
        bit,
        jnp.concatenate([value, other], axis=dim),
        jnp.concatenate([other, value], axis=dim),
    )


def reduce_over_all(value):
    f_index, c_index = lax.axis_index("fsdp"), lax.axis_index("ctx")
    value = halve(value, "ctx", 1, 1, c_index)
    for bit in reversed(bits_of(lax.axis_size("fsdp"))):
        value = halve(value, "fsdp", 0, bit, f_index)
    value = value[0]
    rest = bits_of(lax.axis_size("ctx"))[1:]
    for bit in rest:
        value = halve(value, "ctx", 0, bit, c_index)
    value = value.astype(BF16)
    for bit in reversed(rest):
        value = double(value, "ctx", 0, bit, c_index)
    return double(value, "ctx", 0, 1, c_index).astype(F32)


def local(
    tokens, segments, rand_blocks, w_qkv, w_out, w_up, w_down, ln_gains, biases, up_bias, cotangent
):
    positions, seq_count, width = tokens.shape
    n_f, n_c = lax.axis_size("fsdp"), lax.axis_size("ctx")
    f_index, c_index = lax.axis_index("fsdp"), lax.axis_index("ctx")
    group = n_c // seq_count
    plane, member = c_index // group, c_index % group
    head_count = width // HD
    heads = -(-head_count // group)
    per_chunk = positions // BLK
    blocks = per_chunk * n_c
    rows_here = seq_count * positions
    f_width = width // n_f
    slab = heads * HD
    spare = group * slab - width

    def to_planes(parts):
        return [swap(part, "ctx", p * group) if p else part for p, part in enumerate(parts)]

    def from_planes(parts):
        return jnp.stack(to_absolute(parts, plane), axis=1)

    fast = n_f == 2 and group == 4 and seq_count == 4 and not spare and f_width % slab == 0
    turns = jnp.stack([f_index, member & 1, (member >> 1) & 1, plane, member, c_index])
    rand = jnp.pad(rand_blocks, ((0, 0), (0, 0), (0, group * heads - head_count), (0, 0)))
    rand = rand.reshape(seq_count, per_chunk, group, heads, -1).transpose(0, 2, 1, 3, 4)
    rand = rand.reshape(seq_count, group, -1)
    rand = jnp.pad(rand, ((0, 0), (0, 0), (0, LANES // group - rand.shape[2])))
    line = jnp.concatenate([segments.T, rand.reshape(seq_count, LANES)], axis=1).astype(BF16)
    line = jnp.pad(line, ((0, 0), (0, width - line.shape[1])))
    token_parts = split_planes(turns, tokens, line)
    w_qkv, small_in = lax.optimization_barrier(((w_qkv, (ln_gains, biases, up_bias)), *token_parts))[0]
    ln_gains, biases, up_bias = small_in
    x_rows = to_planes(token_parts)
    if fast:
        across = [swap(part, "ctx", 2) for part in x_rows]
        x_pieces = [*x_rows, swap(jnp.concatenate(x_rows), "ctx", 1), *across]
        x_pieces += [swap(part, "ctx", 1) for part in across]
    else:
        x_all = {(0, p): x_rows[p] for p in range(seq_count)}
        for bit in reversed(bits_of(group)):
            for r, p in list(x_all):
                x_all[r ^ bit, p] = swap(x_all[r, p], "ctx", bit)
        x_pieces = [x_all[r, p] for r in range(group) for p in range(seq_count)]

    w_parts = jnp.pad(w_qkv.reshape(-1, 3, width), ((0, 0), (0, 0), (0, spare))) if spare else None
    if spare:
        w_mine = [lax.dynamic_slice_in_dim(w_parts[:, k], member * slab, slab, 1) for k in (1, 2, 0)]
    else:
        w_mine = [lax.dynamic_slice_in_dim(w_qkv, k * width + member * slab, slab, 1) for k in (1, 2, 0)]
    small = jnp.concatenate([ln_gains.reshape(-1), biases.reshape(-1), up_bias])
    small_rows = -(-small.shape[0] // (3 * slab) // 16) * 16
    small_count = small.shape[0]
    small = jnp.pad(small, (0, small_rows * 3 * slab - small_count)).reshape(small_rows, 3 * slab)
    w_mine = jnp.concatenate([jnp.concatenate(w_mine, axis=1), small], axis=0)
    w_pieces = [w_mine]
    for bit in bits_of(n_f):
        w_pieces += [swap(part, "fsdp", bit) for part in w_pieces]
    small = [part[f_width:].reshape(-1)[:small_count] for part in w_pieces]
    small = jnp.stack(to_absolute(small, f_index)).astype(F32)
    gains_all = small[:, : 2 * f_width].reshape(n_f, 2, f_width).transpose(1, 0, 2).reshape(2, width)
    biases_all = (
        small[:, 2 * f_width : 8 * f_width].reshape(n_f, 6, f_width).transpose(1, 0, 2).reshape(6, width)
    )
    up_shift = small[:, 8 * f_width :].reshape(-1)
    bias_mine = lax.dynamic_slice_in_dim(
        jnp.pad(biases_all[:2], ((0, 0), (0, spare))), member * slab, slab, 1
    ).reshape(2, heads, HD)
    bias_wide = jnp.concatenate(
        [jnp.zeros_like(bias_mine[0]), bias_mine[1], bias_mine[0]], axis=0
    ).reshape(1, -1)

    cot_in = gate(cotangent, x_rows)
    cots = to_planes([lax.dynamic_index_in_dim(cot_in, plane ^ p, 1, keepdims=False) for p in range(seq_count)])
    if fast:
        core, chip = member & 1, member >> 1
        quarter, half = f_width // 4, f_width // 2
        up_quarter = lax.dynamic_slice_in_dim(w_up, (core * 2 + chip) * quarter, quarter, 0)
        up_quarter = gate(up_quarter, w_mine, across[0])
        tall = w_down.shape[0] // 2
        joint = lax.dynamic_slice_in_dim(w_down, core * tall, tall, 0).reshape(-1, half, width)
        joint = [lax.dynamic_slice_in_dim(w_out, core * half, half, 0), *joint]
        joint = swap(gate(jnp.concatenate(joint, axis=1), up_quarter), "fsdp", 1)
        up_quarter = swap(up_quarter, "fsdp", 1)
        up_across = swap(up_quarter, "ctx", 2)
    else:
        up_halves = fetch_halves(w_up)
        down_halves = fetch_halves(w_down)
    x_pieces = [piece.reshape(-1, positions + 16, width) for piece in x_pieces]
    x_seq, qa, ka, va, loc, *ctx_parts = attention_forward(
        turns, x_pieces, w_pieces, bias_wide, heads, group, seq_count, positions
    )
    x_seq = x_seq.reshape(blocks * BLK, width)
    if fast:
        ctx_parts, up_across, cots = lax.optimization_barrier((ctx_parts, up_across, cots))
        up_other = [swap(part, "ctx", 1) for part in (gate(up_quarter, ctx_parts[0]), up_across)]
    ctx_mine = ctx_parts
    if fast:
        ctx_parts = [ctx_parts[0]] + [swap(ctx_parts[r], "ctx", r) for r in (1, 2, 3)]
    else:
        ctx_parts = exchange(ctx_parts[: group // 2], jnp.stack(ctx_parts[group // 2 :]))
    if fast:
        joint_other = swap(gate(joint, ctx_mine[0]), "ctx", 1)
        parts = [w_out.reshape(2, slab, width), w_up, w_down, up_quarter, up_across, *up_other, joint, joint_other]
        plan = [(0, None, 0), (1, None, 1), (2, None, 2)] + [(3 + k, None, 1) for k in range(4)]
        theirs = 1 - f_index
        places = [2 * f_index, f_index * f_width, f_index * 2 * tall]
        for k in range(4):
            part = (core ^ (k >> 1)) * 2 + (chip ^ (k & 1))
            places.append(theirs * f_width + part * quarter)
        for k in range(2):
            plan += [(7 + k, n * width, 0 if n == 0 else 2) for n in range(1 + tall // half)]
            places.append(2 * theirs + (core ^ k))
            places += [theirs * 2 * tall + (core ^ k) * tall + n * half for n in range(tall // half)]
    else:
        out_full = jnp.concatenate(gather_fsdp(w_out), axis=0)
        out_full = jnp.pad(out_full, ((0, spare), (0, 0))).reshape(group, slab, width)
        up_parts, up_places = weight_parts(w_up, up_halves)
        down_parts, down_places = weight_parts(w_down, down_halves)
        parts, places = [out_full, *up_parts, *down_parts], [0, *up_places, *down_places]
        plan = [(0, None, 0)] + [(1 + k, None, 1) for k in range(len(up_parts))]
        plan += [(1 + len(up_parts) + k, None, 2) for k in range(len(down_parts))]
    vectors = jnp.concatenate([biases_all, gains_all])
    place = jnp.stack([member] + [jnp.int32(p) for p in places])
    done = layer(
        place,
        x_seq,
        cots,
        vectors,
        up_shift.reshape(1, -1),
        ctx_parts,
        parts,
        plan,
        fast,
    )
    pieces = group // 2 + 1
    results, d_parts, done = done[:seq_count], done[-pieces:], done[seq_count:-pieces]
    results = to_planes(results)
    back = partial(attention_backward, loc, turns, qa, ka, va, w_pieces, width)
    hidden_width = w_up.shape[1]
    used = 6 * f_width + hidden_width // n_f

    if fast:
        act_mine, pack_one, d_second, first_low, dh1, dhid_mine, dbr_mine, pack_two, small_sums = done
        piece = hidden_width // n_f // 16
        pack_one = swap(pack_one, "ctx", 1)
        pack_two = swap(pack_two, "ctx", 1)
        step = (hidden_width + width + 256) // 16
        shape = jax.ShapeDtypeStruct((2, 4, f_width, step), BF16)
        up_keep, up_send = local_call(
            up_grad_kernel,
            (shape,) * 2,
            (
                turns,
                first_low,
                dhid_mine,
                dbr_mine,
                small_sums,
                pack_two,
                *ctx_parts,
            ),
            [
                pltpu.VMEM((width, 2 * rows_here), BF16),
                pltpu.VMEM((group, slab, 2 * rows_here), BF16),
                pltpu.VMEM((2, f_width, LANES), F32),
                pltpu.VMEM(first_low.shape, BF16),
                pltpu.VMEM(dhid_mine.shape, BF16),
                pltpu.VMEM(dbr_mine.shape, BF16),
                pltpu.VMEM(pack_two.shape, BF16),
                pltpu.VMEM(shape.shape, BF16),
                pltpu.VMEM(shape.shape, BF16),
                pltpu.SemaphoreType.DMA((8,)),
            ],
            "up_grad",
            loose=(1, 2, 3, 5, 10, 11),
            limit=56,
        )
        shape = jax.ShapeDtypeStruct((2, 4, piece, width), BF16)
        down_keep, down_send = local_call(
            down_grad_kernel,
            (shape,) * 2,
            (turns, gate(act_mine, up_send), d_second, pack_one),
            [
                pltpu.VMEM(act_mine.shape, BF16),
                pltpu.VMEM(d_second.shape, BF16),
                pltpu.VMEM(pack_one.shape, BF16),
                pltpu.VMEM(shape.shape, BF16),
                pltpu.VMEM(shape.shape, BF16),
                pltpu.SemaphoreType.DMA((7,)),
            ],
            "down_grad",
            loose=range(1, 6),
        )
        d_parts = exchange(d_parts[:-1], d_parts[-1], between=up_send)
        d_parts = gate(d_parts, down_send, up_send)
        down_got, up_got = swap(down_send, "fsdp", 1), swap(up_send, "ctx", 2)
        keep, send, d_qkv = back(ctx_mine, d_parts, heads)
        down_first, down_got = reduce_square(down_keep, down_got, send, "ctx", 2)
        up_first, up_got = reduce_square(up_keep, up_got, send, "fsdp", 1)
        output = from_planes([gate(results[0], send)] + results[1:])
        keep, send, d_qkv, down_first, up_first, output = lax.optimization_barrier(
            (keep, send, d_qkv, down_first, up_first, output)
        )
        shape = jax.ShapeDtypeStruct((4, (f_width + 64) // 4, 3 * slab), BF16)
        mine, theirs = local_call(
            projection_grad_kernel,
            (shape, shape),
            (turns, x_seq, d_qkv),
            [
                pltpu.VMEM(x_seq.shape, BF16),
                pltpu.VMEM(d_qkv.shape, BF16),
                pltpu.SemaphoreType.DMA((2,)),
            ],
            "projection_grad",
            loose=(1, 2),
        )
        cores = swap(send, "ctx", 1)
    else:
        dh1, active, d_hidden, first_low, d_second, d_branch, sums, upb_grad = done
        d_parts = exchange(d_parts[:-1], d_parts[-1])
        keep, send, d_qkv = back(ctx_mine, d_parts, heads)
        output = from_planes(results)
        context_low = jnp.concatenate(to_absolute(ctx_parts, member), axis=1)[:, :width]
        grad_down = dot(active, d_second, ((0,), (0,)))
        grad_up = dot(first_low, d_hidden, ((0,), (0,)))
        grad_out = dot(context_low, d_branch, ((0,), (0,)))
        down_total = reduce_over_all(grad_down.reshape(n_f, -1, width))
        vectors = sums[:6].reshape(6, n_f, f_width).transpose(1, 0, 2).reshape(n_f, -1)
        vectors = jnp.concatenate([vectors, upb_grad.reshape(n_f, -1)], axis=1)
        extra = -(-used // f_width // LANES) * LANES
        vectors = jnp.pad(vectors, ((0, 0), (0, f_width * extra - used))).reshape(n_f, f_width, extra)
        up_out = jnp.concatenate(
            [grad_up.reshape(n_f, f_width, -1), grad_out.reshape(n_f, f_width, -1), vectors], axis=2
        )
        up_out = reduce_over_all(up_out)
        up_total = up_out[:, :hidden_width]
        out_total = up_out[:, hidden_width : hidden_width + width]
        vectors = up_out[:, hidden_width + width :].reshape(-1)
        gains_total = vectors[: 2 * f_width].reshape(2, f_width)
        biases_late = vectors[2 * f_width : 6 * f_width].reshape(4, f_width)
        up_bias_total = vectors[6 * f_width : used]

    if not fast:
        cores = swap(send, "ctx", 1)
    shape = (seq_count, positions, width)
    pieces = {2 * i: list((keep[i] + cores[i].astype(F32)).reshape(shape)) for i in range(group // 2)}
    far, close = [], []
    for bit in bits_of(group)[1:]:
        for r in [r for r in pieces if r & bit]:
            part = pieces.pop(r)
            cut = seq_count // 2
            far = jnp.stack([part[p].astype(BF16) for p in range(cut, seq_count)])
            close = jnp.stack([part[p].astype(BF16) for p in range(cut)])
            if fast:
                down_first = gate(down_first, far)
            far, close = swap(far, "ctx", bit), swap(close, "ctx", bit)
            got = [*close, *far]
            pieces[r ^ bit] = [pieces[r ^ bit][p] + got[p].astype(F32) for p in range(seq_count)]
    dh1 = dh1.reshape(shape)
    input_grad = from_planes(
        to_planes([(dh1[p] + pieces[0][p]).astype(BF16) for p in range(seq_count)])
    )

    if fast:
        got = swap(theirs, "fsdp", 1)
        down_four, down_parts = reduce_planes(sum_planes(down_first, [down_got]))
        up_four, up_parts = reduce_planes(sum_planes(gate(up_first, far), [up_got]), late=(down_four,))
        four = range(1, 5)
        down_total = local_call(
            down_final_kernel,
            (jax.ShapeDtypeStruct((hidden_width // n_f, width), F32),),
            (turns, *down_parts),
            [
                pltpu.VMEM((4, 4, piece, width), BF16),
                pltpu.VMEM((hidden_width // n_f, width), F32),
                pltpu.SemaphoreType.DMA((20,)),
            ],
            "down_final",
            loose=(*four, 5),
        )[0]
        up_total, out_total, gains_total, biases_late, up_bias_total = local_call(
            up_final_kernel,
            (
                jax.ShapeDtypeStruct((f_width, hidden_width), F32),
                jax.ShapeDtypeStruct((f_width, width), F32),
                jax.ShapeDtypeStruct((2, f_width), F32),
                jax.ShapeDtypeStruct((4, f_width), F32),
                jax.ShapeDtypeStruct((hidden_width // n_f,), F32),
            ),
            (turns, *up_parts),
            [
                pltpu.VMEM((4, 4, f_width, step), BF16),
                pltpu.VMEM((16, f_width, step), F32),
                pltpu.SemaphoreType.DMA((20,)),
            ],
            "up_final",
            loose=(*four, 5, 6),
        )
        qkv_parts = reduce_planes(
            sum_planes(gate(mine, close), [got]), last=(up_total, down_total)
        )[1]
        qkv_total, biases_total = local_call(
            qkv_final_kernel,
            (jax.ShapeDtypeStruct((f_width, 3 * width), F32), jax.ShapeDtypeStruct((6, f_width), F32)),
            (turns, biases_late, *qkv_parts),
            [
                pltpu.VMEM((4, f_width + 64, 3 * slab), BF16),
                pltpu.VMEM((4, 4, (f_width + 64) // 4, 3 * slab), BF16),
                pltpu.VMEM((f_width, 3 * width), F32),
                pltpu.VMEM((8, width), F32),
                pltpu.SemaphoreType.DMA((7,)),
            ],
            "qkv_final",
            loose=(2, 3, 4, 5, 6),
        )
    else:
        grad_qkv = dot(x_seq, d_qkv, ((0,), (0,))).reshape(n_f, f_width, 3 * slab)
        sums = jnp.sum(d_qkv.astype(F32), axis=0, keepdims=True)
        sums = jnp.pad(sums, ((0, 15), (0, 0)))
        value = jnp.concatenate([grad_qkv, jnp.broadcast_to(sums[None], (n_f,) + sums.shape)], axis=1)
        for bit in reversed(bits_of(n_f)):
            value = halve(value, "fsdp", 0, bit, f_index)
        value = value[0]
        plane_bits = [bit * group for bit in bits_of(seq_count)]
        for bit in plane_bits:
            value = halve(value, "ctx", 0, bit, c_index)
        value = value.astype(BF16)
        for bit in reversed(plane_bits):
            value = double(value, "ctx", 0, bit, c_index)
        parts = [value]
        for bit in bits_of(group):
            parts += [swap(part, "ctx", bit) for part in parts]
        parts = to_absolute(parts, member)
        qkv_total = jnp.stack([part.reshape(-1, 3, slab) for part in parts], axis=2).reshape(-1, 3, group * slab)
        qkv_total = jnp.concatenate([qkv_total[:, 2:], qkv_total[:, :2]], axis=1)[:, :, :width].astype(F32)
        early = lax.dynamic_slice_in_dim(qkv_total[f_width][0::2], f_index * f_width, f_width, 1)
        qkv_total = qkv_total[:f_width].reshape(f_width, 3 * width)
        biases_total = jnp.concatenate([early, biases_late])
    return (
        output,
        input_grad,
        qkv_total,
        out_total,
        up_total,
        down_total,
        gains_total,
        biases_total,
        up_bias_total,
    )


def solution(mesh):
    placed = (
        P("ctx", "fsdp", None),
        P("ctx", "fsdp"),
        P("fsdp", "ctx", None, None),
        P("fsdp", None),
        P("fsdp", None),
        P("fsdp", None),
        P("fsdp", None),
        P(None, "fsdp"),
        P(None, "fsdp"),
        P("fsdp"),
        P("ctx", "fsdp", None),
    )
    return jax.shard_map(
        local,
        mesh=mesh,
        in_specs=placed,
        out_specs=(
            P("ctx", "fsdp", None),
            P("ctx", "fsdp", None),
            P("fsdp", None),
            P("fsdp", None),
            P("fsdp", None),
            P("fsdp", None),
            P(None, "fsdp"),
            P(None, "fsdp"),
            P("fsdp"),
        ),
        check_vma=False,
    )
```

```python
import math
from functools import partial

import jax
import jax.numpy as jnp
from jax import lax
from jax.experimental import pallas as pl
from jax.experimental.pallas import tpu as pltpu
from jax.sharding import PartitionSpec as P

HD = 64
BLK = 64
LANES = 128
SLOTS = 8
DOCS = 32
EPSILON = 1e-06
NEGATIVE = -1e30
SCALE = HD**-0.5
RATE = SCALE / math.log(2.0)
MIB = 1024 * 1024
WEIGHT = 0

BF16 = jnp.bfloat16
F32 = jnp.float32


def dot(left, right, dims):
    return lax.dot_general(left, right, ((dims[0], dims[1]), ((), ())), preferred_element_type=F32)


def swap(value, axis, mask):
    count = lax.axis_size(axis)
    return lax.ppermute(value, axis, [(i, i ^ mask) for i in range(count)])


def gate(value, *after):
    return lax.optimization_barrier((value, *after))[0]


def bits_of(count):
    return [1 << k for k in range((count - 1).bit_length())]


def choose(index, cases):
    return cases[0] if len(cases) == 1 else lax.select_n(index, *cases)


def to_absolute(relative, index):
    count = len(relative)
    return [choose(index, [relative[k ^ i] for i in range(count)]) for k in range(count)]


def split_three(values):
    high = values.astype(BF16)
    rest = values - high.astype(F32)
    middle = rest.astype(BF16)
    return high, middle, (rest - middle.astype(F32)).astype(BF16)


def lane_ids(shape):
    return lax.broadcasted_iota(jnp.int32, shape, len(shape) - 1)


def place_three(base, values, lane, first):
    high, middle, small = split_three(values)
    base = jnp.where(lane == first, high.astype(F32), base)
    base = jnp.where(lane == first + 1, middle.astype(F32), base)
    return jnp.where(lane == first + 2, small.astype(F32), base)


def picked(ref, loc_ref, head, place):
    parts = [
        ref[head, pl.ds(pl.multiple_of(loc_ref[place + s] * BLK, BLK), BLK), :]
        for s in range(SLOTS)
    ]
    return jnp.concatenate(parts, axis=0)


def gathered(pieces, places, target, sem, first):
    copies = []
    for k, (piece, place) in enumerate(zip(pieces, places)):
        copy = pltpu.make_async_copy(piece, target.at[pl.ds(place, piece.shape[0])], sem.at[first + k])
        copy.start()
        copies.append(copy)
    return copies


def put(source, target, sem, place):
    copy = pltpu.make_async_copy(source, target, sem.at[place])
    copy.start()
    return copy


def over(value, size):
    assert size & (size - 1) == 0
    return lax.shift_right_logical(value, size.bit_length() - 1)


def within(value, size):
    assert size & (size - 1) == 0
    return value & (size - 1)


def absolute_chunk(turn, own, seqs, group):
    return (within(turn, seqs) * group + over(turn, seqs)) ^ own


def split_kernel(tail, at_ref, rows_ref, *rest):
    positions, seqs, width = rows_ref.shape
    if tail:
        line_ref, *rest = rest
    for p, ref in enumerate(rest):
        for s in range(seqs):

            @pl.when((at_ref[3] ^ p) == s)
            def _(ref=ref, s=s):
                ref[:positions, :] = rows_ref[:, s, :]
                if tail:
                    blank = jnp.zeros((tail - 1, width), F32)
                    line = line_ref[s : s + 1, :].astype(F32)
                    ref[positions:, :] = jnp.concatenate([line, blank], axis=0).astype(BF16)


def split_planes(turns, rows, line=None):
    positions, seqs, width = rows.shape
    tail = 0 if line is None else 16
    shape = jax.ShapeDtypeStruct((positions + tail, width), BF16)
    ins = (turns, rows) if line is None else (turns, rows, line)
    return local_call(partial(split_kernel, tail), (shape,) * seqs, ins, [], "split_planes")


def forward_kernel(heads, group, seqs, counts, at_ref, bias_ref, *rest):
    x_pieces, w_pieces, rest = rest[: counts[0]], rest[counts[0] : sum(counts)], rest[sum(counts) :]
    x_out, q_out, k_out, v_out, loc_ref = rest[:5]
    ctx_refs, rest = rest[5 : 5 + group], rest[5 + group :]
    x_s, q_s, k_s, v_s, w_s, seg_s, number_v, number_s, sem = rest
    chunks, tall, width = x_s.shape
    chunk, blocks = x_out.shape[1], q_s.shape[1] // BLK
    rows = chunks * chunk
    w_rows = width // counts[1]
    w_copies = gathered(
        [piece.at[pl.ds(0, w_rows)] for piece in w_pieces],
        [pl.multiple_of((at_ref[0] ^ k) * w_rows, 16) for k in range(counts[1])],
        w_s,
        sem,
        counts[0],
    )
    last = sum(counts)
    x_copies, turn = [], 0
    for piece in x_pieces:
        count = piece.shape[0]
        x_copies.append(put(piece, x_s.at[pl.ds(turn, count)], sem, last + 5 + turn))
        turn += count
    for copy in w_copies:
        copy.wait()
    for copy in x_copies:
        copy.wait()
    out_copies = [put(x_s.at[:, pl.ds(0, chunk)], x_out, sem, last)]
    tile = 2 * chunk
    lines = jnp.concatenate(
        [x_s[k, chunk:, : 2 * LANES].astype(F32)[:1] for k in range(chunks)], axis=0
    )
    number_v[...] = lines[:, LANES:].astype(jnp.int32)
    number_copy = put(number_v, number_s, sem, last + 4)
    seg_s[...] = jnp.concatenate([lines[:, :LANES], jnp.zeros((LANES - chunks, LANES), F32)], axis=0).T
    number_copy.wait()
    per = chunk // BLK
    own, member = at_ref[5], at_ref[4]

    def place_of(block):
        c = over(block, per) ^ own
        return (within(c, group) * seqs + over(c, group)) * per + within(block, per)

    def slots_of(j):
        turn, inner = over(j, per), within(j, per)
        real = absolute_chunk(turn, own, seqs, group) * per + inner
        fixed = []
        for d in (-1, 0, 1):
            near = jnp.clip(real + d, 0, blocks - 1)
            fixed.append(jnp.where(near == real + d, place_of(near), blocks))
        for b in range(2):
            fixed.append(jnp.where(jnp.abs(real - b) > 1, place_of(jnp.int32(b)), blocks))
        first = member * (LANES // group) + inner * (heads * 3)
        for h in range(heads):
            free = [place_of(number_s[turn, first + h * 3 + r]) for r in range(3)]
            for s, value in enumerate(fixed + free):
                loc_ref[(j * heads + h) * SLOTS + s] = value

    def project(i, carry):
        at = pl.ds(pl.multiple_of(i * tile, tile), tile)
        x = jnp.concatenate([x_s[2 * i, :chunk, :], x_s[2 * i + 1, :chunk, :]], axis=0)
        lane = lane_ids((tile, LANES))
        seg = []
        for k in range(2):
            mine = lane_ids((LANES, LANES)) == 2 * i + k
            seg.append(jnp.sum(jnp.where(mine, seg_s[...], 0.0), axis=1, keepdims=True))
        same = (lane - HD).astype(F32) == jnp.concatenate(seg, axis=0)
        coded = (lane >= HD) & (lane < HD + DOCS)
        ones = (lane >= HD + DOCS) & (lane < HD + DOCS + 3)
        q_extra = jnp.where(coded & same, NEGATIVE, 0.0)
        k_extra = jnp.where((coded & jnp.logical_not(same)) | ones, 1.0, 0.0)
        v_extra = jnp.where((lane >= HD) & (lane < HD + 3), 1.0, 0.0)
        head_lane = lane < HD
        y = dot(x, w_s[...], ((1,), (0,))) + bias_ref[...]
        for part, extra, ref in ((0, k_extra, k_s), (1, v_extra, v_s), (2, q_extra, q_s)):
            for h in range(heads):
                n = part * heads + h
                here = y[:, n // 2 * LANES : (n // 2 + 1) * LANES]
                if n % 2:
                    here = pltpu.roll(here, HD, 1)
                elif here.shape[1] < LANES:
                    here = jnp.concatenate([here, jnp.zeros((tile, LANES - here.shape[1]), F32)], axis=1)
                ref[h, at, :] = jnp.where(head_lane, here, extra).astype(BF16)
        for k in range(2 * per):
            slots_of(i * 2 * per + k)
        return carry

    lax.fori_loop(0, rows // tile, project, 0)
    lane = lane_ids((BLK, LANES))
    null_key = jnp.where((lane >= HD) & (lane < HD + DOCS), 1.0, 0.0).astype(BF16)
    for h in range(heads):
        k_s[h, rows : rows + BLK, :] = null_key
        v_s[h, rows : rows + BLK, :] = jnp.zeros((BLK, LANES), BF16)
    out_copies += [put(k_s, k_out, sem, last + 1), put(v_s, v_out, sem, last + 2)]
    part_blocks = rows // BLK // group
    together = 8

    for r in range(group):

        def attend(i, carry, r=r):
            units = [(u, h) for u in range(together) for h in range(heads)]
            row = [r * part_blocks + i * together + u for u in range(together)]
            at = [pl.ds(pl.multiple_of(j * BLK, BLK), BLK) for j in row]
            place = [(row[u] * heads + h) * SLOTS for u, h in units]
            q = [q_s[h, at[u], :] for u, h in units]
            scores = [
                dot(q[n], picked(k_s, loc_ref, h, place[n]), ((1,), (1,))) for n, (u, h) in enumerate(units)
            ]
            top = [jnp.max(t, axis=1, keepdims=True) for t in scores]
            prob = [jnp.exp2((t - m) * RATE).astype(BF16) for t, m in zip(scores, top)]
            mixed = [
                dot(prob[n], picked(v_s, loc_ref, h, place[n]), ((1,), (0,))) for n, (u, h) in enumerate(units)
            ]
            total = [m[:, HD : HD + 1] for m in mixed]
            done = [(m / t)[:, :HD] for m, t in zip(mixed, total)]
            level = [-(m + jnp.log2(t) * (1.0 / RATE)) for m, t in zip(top, total)]
            for n, (u, h) in enumerate(units):
                q_s[h, at[u], :] = place_three(q[n].astype(F32), level[n], lane, HD + DOCS).astype(BF16)
            for u in range(together):
                here = pl.ds(pl.multiple_of((i * together + u) * BLK, BLK), BLK)
                ctx_refs[r][here, :] = jnp.concatenate(done[u * heads : (u + 1) * heads], axis=1).astype(BF16)
            return carry

        lax.fori_loop(0, part_blocks // together, attend, 0)
    out_copies.append(put(q_s, q_out, sem, last + 3))
    for copy in out_copies:
        copy.wait()


def backward_kernel(heads, group, count, loc_ref, at_ref, q_in, k_in, v_in, *rest):
    w_pieces, rest = rest[:count], rest[count:]
    ctx_refs, grad_refs, rest = rest[:group], rest[group : 2 * group], rest[2 * group :]
    grad_refs = [ref if len(ref.shape) == 2 else ref.at[0] for ref in grad_refs]
    keep_ref, send_ref, d_out, out_ref, da_s, dq_s, w_s, keep_s, send_s, qa_ref, ka_ref, va_ref, sem, *rest = rest
    dk_even, dk_odd, dv_even, dv_odd = (rest[i * heads : (i + 1) * heads] for i in range(4))
    rows, width = qa_ref.shape[1], w_s.shape[0]
    loads = [
        put(*pair, sem, count + 2 + n)
        for n, pair in enumerate(((q_in, qa_ref), (k_in, ka_ref), (v_in, va_ref)))
    ]
    w_rows = width // count
    w_copies = gathered(
        [piece.at[pl.ds(0, w_rows)] for piece in w_pieces],
        [pl.multiple_of((at_ref[0] ^ k) * w_rows, 16) for k in range(count)],
        w_s,
        sem,
        0,
    )
    part_rows = rows // group
    tile = 128
    lane_tile = lane_ids((tile, LANES))
    blank = jnp.zeros((tile, LANES - HD), F32)

    def load(i, carry):
        at = pl.ds(pl.multiple_of(i * tile, tile), tile)
        for r in range(group):
            all_at = pl.ds(pl.multiple_of(r * part_rows + i * tile, tile), tile)
            grads = grad_refs[r][at, :].astype(F32)
            both = grads * ctx_refs[r][at, :].astype(F32)
            for h in range(heads):
                cols = slice(h * HD, (h + 1) * HD)
                delta = jnp.sum(both[:, cols], axis=1, keepdims=True)
                wide = jnp.concatenate([grads[:, cols], blank], axis=1)
                da_s[h, all_at, :] = place_three(wide, -delta, lane_tile, HD).astype(BF16)
        for b in range(rows // BLK // (part_rows // tile)):
            for ref in (*dk_even, *dk_odd, *dv_even, *dv_odd):
                ref[i * (rows // BLK // (part_rows // tile)) + b] = jnp.zeros((HD, LANES), F32)
        return carry

    lax.fori_loop(0, part_rows // tile, load, 0)
    for ref in (*dk_even, *dk_odd, *dv_even, *dv_odd):
        ref[rows // BLK] = jnp.zeros((HD, LANES), F32)
    for copy in loads:
        copy.wait()
    together = 4

    def attend(i, carry):
        units = [(u, h) for u in range(together) for h in range(heads)]
        row = [i * together + u for u in range(together)]
        at = [pl.ds(pl.multiple_of(j * BLK, BLK), BLK) for j in row]
        place = [(row[u] * heads + h) * SLOTS for u, h in units]
        q = [qa_ref[h, at[u], :] for u, h in units]
        d_mixed = [da_s[h, at[u], :] for u, h in units]
        keys = [picked(ka_ref, loc_ref, h, place[n]) for n, (u, h) in enumerate(units)]
        values = [picked(va_ref, loc_ref, h, place[n]) for n, (u, h) in enumerate(units)]
        scores = [dot(a, b, ((1,), (1,))) for a, b in zip(q, keys)]
        d_prob = [dot(a, b, ((1,), (1,))) for a, b in zip(d_mixed, values)]
        prob = [jnp.exp2(t * RATE) for t in scores]
        d_scores = [(a * b).astype(BF16) for a, b in zip(prob, d_prob)]
        prob = [t.astype(BF16) for t in prob]
        d_q = [dot(a, b, ((1,), (0,))) for a, b in zip(d_scores, keys)]
        q_turned = [t.T[:HD] for t in q]
        d_turned = [t.T[:HD] for t in d_mixed]
        d_keys = [dot(a, b, ((1,), (0,))) for a, b in zip(q_turned, d_scores)]
        d_values = [dot(a, b, ((1,), (0,))) for a, b in zip(d_turned, prob)]
        for n, (u, h) in enumerate(units):
            dq_s[h, at[u], :] = (d_q[n] * SCALE).astype(BF16)
        for u in range(together):
            for s in range(SLOTS):
                for h in range(heads):
                    n = u * heads + h
                    to = loc_ref[place[n] + s]
                    cols = slice((s // 2) * LANES, (s // 2 + 1) * LANES)
                    dk_ref, dv_ref = (dk_odd[h], dv_odd[h]) if s % 2 else (dk_even[h], dv_even[h])
                    dk_ref[to] += d_keys[n][:, cols]
                    dv_ref[to] += d_values[n][:, cols]
        return carry

    lax.fori_loop(0, rows // BLK // together, attend, 0)
    low_lane = lane_ids((HD, LANES)) < BLK

    def finish(i, carry):
        at = [pl.ds(pl.multiple_of((2 * i + u) * BLK, BLK), BLK) for u in range(2)]
        turned = []
        for even, odd, factor in ((dk_even, dk_odd, SCALE), (dv_even, dv_odd, 1.0)):
            for h in range(heads):
                first = even[h][2 * i] + pltpu.roll(odd[h][2 * i], BLK, 1)
                second = pltpu.roll(even[h][2 * i + 1], BLK, 1) + odd[h][2 * i + 1]
                turned.append(jnp.where(low_lane, first, second) * factor)
        pair = pl.ds(pl.multiple_of(2 * i * BLK, 2 * BLK), 2 * BLK)
        for n in range(heads):
            both = jnp.concatenate([turned[2 * n], turned[2 * n + 1]], axis=0)
            out_ref[pair, n * LANES : (n + 1) * LANES] = both.astype(BF16).T
        done = [dq_s[h, pair, :][:, :HD].astype(F32) for h in range(heads)]
        out_ref[pair, heads * LANES :] = jnp.concatenate(done, axis=1).astype(BF16)
        return carry

    lax.fori_loop(0, rows // BLK // 2, finish, 0)
    out_copies = [put(out_ref, d_out, sem, count + 5)]
    for copy in w_copies:
        copy.wait()
    for odd, hold, ref in ((1, send_s, send_ref), (0, keep_s, keep_ref)):

        def to_rows(i, carry, odd=odd, hold=hold):
            at = pl.ds(pl.multiple_of((2 * i + odd) * part_rows, BLK), part_rows)
            hold[i] = dot(out_ref[at, :], w_s[...], ((1,), (1,))).astype(hold.dtype)
            return carry

        lax.fori_loop(0, group // 2, to_rows, 0)
        out_copies.append(put(hold, ref, sem, count + odd))
    for copy in out_copies:
        copy.wait()


def projection_grad_kernel(at_ref, x_in, d_in, mine_ref, theirs_ref, x_s, d_s, sem):
    copies = [put(x_in, x_s, sem, 0), put(d_in, d_s, sem, 1)]
    half = x_s.shape[1] // 2
    copies[1].wait()
    sums = row_sum(d_s[...].astype(F32))
    shape = (64, sums.shape[1])
    tail = jnp.where(lax.broadcasted_iota(jnp.int32, shape, 0) == 0, jnp.broadcast_to(sums, shape), 0.0)
    copies[0].wait()
    for k, ref in ((1, theirs_ref), (0, mine_ref)):
        cols = pl.ds(pl.multiple_of((at_ref[0] ^ k) * half, LANES), half)
        grad = jnp.concatenate([dot(x_s[:, cols], d_s[...], ((0,), (0,))), tail], axis=0).astype(BF16)
        size = grad.shape[0] // 4
        for z in range(4):
            ref[plane_spot(z, at_ref[3])] = grad[z * size : (z + 1) * size]


def cost(microseconds):
    return pl.CostEstimate(flops=int(microseconds * WEIGHT), bytes_accessed=0, transcendentals=0)


def whole(memory):
    return pl.BlockSpec(memory_space=memory)


def pieces_of(group, rows, columns):
    half = group // 2
    near = jax.ShapeDtypeStruct((rows, columns), BF16)
    return (near,) * half + (jax.ShapeDtypeStruct((half, rows, columns), BF16),)


def attention_forward(turns, x_pieces, w_pieces, bias, heads, group, seqs, positions):
    chunks, width = group * seqs, x_pieces[0].shape[2]
    rows = positions * chunks
    counts = (len(x_pieces), len(w_pieces))
    kept = jax.ShapeDtypeStruct((heads, rows + BLK, LANES), BF16)
    return pl.pallas_call(
        partial(forward_kernel, heads, group, seqs, counts),
        out_shape=(
            jax.ShapeDtypeStruct((chunks, positions, width), BF16),
            jax.ShapeDtypeStruct((heads, rows, LANES), BF16),
            kept,
            kept,
            jax.ShapeDtypeStruct((rows // BLK * heads * SLOTS,), jnp.int32),
        )
        + (jax.ShapeDtypeStruct((rows // group, heads * HD), BF16),) * group,
        in_specs=[whole(pltpu.SMEM), whole(pltpu.VMEM)] + [whole(pl.ANY)] * sum(counts),
        out_specs=(whole(pl.ANY),) * 4 + (whole(pltpu.SMEM),) + (whole(pltpu.VMEM),) * group,
        scratch_shapes=[
            pltpu.VMEM((chunks, positions + 16, width), BF16),
            pltpu.VMEM((heads, rows, LANES), BF16),
            pltpu.VMEM((heads, rows + BLK, LANES), BF16),
            pltpu.VMEM((heads, rows + BLK, LANES), BF16),
            pltpu.VMEM((width, 3 * heads * HD), BF16),
            pltpu.VMEM((LANES, LANES), F32),
            pltpu.VMEM((chunks, LANES), jnp.int32),
            pltpu.SMEM((chunks, LANES), jnp.int32),
            pltpu.SemaphoreType.DMA((sum(counts) + 5 + chunks,)),
        ],
        compiler_params=pltpu.CompilerParams(vmem_limit_bytes=56 * MIB),
        cost_estimate=cost(19),
        name="attention_forward",
    )(turns, bias, *x_pieces, *w_pieces)


def attention_backward(loc, turns, qa, ka, va, w_pieces, width, ctx_parts, grads, heads):
    rows = qa.shape[1]
    blocks, group, count, slab = rows // BLK, len(grads), len(w_pieces), heads * HD
    part = (group // 2, rows // group, width)
    outs = (
        jax.ShapeDtypeStruct(part, F32),
        jax.ShapeDtypeStruct(part, BF16),
        jax.ShapeDtypeStruct((rows, 3 * slab), BF16),
    )
    return pl.pallas_call(
        partial(backward_kernel, heads, group, count),
        out_shape=outs,
        in_specs=[whole(pltpu.SMEM)] * 2
        + [whole(pl.ANY)] * (3 + count)
        + [whole(pltpu.VMEM)] * (2 * group),
        out_specs=(whole(pl.ANY),) * 3,
        scratch_shapes=[
            pltpu.VMEM((rows, 3 * slab), BF16),
            pltpu.VMEM((heads, rows, LANES), BF16),
            pltpu.VMEM((heads, rows, LANES), BF16),
            pltpu.VMEM((width, 3 * slab), BF16),
            pltpu.VMEM(part, F32),
            pltpu.VMEM(part, BF16),
            pltpu.VMEM(qa.shape, BF16),
            pltpu.VMEM(ka.shape, BF16),
            pltpu.VMEM(va.shape, BF16),
            pltpu.SemaphoreType.DMA((count + 6,)),
        ]
        + [pltpu.VMEM((blocks + 1, HD, LANES), F32)] * (4 * heads),
        compiler_params=pltpu.CompilerParams(vmem_limit_bytes=56 * MIB),
        cost_estimate=cost(50),
        name="attention_backward",
    )(loc, turns, qa, ka, va, *w_pieces, *ctx_parts, *grads)


def norm_values(values):
    average = jnp.mean(values, axis=-1, keepdims=True)
    centred = values - average
    inv_std = lax.rsqrt(jnp.mean(centred * centred, axis=-1, keepdims=True) + EPSILON)
    return centred * inv_std, inv_std


def norm_pull(upstream, scaled, inv_std, gain_row):
    weighted = upstream * gain_row
    centre_term = jnp.mean(weighted, axis=-1, keepdims=True)
    slope_term = jnp.mean(weighted * scaled, axis=-1, keepdims=True)
    return inv_std * (weighted - centre_term - scaled * slope_term)


def gelu_pair(v):
    rate = math.sqrt(2.0 / math.pi)
    square = v * v
    t = jnp.tanh(rate * v * (1.0 + 0.044715 * square))
    half = 0.5 * (1.0 + t)
    slope = half + (0.5 * rate) * v * (1.0 - t * t) * (1.0 + (3.0 * 0.044715) * square)
    return v * half, slope


def row_sum(values):
    return jnp.sum(values, axis=0, keepdims=True)


def layer_kernel(group, count, plan, seqs, fast, at_ref, x_ref, vec_ref, upb_ref, *rest):
    ctx_refs = rest[:group]
    arrays, rest = rest[group : group + count], rest[group + count :]
    cot_refs, result_refs, rest = rest[:seqs], rest[seqs : 2 * seqs], rest[2 * seqs :]
    if fast:
        early, (dh1_ref, dhid_mine, dbr_mine, pack_two, small_ref) = rest[:4], rest[4:9]
        rest = rest[9:]
        slab = ctx_refs[0].shape[1]
    else:
        dh1_ref, active_ref, dhid_ref, first_low_ref, dsec_ref, dbr_ref, sums_out, upb_out = rest[:8]
        rest = rest[8:]
    near, far, rest = rest[: group // 2], rest[group // 2], rest[group // 2 + 1 :]
    dctx_refs = [*near, *[far.at[r] for r in range(group // 2)]]
    out_s, up_s, down_s, slope_s, scaled_s, inv_s, acc_s, cot_s, result_s, x_s, dbr_s, sums_s, upb_s, sem = rest[:14]
    if fast:
        act_mine, pack_one, dsec_ref, first_low_ref = rest[14:]
    rows, width = acc_s.shape
    hidden = up_s.shape[1]
    member = at_ref[0]
    core = member & 1
    copies = []
    for k, (array, column, w) in enumerate(plan):
        scratch, source = (out_s, up_s, down_s)[w], arrays[array]
        if column is not None:
            source = source.at[:, pl.ds(column, scratch.shape[-1])]
        start = pl.multiple_of(at_ref[1 + k], 1 if w == 0 else 16)
        one = w == 0 and len(source.shape) == 2
        copies.append(put(source, scratch.at[start] if one else scratch.at[pl.ds(start, source.shape[0])], sem, k))
    k = len(plan)
    part_rows = rows // seqs
    starts = [p * part_rows for p in range(seqs)]
    cot_copies = gathered(cot_refs, starts, cot_s, sem, k)
    x_copy = put(x_ref.at[pl.ds(0, rows)], x_s, sem, k + 2 * seqs)
    b_out, b_first, b_last, b_second = (vec_ref[i : i + 1, :] for i in (2, 3, 4, 5))
    gain_one, gain_two = vec_ref[6:7, :], vec_ref[7:8, :]
    tile = min(256, rows)
    sums_s[...] = jnp.zeros_like(sums_s)

    for copy in [x_copy] + [copy for copy, (_, _, w) in zip(copies, plan) if w == 0]:
        copy.wait()

    def first_norm(i, carry):
        at = pl.ds(pl.multiple_of(i * tile, tile), tile)
        total = x_s[at, :].astype(F32) + b_out
        for r in range(group):
            total = total + dot(ctx_refs[r][at, :], out_s[member ^ r], ((1,), (0,)))
        scaled, inv_std = norm_values(total)
        first = scaled * gain_one + b_first
        scaled_s[at, :] = scaled
        inv_s[at, :] = jnp.broadcast_to(inv_std, (tile, LANES))
        first_low_ref[at, :] = first.astype(BF16)
        acc_s[at, :] = first + b_second
        return carry

    lax.fori_loop(0, rows // tile, first_norm, 0)
    for copy in [copy for copy, (_, _, w) in zip(copies, plan) if w > 0]:
        copy.wait()

    def up_down(start, step, ref, to):
        at = pl.ds(pl.multiple_of(start, step), step)
        v = dot(first_low_ref[...], up_s[:, at], ((1,), (0,))) + upb_ref[:, at]
        active, slope = gelu_pair(v)
        active = active.astype(BF16)
        ref[:, pl.ds(pl.multiple_of(to, step), step)] = active
        slope_s[:, at] = slope
        acc_s[...] += dot(active, down_s[at, :], ((1,), (0,)))

    def down_up(start, step, ref, to):
        at = pl.ds(pl.multiple_of(start, step), step)
        d_hidden = dot(dsec_ref[...], down_s[at, :], ((1,), (1,))) * slope_s[:, at]
        low = d_hidden.astype(BF16)
        ref[:rows, pl.ds(pl.multiple_of(to, step), step)] = low
        upb_s[:, at] = row_sum(low.astype(F32))
        acc_s[...] += dot(low, up_s[:, at], ((1,), (1,)))

    def over_hidden(one, refs):
        if fast:
            step = hidden // 4
            for c, ref in enumerate(refs):

                def part(i, carry, c=c, ref=ref):
                    turn = c ^ core
                    one((i * 2 + turn if one is up_down else turn * 2 + i) * step, step, ref, i * step)
                    return carry

                for i in range(2):
                    part(i, 0)
        else:
            step = 512

            def part(i, carry):
                one(i * step, step, refs[0], i * step)
                return carry

            lax.fori_loop(0, hidden // step, part, 0)

    over_hidden(up_down, (act_mine, pack_one) if fast else (active_ref,))
    for copy in cot_copies:
        copy.wait()

    def last_norm(i, carry):
        at = pl.ds(pl.multiple_of(i * tile, tile), tile)
        scaled, inv_std = norm_values(acc_s[at, :])
        result_s[at, :] = (scaled * gain_two + b_last).astype(BF16)
        upstream = cot_s[at, :].astype(F32)
        pulled = norm_pull(upstream, scaled, inv_std, gain_two)
        acc_s[at, :] = pulled
        low = pulled.astype(BF16)
        dsec_ref[at, :] = low
        if fast:
            pack_one[at, hidden // 2 :] = low
        sums_s[1:2, :] += row_sum(upstream * scaled)
        sums_s[4:5, :] += row_sum(upstream)
        sums_s[5:6, :] += row_sum(pulled)
        return carry

    lax.fori_loop(0, rows // tile, last_norm, 0)
    early_copies = []
    if fast:
        held = (act_mine, pack_one, dsec_ref, first_low_ref)
        early_copies = [put(a, b, sem, k + 2 * seqs + 1 + n) for n, (a, b) in enumerate(zip(held, early))]
    result_copies = [
        put(result_s.at[pl.ds(starts[p], part_rows)], result_refs[p], sem, k + seqs + p) for p in range(seqs)
    ]
    over_hidden(down_up, (dhid_mine, pack_two) if fast else (dhid_ref,))

    def first_back(i, carry):
        at = pl.ds(pl.multiple_of(i * tile, tile), tile)
        upstream, scaled = acc_s[at, :], scaled_s[at, :]
        pulled = norm_pull(upstream, scaled, inv_s[at, :1], gain_one)
        dh1_ref[at, :] = pulled
        low = pulled.astype(BF16)
        dbr_s[at, :] = low
        sums_s[0:1, :] += row_sum(upstream * scaled)
        sums_s[2:3, :] += row_sum(pulled)
        sums_s[3:4, :] += row_sum(upstream)
        for r in range(group):
            dctx_refs[r][at, :] = dot(low, out_s[member ^ r], ((1,), (1,))).astype(BF16)
        return carry

    lax.fori_loop(0, rows // tile, first_back, 0)
    if fast:
        half, wide = width // 2, hidden // 2
        dbr_mine[...] = dbr_s[:, pl.ds(pl.multiple_of(core * half, LANES), half)]
        pack_two[:rows, wide : wide + half] = dbr_s[:, pl.ds(pl.multiple_of((1 - core) * half, LANES), half)]
        pack_two[:rows, wide + half : wide + half + width] = first_low_ref[...]
        pack_two[:rows, wide + half + width :] = jnp.concatenate([ref[...] for ref in ctx_refs], axis=1)
        long = [upb_s[:, i * width : (i + 1) * width] for i in range(hidden // width)]
        blank = jnp.zeros((8 - len(long), width), F32)
        small = jnp.concatenate([sums_s[...], *long, blank], axis=0).astype(BF16)
        small_ref[...] = small
        pack_two[rows:, :width] = small
        pack_two[rows:, width:] = jnp.zeros((16, pack_two.shape[1] - width), BF16)
    else:
        dbr_ref[...] = dbr_s[...]
        sums_out[...] = sums_s[...]
        upb_out[...] = upb_s[...]
    for copy in result_copies + early_copies:
        copy.wait()


def layer(place, x_seq, cots, vectors, up_shift, ctx_parts, parts, plan, fast):
    rows, width = len(cots) * cots[0].shape[0], x_seq.shape[1]
    group, slab = len(ctx_parts), ctx_parts[0].shape[1]
    hidden = up_shift.shape[1]

    def like(columns, dtype=BF16, count=rows):
        return jax.ShapeDtypeStruct((count, columns), dtype)

    half, wide = width // 2, hidden // 2
    if fast:
        held = (like(wide), like(wide + width), like(width), like(width))
        outs = held + (like(width, F32), like(wide), like(half))
        outs += (like(wide + half + 2 * width, BF16, rows + 16), like(width, BF16, 16))
    else:
        held = ()
        outs = (like(width, F32), like(hidden), like(hidden), like(width), like(width), like(width))
        outs += (like(width, F32, 8), like(hidden, F32, 1))
    outs = (jax.ShapeDtypeStruct(cots[0].shape, BF16),) * len(cots) + outs + pieces_of(group, rows, slab)
    return pl.pallas_call(
        partial(layer_kernel, group, len(parts), plan, len(cots), fast),
        out_shape=outs,
        in_specs=[whole(pltpu.SMEM), whole(pl.ANY)]
        + [whole(pltpu.VMEM)] * (2 + group)
        + [whole(pl.ANY)] * (len(parts) + len(cots)),
        out_specs=(whole(pl.ANY),) * (len(cots) + len(held))
        + (whole(pltpu.VMEM),) * (len(outs) - len(cots) - len(held)),
        scratch_shapes=[
            pltpu.VMEM((group, slab, width), BF16),
            pltpu.VMEM((width, hidden), BF16),
            pltpu.VMEM((hidden, width), BF16),
            pltpu.VMEM((rows, hidden), F32),
            pltpu.VMEM((rows, width), F32),
            pltpu.VMEM((rows, LANES), F32),
            pltpu.VMEM((rows, width), F32),
            pltpu.VMEM((rows, width), BF16),
            pltpu.VMEM((rows, width), BF16),
            pltpu.VMEM((rows, width), BF16),
            pltpu.VMEM((rows, width), BF16),
            pltpu.VMEM((8, width), F32),
            pltpu.VMEM((1, hidden), F32),
            pltpu.SemaphoreType.DMA((len(plan) + 2 * len(cots) + 1 + len(held),)),
        ]
        + [pltpu.VMEM(one.shape, BF16) for one in held],
        compiler_params=pltpu.CompilerParams(vmem_limit_bytes=56 * MIB),
        cost_estimate=cost(29),
        name="feed_forward",
    )(place, x_seq, vectors, up_shift, *ctx_parts, *parts, *cots)


def plane_spot(z, own):
    turn = z ^ own
    return (turn & 1) * 2 + (turn >> 1)


def down_grad_kernel(at_ref, act_in, d_in, got_in, keep_ref, send_ref, act_ref, d_ref, got_ref, keep_s, send_s, sem):
    piece = keep_s.shape[2]
    chunk = 4 * piece
    wide = act_ref.shape[1]
    ins = [put(*pair, sem, k) for k, pair in enumerate(((d_in, d_ref), (act_in, act_ref), (got_in, got_ref)))]
    for copy in ins:
        copy.wait()
    outs = []
    for f, hold, ref in ((1, send_s, send_ref), (0, keep_s, keep_ref)):
        for x in range(2):
            t = (f ^ at_ref[0]) * 2 + (x ^ at_ref[2])
            at = pl.ds(pl.multiple_of(t * chunk, LANES), chunk)
            grad = dot(act_ref[:, at], d_ref[...], ((0,), (0,)))
            grad = (grad + dot(got_ref[:, at], got_ref[:, wide:], ((0,), (0,)))).astype(BF16)
            for z in range(4):
                hold[x, plane_spot(z, at_ref[3])] = grad[z * piece : (z + 1) * piece]
            outs.append(put(hold.at[x], ref.at[x], sem, 3 + 2 * f + x))
    for copy in outs:
        copy.wait()


def up_grad_kernel(at_ref, first_in, dhid_in, dbr_in, small_ref, got_in, *rest):
    ctx_refs, (keep_ref, send_ref), rest = rest[:4], rest[4:6], rest[6:]
    first_s, ctx_s, extra_s, first_ref, dhid_ref, dbr_ref, got_ref, keep_s, send_s, sem = rest
    half, step = keep_s.shape[2:]
    rows, width = first_ref.shape
    slab = ctx_refs[0].shape[1]
    wide, narrow = dhid_ref.shape[1], dbr_ref.shape[1]
    ins = [put(first_in, first_ref, sem, 0)]
    cuts = (wide + narrow, wide + narrow + width, wide + narrow + 2 * width)
    for k, (a, b) in enumerate(((cuts[0], cuts[1]), (cuts[1], cuts[2]), (0, cuts[0]))):
        ins.append(put(got_in.at[:, pl.ds(a, b - a)], got_ref.at[:, pl.ds(a, b - a)], sem, 1 + k))
    ins += [put(dhid_in, dhid_ref, sem, 4), put(dbr_in, dbr_ref, sem, 5)]
    for copy in ins[:3]:
        copy.wait()
    first_s[:, :rows] = first_ref[...].T
    first_s[:, rows:] = got_ref[:rows, wide + narrow : wide + narrow + width].T
    got_ctx = got_ref[:rows, wide + narrow + width :].T
    for r in range(4):
        ctx_s[at_ref[4] ^ r, :, :rows] = ctx_refs[r][...].T
        ctx_s[at_ref[4] ^ r ^ 1, :, rows:] = got_ctx[r * slab : (r + 1) * slab]
    ups = wide // step
    for copy in ins[3:]:
        copy.wait()
    extra_s[...] = jnp.zeros_like(extra_s)
    vectors = small_ref[...].astype(F32) + got_ref[rows:, :width].astype(F32)
    for f in range(2):
        for i in range(6):
            for k in range(half // LANES):
                start = f * half + k * LANES
                extra_s[f, i * (half // LANES) + k : i * (half // LANES) + k + 1, :] = vectors[
                    i : i + 1, start : start + LANES
                ]
        row = 6 * (half // LANES)
        for k in range(wide // LANES):
            start = f * wide + k * LANES
            extra_s[f, row + k : row + k + 1, :] = vectors[
                8 + start // width : 9 + start // width, start % width : start % width + LANES
            ]
    outs = []
    for x, ref, out in ((1, send_s, send_ref), (0, keep_s, keep_ref)):

        def one(i, carry, x=x, ref=ref):
            spot = (i & 1) * 2 + (i >> 1)
            k = (x ^ at_ref[2]) * 4 + (i ^ at_ref[3])

            def store(grad):
                for f in range(2):
                    ref[f ^ at_ref[0], spot] = grad[f * half : (f + 1) * half].astype(BF16)

            def out_grad(lanes):
                turned = ctx_s[...].reshape(width, 2 * rows)
                right = jnp.concatenate([dbr_ref[:, lanes], got_ref[:rows, wide + lanes.start : wide + lanes.stop]], axis=0)
                return dot(turned, right, ((1,), (0,)))

            @pl.when(k < ups)
            def _():
                at = pl.ds(pl.multiple_of(k * step, step), step)
                right = jnp.concatenate([dhid_ref[:, at], got_ref[:rows, at]], axis=0)
                store(dot(first_s[...], right, ((1,), (0,))))

            @pl.when(k == ups)
            def _():
                store(out_grad(slice(0, step)))

            @pl.when(k > ups)
            def _():
                extra = extra_s[...].reshape(width, LANES)
                store(jnp.concatenate([out_grad(slice(step, narrow)), extra], axis=1))

            return carry

        lax.fori_loop(0, 4, one, 0)
        outs.append(put(ref, out, sem, 6 + x))
    for copy in outs:
        copy.wait()


def down_final_kernel(at_ref, *rest):
    parts, (out_ref, in_s, out_s, sem) = rest[:4], rest[4:]
    piece = parts[0].shape[1]
    copies_in = [put(part, in_s.at[i], sem, i) for i, part in enumerate(parts)]
    copies = []
    for i in range(4):
        copies_in[i].wait()
        for z in range(4):
            k = (((i & 1) ^ at_ref[1]) * 2 + ((i >> 1) ^ at_ref[2])) * 4 + (z ^ at_ref[3])
            at = pl.ds(pl.multiple_of(k * piece, 16), piece)
            out_s[at, :] = in_s[i, (z & 1) * 2 + (z >> 1)].astype(F32)
            copies.append(put(out_s.at[at], out_ref.at[at], sem, 4 + i * 4 + z))
    for copy in copies:
        copy.wait()


def up_final_kernel(at_ref, *rest):
    parts, (up_ref, out_ref, gains_ref, biases_ref, upb_ref, in_s, out_s, sem) = rest[:4], rest[4:]
    step = parts[0].shape[2]
    wide, narrow = up_ref.shape[1] // 2, out_ref.shape[1] // 2
    ups = wide // step
    half = gains_ref.shape[1]
    count = half // LANES
    copies_in = [put(part, in_s.at[i], sem, i) for i, part in enumerate(parts)]

    def each(i, z, act):
        core = (i & 1) ^ at_ref[1]
        k = ((i >> 1) ^ at_ref[2]) * 4 + (z ^ at_ref[3])
        n = i * 4 + z

        @pl.when(k < ups)
        def _():
            at = pl.ds(pl.multiple_of(core * wide + k * step, LANES), step)
            act(pltpu.make_async_copy(out_s.at[n], up_ref.at[:, at], sem.at[4 + n]))

        @pl.when(k == ups)
        def _():
            at = pl.ds(pl.multiple_of(core * narrow, LANES), step)
            act(pltpu.make_async_copy(out_s.at[n], out_ref.at[:, at], sem.at[4 + n]))

        @pl.when(k > ups)
        def _():
            at = pl.ds(pl.multiple_of(core * narrow + step, LANES), LANES)
            act(pltpu.make_async_copy(out_s.at[n, :, pl.ds(0, LANES)], out_ref.at[:, at], sem.at[4 + n]))

        return core, k

    for i in range(4):
        copies_in[i].wait()
        for z in range(4):
            value = in_s[i, (z & 1) * 2 + (z >> 1)].astype(F32)
            out_s[i * 4 + z] = value
            core, k = each(i, z, lambda copy: copy.start())

            @pl.when((k > ups) & (core == 0))
            def _(value=value):
                extra = value[:, LANES:]
                for a in range(6):
                    for b in range(count):
                        row = extra[a * count + b : a * count + b + 1]
                        lanes = slice(b * LANES, (b + 1) * LANES)
                        if a < 2:
                            gains_ref[a : a + 1, lanes] = row
                        else:
                            biases_ref[a - 2 : a - 1, lanes] = row
                for b in range(upb_ref.shape[0] // LANES):
                    upb_ref[b * LANES : (b + 1) * LANES] = extra[6 * count + b]

    for i in range(4):
        for z in range(4):
            each(i, z, lambda copy: copy.wait())


def qkv_final_kernel(at_ref, late_ref, *rest):
    parts, (out_ref, biases_ref, hold, in_s, out_s, sums_s, sem) = rest[:4], rest[4:]
    half, slab = out_s.shape[0], hold.shape[2] // 3
    width = 4 * slab
    size = parts[0].shape[1]
    copies = [put(part, in_s.at[i], sem, i) for i, part in enumerate(parts)]
    for r in range(4):
        copies[r].wait()
        for z in range(4):
            at = pl.ds(pl.multiple_of((z ^ at_ref[3]) * size, 16), size)
            hold[at_ref[4] ^ r, at, :] = in_s[r, (z & 1) * 2 + (z >> 1)]
    outs = []
    for k, column in ((0, 1), (1, 2), (2, 0)):
        for m in range(4):
            cols = slice(column * width + m * slab, column * width + (m + 1) * slab)
            out_s[:, cols] = hold[m, :half, k * slab : (k + 1) * slab].astype(F32)
        at = pl.ds(column * width, width)
        outs.append(put(out_s.at[:, at], out_ref.at[:, at], sem, 4 + k))
    for k, row in ((2, 0), (1, 1)):
        sums = [hold[m, half : half + 16, k * slab : (k + 1) * slab].astype(F32)[:1] for m in range(4)]
        sums_s[row : row + 1, :] = jnp.concatenate(sums, axis=1)
    biases_ref[0:2, :] = sums_s[0:2, pl.ds(pl.multiple_of(at_ref[0] * half, LANES), half)]
    biases_ref[2:6, :] = late_ref[...]
    for copy in outs:
        copy.wait()


def local_call(kernel, outs, ins, scratch, name, time=3, loose=(), limit=28):
    return pl.pallas_call(
        kernel,
        out_shape=outs,
        in_specs=[whole(pltpu.SMEM)]
        + [whole(pl.ANY if i in loose else pltpu.VMEM) for i in range(1, len(ins))],
        out_specs=tuple(whole(pl.ANY if len(ins) + i in loose else pltpu.VMEM) for i in range(len(outs))),
        scratch_shapes=scratch,
        compiler_params=pltpu.CompilerParams(vmem_limit_bytes=limit * MIB),
        cost_estimate=cost(time),
        name=name,
    )(*ins)


def swap_joint(value, f_mask, c_mask):
    n_f, n_c = lax.axis_size("fsdp"), lax.axis_size("ctx")
    pairs = [(f * n_c + c, (f ^ f_mask) * n_c + (c ^ c_mask)) for f in range(n_f) for c in range(n_c)]
    return lax.ppermute(value, ("fsdp", "ctx"), pairs)


def sum_planes(own, others):
    total = own.astype(F32)
    for other in others:
        total = total + other.astype(F32)
    return total.astype(BF16)


def reduce_square(keep, got, after, axis, mask):
    first, second = sum_planes(gate(keep[0], after), [got[0]]), sum_planes(keep[1], [got[1]])
    return first, swap(second, axis, mask)


def reduce_planes(mine, late=(), last=()):
    two = sum_planes(mine[:2], [swap(mine[2:], "ctx", 4)])
    piece = gate(sum_planes(two[0], [swap(two[1], "ctx", 8)]), *late)
    four = jnp.stack([piece] + [swap(piece, "ctx", mask) for mask in (8, 4, 12)])
    across = swap(four, "ctx", 2)
    return four, [four, swap(four, "ctx", 1), across, swap(gate(across, *last), "ctx", 1)]


def exchange(near, far, between=None):
    half = len(near)
    got = swap(far, "ctx", half)
    if between is not None:
        got = gate(got, between)
    items = {(d, 0): near[d] for d in range(half)}
    items.update({(d, half): got[d] for d in range(half)})
    if between is not None:
        items[0, half] = got
    for bit in reversed(bits_of(half)):
        for d, source in [key for key in items if key[0] & bit]:
            items[d ^ bit, source ^ bit] = swap(items.pop((d, source)), "ctx", bit)
    return [items[0, source] for source in range(2 * half)]


def gather_fsdp(value):
    index = lax.axis_index("fsdp")
    parts = [value]
    for bit in bits_of(lax.axis_size("fsdp")):
        parts += [swap(part, "fsdp", bit) for part in parts]
    return to_absolute(parts, index)


def fetch_halves(value):
    half = value.shape[0] // 2
    parts = [lax.dynamic_slice_in_dim(value, (lax.axis_index("ctx") & 1) * half, half, 0)]
    for bit in bits_of(lax.axis_size("fsdp")):
        parts += [swap(part, "fsdp", bit) for part in parts]
    return parts[1:]


def weight_parts(value, halves):
    index = lax.axis_index("fsdp")
    core = lax.axis_index("ctx") & 1
    size = value.shape[0]
    half = size // 2
    pieces, places = [value], [index * size]
    for k, part in enumerate(halves, 1):
        pieces += [part, swap(part, "ctx", 1)]
        first = (index ^ k) * size
        places += [first + core * half, first + (1 - core) * half]
    return pieces, places


def halve(value, axis, dim, mask, index):
    half = value.shape[dim] // 2
    bit = (index // mask) & 1
    mine = lax.dynamic_slice_in_dim(value, bit * half, half, dim)
    theirs = lax.dynamic_slice_in_dim(value, (1 - bit) * half, half, dim)
    return mine + swap(theirs.astype(BF16), axis, mask).astype(F32)


def double(value, axis, dim, mask, index):
    bit = (index // mask) & 1
    other = swap(value, axis, mask)
    return lax.select_n(
        bit,
        jnp.concatenate([value, other], axis=dim),
        jnp.concatenate([other, value], axis=dim),
    )


def reduce_over_all(value):
    f_index, c_index = lax.axis_index("fsdp"), lax.axis_index("ctx")
    value = halve(value, "ctx", 1, 1, c_index)
    for bit in reversed(bits_of(lax.axis_size("fsdp"))):
        value = halve(value, "fsdp", 0, bit, f_index)
    value = value[0]
    rest = bits_of(lax.axis_size("ctx"))[1:]
    for bit in rest:
        value = halve(value, "ctx", 0, bit, c_index)
    value = value.astype(BF16)
    for bit in reversed(rest):
        value = double(value, "ctx", 0, bit, c_index)
    return double(value, "ctx", 0, 1, c_index).astype(F32)


def local(
    tokens, segments, rand_blocks, w_qkv, w_out, w_up, w_down, ln_gains, biases, up_bias, cotangent
):
    positions, seq_count, width = tokens.shape
    n_f, n_c = lax.axis_size("fsdp"), lax.axis_size("ctx")
    f_index, c_index = lax.axis_index("fsdp"), lax.axis_index("ctx")
    group = n_c // seq_count
    plane, member = c_index // group, c_index % group
    head_count = width // HD
    heads = -(-head_count // group)
    per_chunk = positions // BLK
    blocks = per_chunk * n_c
    rows_here = seq_count * positions
    f_width = width // n_f
    slab = heads * HD
    spare = group * slab - width

    def to_planes(parts):
        return [swap(part, "ctx", p * group) if p else part for p, part in enumerate(parts)]

    def from_planes(parts):
        return jnp.stack(to_absolute(parts, plane), axis=1)

    fast = n_f == 2 and group == 4 and seq_count == 4 and not spare and f_width % slab == 0
    turns = jnp.stack([f_index, member & 1, (member >> 1) & 1, plane, member, c_index])
    rand = jnp.pad(rand_blocks, ((0, 0), (0, 0), (0, group * heads - head_count), (0, 0)))
    rand = rand.reshape(seq_count, per_chunk, group, heads, -1).transpose(0, 2, 1, 3, 4)
    rand = rand.reshape(seq_count, group, -1)
    rand = jnp.pad(rand, ((0, 0), (0, 0), (0, LANES // group - rand.shape[2])))
    line = jnp.concatenate([segments.T, rand.reshape(seq_count, LANES)], axis=1).astype(BF16)
    line = jnp.pad(line, ((0, 0), (0, width - line.shape[1])))
    token_parts = split_planes(turns, tokens, line)
    w_qkv, small_in = lax.optimization_barrier(((w_qkv, (ln_gains, biases, up_bias)), *token_parts))[0]
    ln_gains, biases, up_bias = small_in
    x_rows = to_planes(token_parts)
    if fast:
        across = [swap(part, "ctx", 2) for part in x_rows]
        x_pieces = [*x_rows, swap(jnp.concatenate(x_rows), "ctx", 1), *across]
        x_pieces += [swap(part, "ctx", 1) for part in across]
    else:
        x_all = {(0, p): x_rows[p] for p in range(seq_count)}
        for bit in reversed(bits_of(group)):
            for r, p in list(x_all):
                x_all[r ^ bit, p] = swap(x_all[r, p], "ctx", bit)
        x_pieces = [x_all[r, p] for r in range(group) for p in range(seq_count)]

    w_parts = jnp.pad(w_qkv.reshape(-1, 3, width), ((0, 0), (0, 0), (0, spare))) if spare else None
    if spare:
        w_mine = [lax.dynamic_slice_in_dim(w_parts[:, k], member * slab, slab, 1) for k in (1, 2, 0)]
    else:
        w_mine = [lax.dynamic_slice_in_dim(w_qkv, k * width + member * slab, slab, 1) for k in (1, 2, 0)]
    small = jnp.concatenate([ln_gains.reshape(-1), biases.reshape(-1), up_bias])
    small_rows = -(-small.shape[0] // (3 * slab) // 16) * 16
    small_count = small.shape[0]
    small = jnp.pad(small, (0, small_rows * 3 * slab - small_count)).reshape(small_rows, 3 * slab)
    w_mine = jnp.concatenate([jnp.concatenate(w_mine, axis=1), small], axis=0)
    w_pieces = [w_mine]
    for bit in bits_of(n_f):
        w_pieces += [swap(part, "fsdp", bit) for part in w_pieces]
    small = [part[f_width:].reshape(-1)[:small_count] for part in w_pieces]
    small = jnp.stack(to_absolute(small, f_index)).astype(F32)
    gains_all = small[:, : 2 * f_width].reshape(n_f, 2, f_width).transpose(1, 0, 2).reshape(2, width)
    biases_all = (
        small[:, 2 * f_width : 8 * f_width].reshape(n_f, 6, f_width).transpose(1, 0, 2).reshape(6, width)
    )
    up_shift = small[:, 8 * f_width :].reshape(-1)
    bias_mine = lax.dynamic_slice_in_dim(
        jnp.pad(biases_all[:2], ((0, 0), (0, spare))), member * slab, slab, 1
    ).reshape(2, heads, HD)
    bias_wide = jnp.concatenate(
        [jnp.zeros_like(bias_mine[0]), bias_mine[1], bias_mine[0]], axis=0
    ).reshape(1, -1)

    cot_in = gate(cotangent, x_rows)
    cots = to_planes([lax.dynamic_index_in_dim(cot_in, plane ^ p, 1, keepdims=False) for p in range(seq_count)])
    if fast:
        core, chip = member & 1, member >> 1
        quarter, half = f_width // 4, f_width // 2
        up_quarter = lax.dynamic_slice_in_dim(w_up, (core * 2 + chip) * quarter, quarter, 0)
        up_quarter = gate(up_quarter, w_mine, across[0])
        tall = w_down.shape[0] // 2
        joint = lax.dynamic_slice_in_dim(w_down, core * tall, tall, 0).reshape(-1, half, width)
        joint = [lax.dynamic_slice_in_dim(w_out, core * half, half, 0), *joint]
        joint = swap(gate(jnp.concatenate(joint, axis=1), up_quarter), "fsdp", 1)
        up_quarter = swap(up_quarter, "fsdp", 1)
        up_across = swap(up_quarter, "ctx", 2)
    else:
        up_halves = fetch_halves(w_up)
        down_halves = fetch_halves(w_down)
    x_pieces = [piece.reshape(-1, positions + 16, width) for piece in x_pieces]
    x_seq, qa, ka, va, loc, *ctx_parts = attention_forward(
        turns, x_pieces, w_pieces, bias_wide, heads, group, seq_count, positions
    )
    x_seq = x_seq.reshape(blocks * BLK, width)
    if fast:
        ctx_parts, up_across, cots = lax.optimization_barrier((ctx_parts, up_across, cots))
        up_other = [swap(part, "ctx", 1) for part in (gate(up_quarter, ctx_parts[0]), up_across)]
    ctx_mine = ctx_parts
    if fast:
        ctx_parts = [ctx_parts[0]] + [swap(ctx_parts[r], "ctx", r) for r in (1, 2, 3)]
    else:
        ctx_parts = exchange(ctx_parts[: group // 2], jnp.stack(ctx_parts[group // 2 :]))
    if fast:
        joint_other = swap(gate(joint, ctx_mine[0]), "ctx", 1)
        parts = [w_out.reshape(2, slab, width), w_up, w_down, up_quarter, up_across, *up_other, joint, joint_other]
        plan = [(0, None, 0), (1, None, 1), (2, None, 2)] + [(3 + k, None, 1) for k in range(4)]
        theirs = 1 - f_index
        places = [2 * f_index, f_index * f_width, f_index * 2 * tall]
        for k in range(4):
            part = (core ^ (k >> 1)) * 2 + (chip ^ (k & 1))
            places.append(theirs * f_width + part * quarter)
        for k in range(2):
            plan += [(7 + k, n * width, 0 if n == 0 else 2) for n in range(1 + tall // half)]
            places.append(2 * theirs + (core ^ k))
            places += [theirs * 2 * tall + (core ^ k) * tall + n * half for n in range(tall // half)]
    else:
        out_full = jnp.concatenate(gather_fsdp(w_out), axis=0)
        out_full = jnp.pad(out_full, ((0, spare), (0, 0))).reshape(group, slab, width)
        up_parts, up_places = weight_parts(w_up, up_halves)
        down_parts, down_places = weight_parts(w_down, down_halves)
        parts, places = [out_full, *up_parts, *down_parts], [0, *up_places, *down_places]
        plan = [(0, None, 0)] + [(1 + k, None, 1) for k in range(len(up_parts))]
        plan += [(1 + len(up_parts) + k, None, 2) for k in range(len(down_parts))]
    vectors = jnp.concatenate([biases_all, gains_all])
    place = jnp.stack([member] + [jnp.int32(p) for p in places])
    done = layer(
        place,
        x_seq,
        cots,
        vectors,
        up_shift.reshape(1, -1),
        ctx_parts,
        parts,
        plan,
        fast,
    )
    pieces = group // 2 + 1
    results, d_parts, done = done[:seq_count], done[-pieces:], done[seq_count:-pieces]
    results = to_planes(results)
    back = partial(attention_backward, loc, turns, qa, ka, va, w_pieces, width)
    hidden_width = w_up.shape[1]
    used = 6 * f_width + hidden_width // n_f

    if fast:
        act_mine, pack_one, d_second, first_low, dh1, dhid_mine, dbr_mine, pack_two, small_sums = done
        piece = hidden_width // n_f // 16
        pack_one = swap(pack_one, "ctx", 1)
        pack_two = swap(pack_two, "ctx", 1)
        step = (hidden_width + width + 256) // 16
        shape = jax.ShapeDtypeStruct((2, 4, f_width, step), BF16)
        up_keep, up_send = local_call(
            up_grad_kernel,
            (shape,) * 2,
            (
                turns,
                first_low,
                dhid_mine,
                dbr_mine,
                small_sums,
                pack_two,
                *ctx_parts,
            ),
            [
                pltpu.VMEM((width, 2 * rows_here), BF16),
                pltpu.VMEM((group, slab, 2 * rows_here), BF16),
                pltpu.VMEM((2, f_width, LANES), F32),
                pltpu.VMEM(first_low.shape, BF16),
                pltpu.VMEM(dhid_mine.shape, BF16),
                pltpu.VMEM(dbr_mine.shape, BF16),
                pltpu.VMEM(pack_two.shape, BF16),
                pltpu.VMEM(shape.shape, BF16),
                pltpu.VMEM(shape.shape, BF16),
                pltpu.SemaphoreType.DMA((8,)),
            ],
            "up_grad",
            loose=(1, 2, 3, 5, 10, 11),
            limit=56,
        )
        shape = jax.ShapeDtypeStruct((2, 4, piece, width), BF16)
        down_keep, down_send = local_call(
            down_grad_kernel,
            (shape,) * 2,
            (turns, gate(act_mine, up_send), d_second, pack_one),
            [
                pltpu.VMEM(act_mine.shape, BF16),
                pltpu.VMEM(d_second.shape, BF16),
                pltpu.VMEM(pack_one.shape, BF16),
                pltpu.VMEM(shape.shape, BF16),
                pltpu.VMEM(shape.shape, BF16),
                pltpu.SemaphoreType.DMA((7,)),
            ],
            "down_grad",
            loose=range(1, 6),
        )
        d_parts = exchange(d_parts[:-1], d_parts[-1], between=up_send)
        d_parts = gate(d_parts, down_send, up_send)
        down_got, up_got = swap(down_send, "fsdp", 1), swap(up_send, "ctx", 2)
        keep, send, d_qkv = back(ctx_mine, d_parts, heads)
        down_first, down_got = reduce_square(down_keep, down_got, send, "ctx", 2)
        up_first, up_got = reduce_square(up_keep, up_got, send, "fsdp", 1)
        output = from_planes([gate(results[0], send)] + results[1:])
        keep, send, d_qkv, down_first, up_first, output = lax.optimization_barrier(
            (keep, send, d_qkv, down_first, up_first, output)
        )
        shape = jax.ShapeDtypeStruct((4, (f_width + 64) // 4, 3 * slab), BF16)
        mine, theirs = local_call(
            projection_grad_kernel,
            (shape, shape),
            (turns, x_seq, d_qkv),
            [
                pltpu.VMEM(x_seq.shape, BF16),
                pltpu.VMEM(d_qkv.shape, BF16),
                pltpu.SemaphoreType.DMA((2,)),
            ],
            "projection_grad",
            loose=(1, 2),
        )
        cores = swap(send, "ctx", 1)
    else:
        dh1, active, d_hidden, first_low, d_second, d_branch, sums, upb_grad = done
        d_parts = exchange(d_parts[:-1], d_parts[-1])
        keep, send, d_qkv = back(ctx_mine, d_parts, heads)
        output = from_planes(results)
        context_low = jnp.concatenate(to_absolute(ctx_parts, member), axis=1)[:, :width]
        grad_down = dot(active, d_second, ((0,), (0,)))
        grad_up = dot(first_low, d_hidden, ((0,), (0,)))
        grad_out = dot(context_low, d_branch, ((0,), (0,)))
        down_total = reduce_over_all(grad_down.reshape(n_f, -1, width))
        vectors = sums[:6].reshape(6, n_f, f_width).transpose(1, 0, 2).reshape(n_f, -1)
        vectors = jnp.concatenate([vectors, upb_grad.reshape(n_f, -1)], axis=1)
        extra = -(-used // f_width // LANES) * LANES
        vectors = jnp.pad(vectors, ((0, 0), (0, f_width * extra - used))).reshape(n_f, f_width, extra)
        up_out = jnp.concatenate(
            [grad_up.reshape(n_f, f_width, -1), grad_out.reshape(n_f, f_width, -1), vectors], axis=2
        )
        up_out = reduce_over_all(up_out)
        up_total = up_out[:, :hidden_width]
        out_total = up_out[:, hidden_width : hidden_width + width]
        vectors = up_out[:, hidden_width + width :].reshape(-1)
        gains_total = vectors[: 2 * f_width].reshape(2, f_width)
        biases_late = vectors[2 * f_width : 6 * f_width].reshape(4, f_width)
        up_bias_total = vectors[6 * f_width : used]

    if not fast:
        cores = swap(send, "ctx", 1)
    shape = (seq_count, positions, width)
    pieces = {2 * i: list((keep[i] + cores[i].astype(F32)).reshape(shape)) for i in range(group // 2)}
    far, close = [], []
    for bit in bits_of(group)[1:]:
        for r in [r for r in pieces if r & bit]:
            part = pieces.pop(r)
            cut = seq_count // 2
            far = jnp.stack([part[p].astype(BF16) for p in range(cut, seq_count)])
            close = jnp.stack([part[p].astype(BF16) for p in range(cut)])
            if fast:
                down_first = gate(down_first, far)
            far, close = swap(far, "ctx", bit), swap(close, "ctx", bit)
            got = [*close, *far]
            pieces[r ^ bit] = [pieces[r ^ bit][p] + got[p].astype(F32) for p in range(seq_count)]
    dh1 = dh1.reshape(shape)
    input_grad = from_planes(
        to_planes([(dh1[p] + pieces[0][p]).astype(BF16) for p in range(seq_count)])
    )

    if fast:
        got = swap(theirs, "fsdp", 1)
        down_four, down_parts = reduce_planes(sum_planes(down_first, [down_got]))
        up_four, up_parts = reduce_planes(sum_planes(gate(up_first, far), [up_got]), late=(down_four,))
        four = range(1, 5)
        down_total = local_call(
            down_final_kernel,
            (jax.ShapeDtypeStruct((hidden_width // n_f, width), F32),),
            (turns, *down_parts),
            [
                pltpu.VMEM((4, 4, piece, width), BF16),
                pltpu.VMEM((hidden_width // n_f, width), F32),
                pltpu.SemaphoreType.DMA((20,)),
            ],
            "down_final",
            loose=(*four, 5),
        )[0]
        up_total, out_total, gains_total, biases_late, up_bias_total = local_call(
            up_final_kernel,
            (
                jax.ShapeDtypeStruct((f_width, hidden_width), F32),
                jax.ShapeDtypeStruct((f_width, width), F32),
                jax.ShapeDtypeStruct((2, f_width), F32),
                jax.ShapeDtypeStruct((4, f_width), F32),
                jax.ShapeDtypeStruct((hidden_width // n_f,), F32),
            ),
            (turns, *up_parts),
            [
                pltpu.VMEM((4, 4, f_width, step), BF16),
                pltpu.VMEM((16, f_width, step), F32),
                pltpu.SemaphoreType.DMA((20,)),
            ],
            "up_final",
            loose=(*four, 5, 6),
        )
        qkv_parts = reduce_planes(
            sum_planes(gate(mine, close), [got]), last=(up_total, down_total)
        )[1]
        qkv_total, biases_total = local_call(
            qkv_final_kernel,
            (jax.ShapeDtypeStruct((f_width, 3 * width), F32), jax.ShapeDtypeStruct((6, f_width), F32)),
            (turns, biases_late, *qkv_parts),
            [
                pltpu.VMEM((4, f_width + 64, 3 * slab), BF16),
                pltpu.VMEM((4, 4, (f_width + 64) // 4, 3 * slab), BF16),
                pltpu.VMEM((f_width, 3 * width), F32),
                pltpu.VMEM((8, width), F32),
                pltpu.SemaphoreType.DMA((7,)),
            ],
            "qkv_final",
            loose=(2, 3, 4, 5, 6),
        )
    else:
        grad_qkv = dot(x_seq, d_qkv, ((0,), (0,))).reshape(n_f, f_width, 3 * slab)
        sums = jnp.sum(d_qkv.astype(F32), axis=0, keepdims=True)
        sums = jnp.pad(sums, ((0, 15), (0, 0)))
        value = jnp.concatenate([grad_qkv, jnp.broadcast_to(sums[None], (n_f,) + sums.shape)], axis=1)
        for bit in reversed(bits_of(n_f)):
            value = halve(value, "fsdp", 0, bit, f_index)
        value = value[0]
        plane_bits = [bit * group for bit in bits_of(seq_count)]
        for bit in plane_bits:
            value = halve(value, "ctx", 0, bit, c_index)
        value = value.astype(BF16)
        for bit in reversed(plane_bits):
            value = double(value, "ctx", 0, bit, c_index)
        parts = [value]
        for bit in bits_of(group):
            parts += [swap(part, "ctx", bit) for part in parts]
        parts = to_absolute(parts, member)
        qkv_total = jnp.stack([part.reshape(-1, 3, slab) for part in parts], axis=2).reshape(-1, 3, group * slab)
        qkv_total = jnp.concatenate([qkv_total[:, 2:], qkv_total[:, :2]], axis=1)[:, :, :width].astype(F32)
        early = lax.dynamic_slice_in_dim(qkv_total[f_width][0::2], f_index * f_width, f_width, 1)
        qkv_total = qkv_total[:f_width].reshape(f_width, 3 * width)
        biases_total = jnp.concatenate([early, biases_late])
    return (
        output,
        input_grad,
        qkv_total,
        out_total,
        up_total,
        down_total,
        gains_total,
        biases_total,
        up_bias_total,
    )


def solution(mesh):
    placed = (
        P("ctx", "fsdp", None),
        P("ctx", "fsdp"),
        P("fsdp", "ctx", None, None),
        P("fsdp", None),
        P("fsdp", None),
        P("fsdp", None),
        P("fsdp", None),
        P(None, "fsdp"),
        P(None, "fsdp"),
        P("fsdp"),
        P("ctx", "fsdp", None),
    )
    return jax.shard_map(
        local,
        mesh=mesh,
        in_specs=placed,
        out_specs=(
            P("ctx", "fsdp", None),
            P("ctx", "fsdp", None),
            P("fsdp", None),
            P("fsdp", None),
            P("fsdp", None),
            P("fsdp", None),
            P(None, "fsdp"),
            P(None, "fsdp"),
            P("fsdp"),
        ),
        check_vma=False,
    )
```
